512 devices in a mesh: gx: 64 (over z, y_hi, core), gy: 8 (over x, y_lo).
Axes of the slice: x: 4, y: 4 (y_hi: 2, y_lo: 2; y = y_hi * 2 + y_lo), z: 16, core: 2. Of those that a mesh axis runs over, the one named last changes fastest.
Arguments:
- points: float32 [65536, 512], P(('gx', 'gy')), may hold values from -16 to 16, as said below
- block_cell: int32 [65536], P(('gx', 'gy')), may hold values from 0 to 511
- block_mat: int32 [65536], P(('gx', 'gy')), may hold values from 0 to 7
- density: float32 [8], replicated, may hold values from 1 to 3
- shear_modulus: float32 [8], replicated, may hold values from 0.5 to 4
- lame_modulus: float32 [8], replicated, may hold values from 0.5 to 4
- mig_slot_a: int32 [32768], P(('gx', 'gy')), may hold values from 0 to 63, as said below
- mig_dest_a: int32 [32768], P(('gx', 'gy')), may hold values from 0 to 511, as said below
- mig_cell_a: int32 [32768], P(('gx', 'gy')), may hold values from 0 to 511, as said below
- mig_slot_b: int32 [32768], P(('gx', 'gy')), may hold values from 64 to 127, as said below
- mig_dest_b: int32 [32768], P(('gx', 'gy')), may hold values from 0 to 511, as said below
- mig_cell_b: int32 [32768], P(('gx', 'gy')), may hold values from 0 to 511, as said below
Outputs:
- final_points: float32 [131072, 512], P(('gx', 'gy'))
- final_cells: int32 [131072], P(('gx', 'gy'))
- final_materials: int32 [131072], P(('gx', 'gy'))
The draws below stay inside these ranges and needn't reach their ends.
Inputs may be any that keep to these rules, and one draw needn't show every extreme that they name: `points`: components 0 and 1 of every point lie in [0, 1]; peak pressures are 0 or more. `mig_slot_a`: the slots named by one device's list are distinct and lie below 64. `mig_slot_b`: the slots named by one device's list are distinct and lie in [64, 128). `mig_dest_a`: each entry names the device itself (the block stays) or an existing face neighbour (gx +- 1 or gy +- 1); at most 16 entries of one device name the same neighbour, and some device names one neighbour exactly 16 times. `mig_dest_b`: as for the first list. `mig_cell_a`: A cell local to the destination device. `mig_cell_b`: A cell local to the destination device.
All inputs are finite; a program needn't handle non-finite values.
Results may differ from the reference program's by a relative error of at most 0.0003.
Values sent between devices are 32-bit elements; how exact they have to be, the bound alone decides.
No kernel may reach another device: no remote copies, remote signals or barrier semaphores. Data moves between devices by JAX's collectives and lax.ppermute only.
A program may use at most 64 MiB of HBM per device.

```python
import math
import jax
import jax.numpy as jnp
from jax import lax

CX = 16
CY = 32
BLK_DEV = 128
BLOCK = 64
NMAT = 8
MCAP = 16
MLIST = 64
NX = 1024
NY = 256
N_GX = 64
N_GY = 8
DEVICES = 512


def migration_lists(key, salt, floor_slot):
    key = jax.random.fold_in(key, salt)
    keys = jax.random.split(key, 4)
    devices = N_GX * N_GY
    capacity = BLK_DEV // 8
    length = BLK_DEV // 2
    device_id = jnp.arange(devices, dtype=jnp.int32)
    grid_row = device_id // N_GY
    grid_col = device_id % N_GY
    exists = jnp.stack([grid_row > 0, grid_row < N_GX - 1, grid_col > 0, grid_col < N_GY - 1], axis=1).astype(jnp.int32)
    impact = (grid_row < max(1, N_GX // 8))[:, None]
    sparse = jax.random.randint(keys[0], (devices, 4), 1, max(2, capacity // 4 + 1), dtype=jnp.int32)
    counts = jnp.where(impact, capacity, sparse) * exists
    bounds = jnp.cumsum(counts, axis=1)
    position = jnp.arange(length, dtype=jnp.int32)
    heading = jnp.sum((position[None, :, None] >= bounds[:, None, :]).astype(jnp.int32), axis=2)
    steps_table = jnp.array([-N_GY, N_GY, -1, 1, 0], dtype=jnp.int32)
    target = device_id[:, None] + steps_table[heading]
    scores = jax.random.randint(keys[1], (devices, length), 0, length, dtype=jnp.int32) * length + position[None, :]
    shuffle = jnp.argsort(scores, axis=1, stable=True)
    target = jnp.take_along_axis(target, shuffle, axis=1)
    slot_scores = jax.random.randint(keys[2], (devices, length), 0, length, dtype=jnp.int32) * length + position[None, :]
    slots = jnp.argsort(slot_scores, axis=1, stable=True).astype(jnp.int32) + floor_slot
    cells = jax.random.randint(keys[3], (devices, length), 0, CX * CY, dtype=jnp.int32)
    return (slots.reshape(-1), target.reshape(-1).astype(jnp.int32), cells.reshape(-1))


def draw_mig_slot_a(key, part):
    return migration_lists(key, 11, 0)[0]


def draw_mig_dest_a(key, part):
    return migration_lists(key, 11, 0)[1]


def draw_mig_cell_a(key, part):
    return migration_lists(key, 11, 0)[2]


def draw_mig_slot_b(key, part):
    return migration_lists(key, 12, BLK_DEV // 2)[0]


def draw_mig_dest_b(key, part):
    return migration_lists(key, 12, BLK_DEV // 2)[1]


def draw_mig_cell_b(key, part):
    return migration_lists(key, 12, BLK_DEV // 2)[2]


def draw_points(key, part):
    key = jax.random.fold_in(key, 5)
    keys = jax.random.split(key, 5)
    total = N_GX * N_GY * BLK_DEV
    fraction = jax.random.uniform(keys[0], (total, 2, BLOCK), jnp.float32)
    peak_pressure = jax.random.uniform(keys[1], (total, 1, BLOCK), jnp.float32, 0.0, 2.0)
    velocity = jnp.clip(jax.random.normal(keys[2], (total, 2, BLOCK), jnp.float32), -4.0, 4.0)
    stress = jnp.clip(2.0 * jax.random.normal(keys[4], (total, 3, BLOCK), jnp.float32), -8.0, 8.0)
    return jnp.concatenate([fraction, velocity, stress, peak_pressure], axis=1).reshape(total, 8 * BLOCK)


def plant(values, stream_key, least, top_value):
    extent = values.shape
    index_at = [jax.random.randint(jax.random.fold_in(stream_key, axis), (), 0, extent[axis]) for axis in range(len(extent))]
    values = values.at[tuple(index_at)].set(least)
    longest = extent.index(max(extent))
    index_at[longest] = (index_at[longest] + 1) % extent[longest]
    return values.at[tuple(index_at)].set(top_value)


def setup_inputs(seed: int = 0) -> dict:
    arg_keys = jax.random.split(jax.random.key(seed), 13)
    return {
        "points": draw_points(jax.random.fold_in(arg_keys[12], 71), 0),
        "block_cell": plant(jax.random.randint(arg_keys[1], (DEVICES * BLK_DEV,), 0, CX * CY), jax.random.fold_in(arg_keys[1], 1), 0, (CX * CY) - 1).astype(jnp.int32),
        "block_mat": plant(jax.random.randint(arg_keys[2], (DEVICES * BLK_DEV,), 0, NMAT), jax.random.fold_in(arg_keys[2], 1), 0, NMAT - 1).astype(jnp.int32),
        "density": jnp.clip(jnp.exp(jax.random.uniform(arg_keys[3], (NMAT,), jnp.float32, math.log(1.0), math.log(3.0))), 1.0, 3.0),
        "shear_modulus": jnp.clip(jnp.exp(jax.random.uniform(arg_keys[4], (NMAT,), jnp.float32, math.log(0.5), math.log(4.0))), 0.5, 4.0),
        "lame_modulus": jnp.clip(jnp.exp(jax.random.uniform(arg_keys[5], (NMAT,), jnp.float32, math.log(0.5), math.log(4.0))), 0.5, 4.0),
        "mig_slot_a": draw_mig_slot_a(jax.random.fold_in(arg_keys[12], 71), 0),
        "mig_dest_a": draw_mig_dest_a(jax.random.fold_in(arg_keys[12], 71), 0),
        "mig_cell_a": draw_mig_cell_a(jax.random.fold_in(arg_keys[12], 71), 0),
        "mig_slot_b": draw_mig_slot_b(jax.random.fold_in(arg_keys[12], 71), 0),
        "mig_dest_b": draw_mig_dest_b(jax.random.fold_in(arg_keys[12], 71), 0),
        "mig_cell_b": draw_mig_cell_b(jax.random.fold_in(arg_keys[12], 71), 0),
    }


TIME_STEP = 0.2
HALF_WIDTH = 0.25
MASS_FLOOR = 0.25
EXACT = lax.Precision.HIGHEST


def stencil(offset):
    distance = offset[None, :] + 1.0 - jnp.arange(4).astype(offset.dtype)[:, None]
    magnitude = jnp.abs(distance)
    direction_sign = jnp.sign(distance)
    inside = magnitude < HALF_WIDTH
    middle = magnitude < 1.0 - HALF_WIDTH
    shoulder = magnitude < 1.0 + HALF_WIDTH
    spare = 1.0 + HALF_WIDTH - magnitude
    weight = jnp.where(inside, 1.0 - (distance * distance + HALF_WIDTH * HALF_WIDTH) / (2.0 * HALF_WIDTH),
                       jnp.where(middle, 1.0 - magnitude,
                                 jnp.where(shoulder, spare * spare / (4.0 * HALF_WIDTH), 0.0)))
    slope = jnp.where(inside, -distance / HALF_WIDTH,
                      jnp.where(middle, -direction_sign,
                                jnp.where(shoulder, -direction_sign * spare / (2.0 * HALF_WIDTH), 0.0)))
    return weight, slope


def unpack(block_rows):
    block_count = block_rows.shape[0]
    return block_rows.reshape(block_count, 8, BLOCK).transpose(1, 0, 2).reshape(8, block_count * BLOCK)


def repack(components):
    block_count = components.shape[1] // BLOCK
    return components.reshape(8, block_count, BLOCK).transpose(1, 0, 2).reshape(block_count, 8 * BLOCK)


def point_weights(components):
    weight_x, slope_x = stencil(components[0])
    weight_y, slope_y = stencil(components[1])
    shape_out = (16, components.shape[1] // BLOCK, BLOCK)
    mass_w = (weight_x[:, None] * weight_y[None]).reshape(shape_out)
    grad_x = (slope_x[:, None] * weight_y[None]).reshape(shape_out)
    grad_y = (weight_x[:, None] * slope_y[None]).reshape(shape_out)
    return mass_w, grad_x, grad_y


def material_values(materials, mat_table):
    onehot = (materials[:, None] == jnp.arange(NMAT, dtype=jnp.int32)[None]).astype(mat_table.dtype)
    return jnp.dot(onehot, mat_table, precision=EXACT).T


def cell_table(block_cells):
    return (block_cells[:, None] == jnp.arange(CX * CY, dtype=jnp.int32)[None]).astype(jnp.float32)


def node_partials(weights, components, material, block_cells):
    mass_w, grad_x, grad_y = weights
    block_count = block_cells.shape[0]
    blocked = components.reshape(8, block_count, BLOCK)
    volume = 1.0 / BLOCK
    mass_pts = jnp.broadcast_to(material[0][:, None] * volume, (block_count, BLOCK))
    carried = jnp.stack([mass_pts, mass_pts * blocked[2], mass_pts * blocked[3]])
    pull_x = -volume * jnp.stack([blocked[4], blocked[6]])
    pull_y = -volume * jnp.stack([blocked[6], blocked[5]])
    moment = jnp.einsum('osp,qsp->soq', mass_w, carried, precision=EXACT)
    forces = jnp.einsum('osp,qsp->soq', grad_x, pull_x, precision=EXACT) + jnp.einsum('osp,qsp->soq', grad_y, pull_y, precision=EXACT)
    contribution = jnp.concatenate([moment, forces], axis=-1).reshape(block_count, 80)
    cell_sums = jnp.einsum('sc,sq->cq', cell_table(block_cells), contribution, precision=EXACT)
    spread = cell_sums.reshape(CX, CY, 4, 4, 5).transpose(4, 2, 3, 0, 1)
    extended = jnp.zeros((5, CX + 4, CY + 4), jnp.float32)
    for a in range(4):
        for b in range(4):
            extended = extended.at[:, a + 1:a + 1 + CX, b + 1:b + 1 + CY].add(spread[:, a, b])
    return extended


def grid_velocity(node_sums, node_x, node_y, total_x, total_y):
    node_mass = jnp.maximum(node_sums[0], MASS_FLOOR)
    velocity = (node_sums[1:3] + TIME_STEP * node_sums[3:5]) / node_mass
    pinned = ((node_x <= 0) | (node_x >= total_x - 1))[:, None] | ((node_y <= 0) | (node_y >= total_y - 1))[None, :]
    return jnp.where(pinned[None], 0.0, velocity)


def advance(components, weights, material, block_cells, materials, vel_ext):
    mass_w, grad_x, grad_y = weights
    block_count = block_cells.shape[0]
    blocked = components.reshape(8, block_count, BLOCK)
    stencil_vel = jnp.stack([vel_ext[:, a + 1:a + 1 + CX, b + 1:b + 1 + CY] for a in range(4) for b in range(4)])
    stencil_vel = stencil_vel.reshape(32, CX * CY)
    near_vel = jnp.einsum('sc,qc->sq', cell_table(block_cells), stencil_vel, precision=EXACT).reshape(block_count, 16, 2)
    velocity = jnp.einsum('osp,soc->csp', mass_w, near_vel, precision=EXACT)
    rate_x = jnp.einsum('osp,soc->csp', grad_x, near_vel, precision=EXACT)
    rate_y = jnp.einsum('osp,soc->csp', grad_y, near_vel, precision=EXACT)
    shear_pts = material[1][:, None]
    lame_pts = material[2][:, None]
    frac_x = jnp.clip(blocked[0] + TIME_STEP * velocity[0], 0.0, 1.0)
    frac_y = jnp.clip(blocked[1] + TIME_STEP * velocity[1], 0.0, 1.0)
    rate_xx = rate_x[0]
    rate_yy = rate_y[1]
    rate_xy = 0.5 * (rate_y[0] + rate_x[1])
    trace_rate = rate_xx + rate_yy
    stress_xx = blocked[4] + TIME_STEP * (2.0 * shear_pts * rate_xx + lame_pts * trace_rate)
    stress_yy = blocked[5] + TIME_STEP * (2.0 * shear_pts * rate_yy + lame_pts * trace_rate)
    stress_xy = blocked[6] + TIME_STEP * 2.0 * shear_pts * rate_xy
    pressure = -0.5 * (stress_xx + stress_yy)
    peak_pressure = jnp.maximum(blocked[7], pressure)
    alive_mask = (materials >= 0).astype(jnp.float32)[:, None]
    fresh = jnp.stack([frac_x, frac_y, velocity[0], velocity[1], stress_xx, stress_yy, stress_xy, peak_pressure])
    fresh = fresh * alive_mask[None]
    return fresh.reshape(8, block_count * BLOCK)


def outgoing(picked, picked_mats, list_slot, list_dest, list_cell, home_id, across, block_count):
    targets = jnp.stack([home_id - across, home_id + across, home_id - 1, home_id + 1])
    moving = list_dest != home_id
    matched = ((list_dest[None, :] == targets[:, None]) & moving[None, :]).astype(jnp.int32)
    order_rank = jnp.cumsum(matched, axis=1) - matched
    placing = matched[:, None, :] * (order_rank[:, None, :] == jnp.arange(MCAP, dtype=jnp.int32)[None, :, None]).astype(jnp.int32)
    outbox = jnp.einsum('krj,jc->krc', placing.astype(jnp.float32), picked, precision=EXACT)
    out_cell = jnp.sum(placing * list_cell[None, None, :], axis=-1)
    out_mat = jnp.sum(placing * (picked_mats + 1)[None, None, :], axis=-1)
    hits = moving.astype(jnp.int32)[None, :] * (list_slot[None, :] == jnp.arange(block_count, dtype=jnp.int32)[:, None]).astype(jnp.int32)
    vacated = jnp.sum(hits, axis=1) > 0
    return outbox, out_cell, out_mat, vacated


def from_low(values, axis_pos):
    first = lax.slice_in_dim(values, 0, 1, axis=axis_pos)
    rest = lax.slice_in_dim(values, 0, values.shape[axis_pos] - 1, axis=axis_pos)
    return jnp.concatenate([jnp.zeros_like(first), rest], axis=axis_pos)


def from_high(values, axis_pos):
    first = lax.slice_in_dim(values, 0, 1, axis=axis_pos)
    rest = lax.slice_in_dim(values, 1, values.shape[axis_pos], axis=axis_pos)
    return jnp.concatenate([rest, jnp.zeros_like(first)], axis=axis_pos)


def arrange(outbox):
    shaped = outbox.reshape((N_GX, N_GY) + outbox.shape[1:])
    incoming = jnp.stack([from_low(shaped[:, :, 1], 0), from_high(shaped[:, :, 0], 0),
                          from_low(shaped[:, :, 3], 1), from_high(shaped[:, :, 2], 1)], axis=2)
    return incoming.reshape((N_GX * N_GY, 4 * MCAP) + outbox.shape[3:])


def one_step(block_rows, block_cells, materials, mat_table, list_slot, list_dest, list_cell):
    devices = N_GX * N_GY
    block_count = block_rows.shape[0] // devices
    grouped = (block_rows.reshape(devices, block_count, 8 * BLOCK), block_cells.reshape(devices, block_count),
               materials.reshape(devices, block_count))

    def partial_of(packet):
        rows_here, cells_here, mats_here = packet
        components = unpack(rows_here)
        return node_partials(point_weights(components), components, material_values(mats_here, mat_table), cells_here)

    partial_grids = lax.map(partial_of, grouped)
    zero_idx = jnp.zeros((), jnp.int32)

    def accumulate(index, global_grid):
        index = index.astype(jnp.int32)
        corner = (zero_idx, (index // N_GY) * CX, (index % N_GY) * CY)
        current = lax.dynamic_slice(global_grid, corner, (5, CX + 4, CY + 4))
        return lax.dynamic_update_slice(global_grid, current + partial_grids[index], corner)

    global_grid = lax.fori_loop(0, devices, accumulate, jnp.zeros((5, NX + 4, NY + 4), jnp.float32))
    velocity = grid_velocity(global_grid[:, 2:NX + 2, 2:NY + 2], jnp.arange(NX, dtype=jnp.int32),
                             jnp.arange(NY, dtype=jnp.int32), NX, NY)
    vel_ext = jnp.pad(velocity, ((0, 0), (2, 2), (2, 2)))
    lists = (list_slot.reshape(devices, MLIST), list_dest.reshape(devices, MLIST), list_cell.reshape(devices, MLIST),
             jnp.arange(devices, dtype=jnp.int32))

    def move_of(packet):
        rows_here, cells_here, mats_here, slot_here, dest_here, cell_here, index = packet
        corner = (zero_idx, (index // N_GY) * CX, (index % N_GY) * CY)
        local_vel = lax.dynamic_slice(vel_ext, corner, (2, CX + 4, CY + 4))
        components = unpack(rows_here)
        fresh = repack(advance(components, point_weights(components), material_values(mats_here, mat_table),
                               cells_here, mats_here, local_vel))
        picked = jnp.take(fresh, slot_here, axis=0)
        picked_mats = jnp.take(mats_here, slot_here, axis=0)
        outbox, out_cell, out_mat, vacated = outgoing(picked, picked_mats, slot_here, dest_here, cell_here, index, N_GY, block_count)
        fresh = jnp.where(vacated[:, None], 0.0, fresh)
        kept_cells = jnp.where(vacated, 0, cells_here)
        kept_mats = jnp.where(vacated, -1, mats_here)
        return fresh, kept_cells, kept_mats, outbox, out_cell, out_mat

    fresh, kept_cells, kept_mats, outbox, out_cell, out_mat = lax.map(move_of, grouped + lists)
    new_rows = jnp.concatenate([fresh, arrange(outbox)], axis=1).reshape(-1, 8 * BLOCK)
    new_cells = jnp.concatenate([kept_cells, arrange(out_cell)], axis=1).reshape(-1)
    new_mats = jnp.concatenate([kept_mats, arrange(out_mat) - 1], axis=1).reshape(-1)
    return new_rows, new_cells, new_mats


def reference(points, block_cell, block_mat, density, shear_modulus, lame_modulus, mig_slot_a, mig_dest_a, mig_cell_a,
              mig_slot_b, mig_dest_b, mig_cell_b):
    mat_table = jnp.stack([density, shear_modulus, lame_modulus], axis=1)
    block_rows, block_cells, materials = points, block_cell, block_mat
    for list_slot, list_dest, list_cell in ((mig_slot_a, mig_dest_a, mig_cell_a), (mig_slot_b, mig_dest_b, mig_cell_b)):
        block_rows, block_cells, materials = one_step(block_rows, block_cells, materials, mat_table, list_slot, list_dest, list_cell)
    return block_rows, block_cells, materials
```

```python
import jax
import jax.numpy as jnp
from jax import lax
from jax.experimental import pallas as pl
from jax.experimental.pallas import tpu as pltpu
from jax.sharding import PartitionSpec as P

CX = 16
CY = 32
BLOCK = 64
NMAT = 8
MCAP = 16
LANES = 128
SUB = 8
ROWS = 160
HALO = 24
TOP = CX * SUB
MSG = MCAP + SUB

TIME_STEP = 0.2
MASS_FLOOR = 0.25
VOLUME = 1.0 / BLOCK
VMEM_LIMIT = 12 * 1024 * 1024

IN_VMEM = pl.BlockSpec(memory_space=pltpu.VMEM)
IN_SMEM = pl.BlockSpec(memory_space=pltpu.SMEM)
F32 = jnp.float32
BF16 = jnp.bfloat16
NN = (((1,), (0,)), ((), ()))
NT = (((1,), (1,)), ((), ()))


def call(kernel, outs, scratch, in_specs, *operands):
    return pl.pallas_call(
        kernel,
        out_shape=tuple(jax.ShapeDtypeStruct(shape, dtype) for shape, dtype in outs),
        in_specs=in_specs,
        out_specs=tuple(IN_VMEM for _ in outs),
        scratch_shapes=scratch,
        compiler_params=pltpu.CompilerParams(vmem_limit_bytes=VMEM_LIMIT),
    )(*operands)


def swap(value, axis, first):
    count = lax.axis_size(axis)
    pairs = []
    for low in range(first, count - 1, 2):
        pairs += [(low, low + 1), (low + 1, low)]
    return lax.ppermute(value, axis, pairs)


def iota(shape, dim):
    return lax.broadcasted_iota(jnp.int32, shape, dim)


def thirds(value):
    high = value.astype(BF16)
    rest = value - high.astype(F32)
    middle = rest.astype(BF16)
    low = (rest - middle.astype(F32)).astype(BF16)
    return (high, middle, low)


def product(parts, onehot, dims):
    total = None
    for part in parts:
        term = lax.dot_general(part, onehot, dims, preferred_element_type=F32)
        total = term if total is None else total + term
    return total


def stencil(u):
    p = jnp.maximum(0.25 - u, 0.0)
    q = jnp.maximum(u - 0.75, 0.0)
    p2 = p * p
    q2 = q * q
    weight = (p2, (1.0 - u) - 2.0 * p2 + q2, u + p2 - 2.0 * q2, q2)
    slope = (-2.0 * p, 4.0 * p + 2.0 * q - 1.0, 1.0 - 2.0 * p - 4.0 * q, 2.0 * q)
    return (weight, slope)


def by_material(materials, table):
    value = jnp.zeros(materials.shape, F32)
    for index in range(NMAT):
        value = jnp.where(materials == index, table[index], value)
    return value


def column_onehot(cells):
    cross = jnp.broadcast_to(cells & (CY - 1), (LANES, LANES))
    column = iota((LANES, LANES), 0)
    return [(column == cross + b).astype(F32).astype(BF16) for b in range(4)]


def row_masks(cells):
    depth = jnp.broadcast_to(cells >> 5, (SUB, LANES))
    return [depth == index for index in range(CX)]


def node_terms(load, chunks, rho):
    sub = iota((SUB, LANES), 0)
    scale = jnp.where(sub < 3, jnp.broadcast_to(rho * VOLUME, (SUB, LANES)), -VOLUME)
    scale = jnp.where(sub < 5, scale, 0.0)
    stencils = [(stencil(load(0, k)), stencil(load(1, k))) for k in range(chunks)]
    terms = [[None] * 4 for _ in range(4)]
    for b in range(4):
        acc = [[None] * 5 for _ in range(4)]
        for k in range(chunks):
            (weight_x, slope_x), (weight_y, slope_y) = stencils[k]
            wy, dy = weight_y[b], slope_y[b]
            sxy = load(6, k)
            y1 = wy * load(2, k)
            y2 = wy * load(3, k)
            y3 = wy * load(4, k)
            y4 = wy * sxy
            y5 = dy * sxy
            y6 = dy * load(5, k)
            for a in range(4):
                wx, dx = weight_x[a], slope_x[a]
                new = (wx * wy, wx * y1, wx * y2, dx * y3 + wx * y5, dx * y4 + wx * y6)
                acc[a] = [n if o is None else o + n for o, n in zip(acc[a], new)]
        for a in range(4):
            packed = jnp.zeros((SUB, LANES), F32)
            for q in range(5):
                total = jnp.sum(acc[a][q], axis=0, keepdims=True)
                packed = jnp.where(sub == q, jnp.broadcast_to(total, (SUB, LANES)), packed)
            terms[a][b] = packed * scale
    return terms


def spread_rows(terms, masks, left_ref, lane):
    zero = jnp.zeros((SUB, LANES), F32)
    for b in range(4):
        for x in range(ROWS // SUB):
            total = zero
            for a in range(4):
                if 0 <= x - a < CX:
                    total = total + jnp.where(masks[x - a], terms[a][b], zero)
            left_ref[x * SUB : (x + 1) * SUB, lane + b * LANES : lane + (b + 1) * LANES] = total


def parity(axis):
    return (lax.axis_index(axis) & 1) == 1


def emit_sums(left_ref, onehots, sums_ref, inner_ref, outer_ref):
    sums = product(thirds(left_ref[...]), jnp.concatenate(onehots, axis=1), NT)
    sums_ref[...] = sums
    odd = parity("gx")
    bottom, top = (sums[0:HALO], sums[TOP : TOP + HALO])
    inner_ref[...] = jnp.where(odd, bottom, top)
    outer_ref[...] = jnp.where(odd, top, bottom)


def sums_one(points_ref, meta_ref, density_ref, sums_ref, inner_ref, outer_ref, turned_ref, left_ref):
    turned_ref[...] = points_ref[...].T
    cells = meta_ref[0:1, :]
    rho = by_material(meta_ref[1:2, :], density_ref)
    load = lambda c, k: turned_ref[c * BLOCK + k * SUB : c * BLOCK + (k + 1) * SUB, :]
    terms = node_terms(load, BLOCK // SUB, rho)
    spread_rows(terms, row_masks(cells), left_ref, 0)
    emit_sums(left_ref, column_onehot(cells), sums_ref, inner_ref, outer_ref)


def regions(from_inner_x, from_outer_x, from_inner_y, from_outer_y):
    odd_x, odd_y = (parity("gx"), parity("gy"))
    return (
        jnp.where(odd_x, from_inner_x, from_outer_x),
        jnp.where(odd_x, from_outer_x, from_inner_x),
        jnp.where(odd_y, from_inner_y, from_outer_y),
        jnp.where(odd_y, from_outer_y, from_inner_y),
    )


def arrived_meta(boxes):
    packed = boxes[0][MCAP:MSG, 0:LANES]
    for index in range(1, 4):
        packed = packed + pltpu.roll(boxes[index][MCAP:MSG, 0:LANES], MCAP * index, 1)
    packed = packed + pltpu.roll(packed, 4 * MCAP, 1)
    sub = iota((SUB, LANES), 0)
    return packed.astype(jnp.int32) - (sub == 1).astype(jnp.int32)


def sums_two(
    kept_ref, meta_ref, xi_ref, xo_ref, yi_ref, yo_ref, density_ref,
    sums_ref, inner_ref, outer_ref, turned_ref, new_meta_ref,
    left_ref, wide_ref,
):
    boxes = regions(xi_ref[...], xo_ref[...], yi_ref[...], yo_ref[...])
    new_meta = arrived_meta(boxes)
    new_meta_ref[...] = new_meta
    rows = jnp.concatenate([box[0:MCAP] for box in boxes], axis=0)
    wide_ref[...] = jnp.concatenate([rows, jnp.zeros_like(rows)], axis=0).T
    half = BLOCK // 2
    for c in range(8):
        first = wide_ref[c * BLOCK : c * BLOCK + half, :]
        second = wide_ref[c * BLOCK + half : (c + 1) * BLOCK, :]
        turned_ref[c * half : (c + 1) * half, :] = first + pltpu.roll(second, BLOCK, 1)
    onehots = []
    for lane, chunks, ref, cells, mats in (
        (0, BLOCK // SUB, kept_ref, meta_ref[0:1, :], meta_ref[1:2, :]),
        (4 * LANES, half // SUB, turned_ref, new_meta[0:1], new_meta[1:2]),
    ):
        stride = chunks * SUB
        load = lambda c, k: ref[c * stride + k * SUB : c * stride + (k + 1) * SUB, :]
        terms = node_terms(load, chunks, by_material(mats, density_ref))
        spread_rows(terms, row_masks(cells), left_ref, lane)
        onehots += column_onehot(cells)
    emit_sums(left_ref, onehots, sums_ref, inner_ref, outer_ref)


def merge_depth(sums_ref, from_inner_ref, from_outer_ref, merged_ref, inner_ref, outer_ref):
    odd = parity("gx")
    from_inner, from_outer = (from_inner_ref[...], from_outer_ref[...])
    merged_ref[...] = sums_ref[...]
    merged_ref[0:HALO] = sums_ref[0:HALO] + jnp.where(odd, from_inner, from_outer)
    merged_ref[TOP : TOP + HALO] = sums_ref[TOP : TOP + HALO] + jnp.where(odd, from_outer, from_inner)
    lane = iota((SUB, LANES), 1)
    low = jnp.zeros((SUB, LANES), F32)
    high = jnp.zeros((SUB, LANES), F32)
    for x in range(CX + 3):
        row = merged_ref[x * SUB : (x + 1) * SUB, :]
        here = (lane >= 3 * x) & (lane < 3 * x + 3)
        shift = 3 * x
        low = jnp.where(here, pltpu.roll(row, shift, 1) if shift else row, low)
        high = jnp.where(here, pltpu.roll(row, (shift - CY) % LANES, 1), high)
    odd_y = parity("gy")
    inner_ref[...] = jnp.where(odd_y, low, high)
    outer_ref[...] = jnp.where(odd_y, high, low)


def node_velocity(merged_ref, from_inner_ref, from_outer_ref, velocity_ref):
    odd_y = parity("gy")
    from_inner, from_outer = (from_inner_ref[...], from_outer_ref[...])
    low = jnp.where(odd_y, from_inner, from_outer)
    high = jnp.where(odd_y, from_outer, from_inner)
    lane = iota((SUB, LANES), 1)
    total_x = CX * lax.axis_size("gx")
    total_y = CY * lax.axis_size("gy")
    base_x = lax.axis_index("gx") * CX - 1
    node_y = lax.axis_index("gy") * CY - 1 + lane
    inside_y = (node_y > 0) & (node_y < total_y - 1)
    for x in range(ROWS // SUB):
        row = merged_ref[x * SUB : (x + 1) * SUB, :]
        if x < CX + 3:
            shift = 3 * x
            row = row + jnp.where(lane < 3, pltpu.roll(low, (-shift) % LANES, 1) if shift else low, 0.0)
            row = row + jnp.where(
                (lane >= CY) & (lane < CY + 3), pltpu.roll(high, (CY - shift) % LANES, 1), 0.0
            )
        mass = jnp.maximum(jnp.broadcast_to(row[0:1], (SUB, LANES)), MASS_FLOOR)
        value = (row + TIME_STEP * pltpu.roll(row, SUB - 2, 0)) / mass
        node_x = base_x + x
        inside_x = (node_x > 0) & (node_x < total_x - 1)
        velocity_ref[x * SUB : (x + 1) * SUB, :] = jnp.where(inside_y & inside_x, value, 0.0)


def gathered(velocity_parts, cells):
    masks = row_masks(cells)
    near = [[None] * 4 for _ in range(4)]
    for b, onehot in enumerate(column_onehot(cells)):
        column = product(velocity_parts, onehot, NN)
        for a in range(4):
            total = jnp.zeros((SUB, LANES), F32)
            for x in range(CX):
                total = jnp.where(masks[x], column[(x + a) * SUB : (x + a + 1) * SUB], total)
            near[a][b] = total
    return near


def move_points(load, store, chunks, near, materials, shear_ref, lame_ref):
    wide = lambda row: jnp.broadcast_to(row, (SUB, LANES))
    twice_shear = wide(2.0 * by_material(materials, shear_ref))
    lame = wide(by_material(materials, lame_ref))
    alive = wide(materials) >= 0
    for k in range(chunks):
        u, v = (load(0, k), load(1, k))
        weight_x, slope_x = stencil(u)
        weight_y, slope_y = stencil(v)
        speed, along, across = ([], [], [])
        for row in (1, 2):
            value = rate_x = rate_y = None
            for a in range(4):
                inner = slant = None
                for b in range(4):
                    node = wide(near[a][b][row : row + 1])
                    term, tilt = (weight_y[b] * node, slope_y[b] * node)
                    inner = term if b == 0 else inner + term
                    slant = tilt if b == 0 else slant + tilt
                add = (weight_x[a] * inner, slope_x[a] * inner, weight_x[a] * slant)
                if a == 0:
                    value, rate_x, rate_y = add
                else:
                    value, rate_x, rate_y = (value + add[0], rate_x + add[1], rate_y + add[2])
            speed.append(value)
            along.append(rate_x)
            across.append(rate_y)
        rate_xx, rate_yy = (along[0], across[1])
        rate_xy = 0.5 * (across[0] + along[1])
        spherical = lame * (rate_xx + rate_yy)
        stress_xx = load(4, k) + TIME_STEP * (twice_shear * rate_xx + spherical)
        stress_yy = load(5, k) + TIME_STEP * (twice_shear * rate_yy + spherical)
        stress_xy = load(6, k) + TIME_STEP * twice_shear * rate_xy
        fresh = (
            jnp.clip(u + TIME_STEP * speed[0], 0.0, 1.0),
            jnp.clip(v + TIME_STEP * speed[1], 0.0, 1.0),
            speed[0],
            speed[1],
            stress_xx,
            stress_yy,
            stress_xy,
            jnp.maximum(load(7, k), -0.5 * (stress_xx + stress_yy)),
        )
        for c in range(8):
            store(c, k, jnp.where(alive, fresh[c], 0.0))


def outgoing(fresh, cells, materials, list_ref, message_refs):
    across = lax.axis_size("gy")
    gx, gy = (lax.axis_index("gx"), lax.axis_index("gy"))
    home = gx * across + gy
    step_x = across - 2 * across * (gx & 1)
    step_y = 1 - 2 * (gy & 1)
    slots, dests, places = (list_ref[0:1, :], list_ref[1:2, :], list_ref[2:3, :])
    dest = jnp.broadcast_to(dests, (2 * SUB, LANES))
    sub = iota((2 * SUB, LANES), 0)
    matched = jnp.zeros((2 * SUB, LANES), F32)
    for o, target in enumerate((home + step_x, home - step_x, home + step_y, home - step_y)):
        matched = jnp.where((sub == o) & (dest == target), 1.0, matched)
    square = (LANES, LANES)
    earlier = (iota(square, 0) < iota(square, 1)).astype(F32).astype(BF16)
    rank = lax.dot_general(matched.astype(BF16), earlier, NN, preferred_element_type=F32)
    place_rank = iota((MCAP, LANES), 0).astype(F32)
    placing = []
    for o in range(4):
        hit = jnp.broadcast_to(rank[o : o + 1], (MCAP, LANES)) == place_rank
        placing.append(jnp.where(hit, jnp.broadcast_to(matched[o : o + 1], (MCAP, LANES)), 0.0))
    placing.append(jnp.zeros((LANES - 4 * MCAP, LANES), F32))
    placing = jnp.concatenate(placing, axis=0).astype(BF16)
    holds = (iota(square, 0) == jnp.broadcast_to(slots, square)).astype(F32).astype(BF16)
    moving = jnp.where((dest >= 0) & (dest != home), 1.0, 0.0).astype(BF16)
    vacated = lax.dot_general(moving, holds, NT, preferred_element_type=F32)[0:1] > 0.5
    chosen = lax.dot_general(placing, holds, NT, preferred_element_type=F32).astype(BF16)
    listed = jnp.where(sub == 0, jnp.broadcast_to(places >> 5, dest.shape), 0)
    listed = jnp.where(sub == 1, jnp.broadcast_to(places & (CY - 1), dest.shape), listed)
    listed = lax.dot_general(listed.astype(F32).astype(BF16), placing, NT, preferred_element_type=F32)
    kinds = jnp.broadcast_to(materials + 1, dest.shape).astype(F32).astype(BF16)
    kinds = lax.dot_general(kinds, chosen, NT, preferred_element_type=F32)
    new_cells = jnp.broadcast_to(listed[0:1] * float(CY) + listed[1:2], (SUB, LANES))
    new_kinds = jnp.broadcast_to(kinds[0:1], (SUB, LANES))
    low_sub, lane = (iota((SUB, LANES), 0), iota((SUB, LANES), 1))
    tags = jnp.where(low_sub == 0, new_cells, jnp.where(low_sub == 1, new_kinds, 0.0))
    total = None
    for part in thirds(fresh):
        term = lax.dot_general(chosen[0 : 4 * MCAP], part, NN, preferred_element_type=F32)
        total = term if total is None else total + term
    for o, ref in enumerate(message_refs):
        ref[0:MCAP, :] = total[o * MCAP : (o + 1) * MCAP]
        tag = pltpu.roll(tags, LANES - o * MCAP, 1) if o else tags
        ref[MCAP:MSG, 0:LANES] = jnp.where(lane < MCAP, tag, 0.0)
        ref[MCAP:MSG, LANES:] = jnp.zeros((SUB, 8 * BLOCK - LANES), F32)
    return vacated


def vacate(meta, vacated):
    sub = iota((SUB, LANES), 0)
    gone = jnp.broadcast_to(vacated.astype(F32), (SUB, LANES)) > 0.5
    return jnp.where(gone, jnp.where(sub == 1, -1, 0), meta)


def advance_one(
    turned_ref, meta_ref, list_ref, merged_ref, yi_ref, yo_ref, shear_ref, lame_ref,
    kept_ref, kept_meta_ref, m0_ref, m1_ref, m2_ref, m3_ref,
    velocity_ref, fresh_ref,
):
    node_velocity(merged_ref, yi_ref, yo_ref, velocity_ref)
    parts = thirds(velocity_ref[...])
    meta = meta_ref[...]
    cells, materials = (meta[0:1], meta[1:2])
    at = lambda c, k: slice(c * BLOCK + k * SUB, c * BLOCK + (k + 1) * SUB)

    def store(c, k, value):
        fresh_ref[at(c, k), :] = value

    load = lambda c, k: turned_ref[at(c, k), :]
    move_points(load, store, BLOCK // SUB, gathered(parts, cells), materials, shear_ref, lame_ref)
    fresh = fresh_ref[...]
    vacated = outgoing(fresh.T, cells, materials, list_ref, (m0_ref, m1_ref, m2_ref, m3_ref))
    gone = jnp.broadcast_to(vacated.astype(F32), fresh.shape) > 0.5
    kept_ref[...] = jnp.where(gone, 0.0, fresh)
    kept_meta_ref[...] = vacate(meta, vacated)


def advance_two(
    kept_ref, meta_ref, turned_ref, new_meta_ref, list_ref, merged_ref, yi_ref, yo_ref, shear_ref, lame_ref,
    old_ref, new_ref, old_meta_ref, m0_ref, m1_ref, m2_ref, m3_ref,
    velocity_ref, fresh_ref, wide_ref,
):
    node_velocity(merged_ref, yi_ref, yo_ref, velocity_ref)
    parts = thirds(velocity_ref[...])
    meta = meta_ref[...]
    cells, materials = (meta[0:1], meta[1:2])
    at = lambda c, k: slice(c * BLOCK + k * SUB, c * BLOCK + (k + 1) * SUB)

    def store(c, k, value):
        fresh_ref[at(c, k), :] = value

    load = lambda c, k: kept_ref[at(c, k), :]
    move_points(load, store, BLOCK // SUB, gathered(parts, cells), materials, shear_ref, lame_ref)
    fresh = fresh_ref[...]
    rows = fresh.T
    vacated = outgoing(rows, cells, materials, list_ref, (m0_ref, m1_ref, m2_ref, m3_ref))
    gone = jnp.broadcast_to(vacated.astype(F32), fresh.shape) > 0.5
    old_ref[...] = jnp.where(gone, 0.0, fresh).T
    old_meta_ref[...] = vacate(meta, vacated)

    half = BLOCK // 2
    new_cells, new_materials = (new_meta_ref[0:1, :], new_meta_ref[1:2, :])

    def store_new(c, k, value):
        wide_ref[c * BLOCK + k * SUB : c * BLOCK + (k + 1) * SUB, :] = value
        wide_ref[c * BLOCK + half + k * SUB : c * BLOCK + half + (k + 1) * SUB, :] = pltpu.roll(value, BLOCK, 1)

    load_new = lambda c, k: turned_ref[c * half + k * SUB : c * half + (k + 1) * SUB, :]
    near = gathered(parts, new_cells)
    move_points(load_new, store_new, half // SUB, near, new_materials, shear_ref, lame_ref)
    new_ref[...] = wide_ref[...].T[0 : 4 * MCAP]


def assemble(
    old_ref, new_ref, old_meta_ref, new_meta_ref, xi_ref, xo_ref, yi_ref, yo_ref,
    points_ref, cells_ref, mats_ref,
):
    old, new = (old_ref.shape[0], 4 * MCAP)
    points_ref[0:old, :] = old_ref[...]
    points_ref[old : old + new, :] = new_ref[...]
    boxes = regions(xi_ref[...], xo_ref[...], yi_ref[...], yo_ref[...])
    for index, box in enumerate(boxes):
        start = old + new + index * MCAP
        points_ref[start : start + MCAP, :] = box[0:MCAP]
    last_meta = arrived_meta(boxes)
    lane = iota((1, LANES), 1)
    for row, ref in ((0, cells_ref), (1, mats_ref)):
        ref[0:1, :] = old_meta_ref[row : row + 1, :]
        ref[1:2, :] = jnp.where(lane < new, new_meta_ref[row : row + 1, :], last_meta[row : row + 1])


def shards(
    points,
    block_cell,
    block_mat,
    density,
    shear_modulus,
    lame_modulus,
    mig_slot_a,
    mig_dest_a,
    mig_cell_a,
    mig_slot_b,
    mig_dest_b,
    mig_cell_b,
):
    wide = 8 * BLOCK
    I32 = jnp.int32
    blank = jnp.zeros((LANES,), I32)
    meta = jnp.stack([block_cell, block_mat] + [blank] * 6)
    lists = []
    for entries in ((mig_slot_a, mig_dest_a, mig_cell_a), (mig_slot_b, mig_dest_b, mig_cell_b)):
        rows = [jnp.pad(e, (0, LANES - e.shape[0]), constant_values=-1) for e in entries]
        lists.append(jnp.stack(rows + [blank] * 5))

    halo = ((HALO, LANES), F32)
    tile = ((SUB, LANES), F32)
    tags = ((SUB, LANES), I32)
    grid = ((ROWS, LANES), F32)
    message = ((MSG, wide), F32)
    turned_form = ((wide, LANES), F32)
    half_form = ((wide // 2, LANES), F32)

    def exchange_sums(sums, inner, outer):
        from_inner, from_outer = (swap(inner, "gx", 0), swap(outer, "gx", 1))
        merged, inner, outer = call(
            merge_depth, (grid, tile, tile), (), (IN_VMEM,) * 3, sums, from_inner, from_outer
        )
        return (merged, swap(inner, "gy", 0), swap(outer, "gy", 1))

    def exchange_blocks(messages):
        return (
            swap(messages[0], "gx", 0),
            swap(messages[1], "gx", 1),
            swap(messages[2], "gy", 0),
            swap(messages[3], "gy", 1),
        )

    sums, inner, outer, turned = call(
        sums_one,
        (grid, halo, halo, turned_form),
        (pltpu.VMEM((ROWS, 4 * LANES), F32),),
        (IN_VMEM, IN_VMEM, IN_SMEM),
        points, meta, density,
    )
    merged, from_inner, from_outer = exchange_sums(sums, inner, outer)
    kept, kept_meta, *messages = call(
        advance_one,
        (turned_form, tags) + (message,) * 4,
        (pltpu.VMEM((ROWS, LANES), F32), pltpu.VMEM((wide, LANES), F32)),
        (IN_VMEM,) * 6 + (IN_SMEM,) * 2,
        turned, meta, lists[0], merged, from_inner, from_outer, shear_modulus, lame_modulus,
    )
    arrived = exchange_blocks(messages)
    sums, inner, outer, turned, new_meta = call(
        sums_two,
        (grid, halo, halo, half_form, tags),
        (pltpu.VMEM((ROWS, 8 * LANES), F32), pltpu.VMEM((wide, LANES), F32)),
        (IN_VMEM,) * 6 + (IN_SMEM,),
        kept, kept_meta, *arrived, density,
    )
    merged, from_inner, from_outer = exchange_sums(sums, inner, outer)
    old, new, old_meta, *messages = call(
        advance_two,
        (((LANES, wide), F32), ((4 * MCAP, wide), F32), tags) + (message,) * 4,
        (
            pltpu.VMEM((ROWS, LANES), F32),
            pltpu.VMEM((wide, LANES), F32),
            pltpu.VMEM((wide, LANES), F32),
        ),
        (IN_VMEM,) * 8 + (IN_SMEM,) * 2,
        kept, kept_meta, turned, new_meta, lists[1], merged, from_inner, from_outer, shear_modulus, lame_modulus,
    )
    arrived = exchange_blocks(messages)
    final_points, cells, mats = call(
        assemble,
        (((2 * LANES, wide), F32), ((2, LANES), I32), ((2, LANES), I32)),
        (),
        (IN_VMEM,) * 8,
        old, new, old_meta, new_meta, *arrived,
    )
    return (final_points, cells.reshape(-1), mats.reshape(-1))


def solution(mesh):
    split = P(("gx", "gy"))
    rows = P(("gx", "gy"), None)
    return jax.shard_map(
        shards,
        mesh=mesh,
        in_specs=(rows, split, split, P(), P(), P()) + (split,) * 6,
        out_specs=(rows, split, split),
        check_vma=False,
    )
```

```python
import jax
import jax.numpy as jnp
from jax import lax
from jax.experimental import pallas as pl
from jax.experimental.pallas import tpu as pltpu
from jax.sharding import PartitionSpec as P

CX = 16
CY = 32
BLOCK = 64
NMAT = 8
MCAP = 16
LANES = 128
SUB = 8
ROWS = 160
HALO = 24
TOP = CX * SUB
MSG = MCAP + SUB

TIME_STEP = 0.2
MASS_FLOOR = 0.25
VOLUME = 1.0 / BLOCK
VMEM_LIMIT = 12 * 1024 * 1024

IN_VMEM = pl.BlockSpec(memory_space=pltpu.VMEM)
IN_HBM = pl.BlockSpec(memory_space=pltpu.HBM)
F32 = jnp.float32
BF16 = jnp.bfloat16
NN = (((1,), (0,)), ((), ()))
NT = (((1,), (1,)), ((), ()))


def call(kernel, outs, scratch, in_specs, *operands, out_specs=None, aliases=None):
    return pl.pallas_call(
        kernel,
        out_shape=tuple(jax.ShapeDtypeStruct(shape, dtype) for shape, dtype in outs),
        in_specs=in_specs,
        out_specs=out_specs or tuple(IN_VMEM for _ in outs),
        scratch_shapes=scratch,
        input_output_aliases=aliases or {},
        compiler_params=pltpu.CompilerParams(vmem_limit_bytes=VMEM_LIMIT),
        cost_estimate=pl.CostEstimate(flops=1 << 22, bytes_accessed=1 << 19, transcendentals=0),
    )(*operands)


def swap(value, axis, first):
    count = lax.axis_size(axis)
    pairs = []
    for low in range(first, count - 1, 2):
        pairs += [(low, low + 1), (low + 1, low)]
    return lax.ppermute(value, axis, pairs)


def iota(shape, dim):
    return lax.broadcasted_iota(jnp.int32, shape, dim)


def thirds(value):
    high = value.astype(BF16)
    rest = value - high.astype(F32)
    middle = rest.astype(BF16)
    low = (rest - middle.astype(F32)).astype(BF16)
    return (high, middle, low)


def product(parts, onehot, dims):
    total = None
    for part in parts:
        term = lax.dot_general(part, onehot, dims, preferred_element_type=F32)
        total = term if total is None else total + term
    return total


def stencil(u):
    p = jnp.maximum(0.25 - u, 0.0)
    q = jnp.maximum(u - 0.75, 0.0)
    p2 = p * p
    q2 = q * q
    weight = (p2, (1.0 - u) - 2.0 * p2 + q2, u + p2 - 2.0 * q2, q2)
    slope = (-2.0 * p, 4.0 * p + 2.0 * q - 1.0, 1.0 - 2.0 * p - 4.0 * q, 2.0 * q)
    return (weight, slope)


def by_material(materials, tables_ref, which):
    value = jnp.zeros(materials.shape, F32)
    for index in range(NMAT):
        row = which * NMAT + index
        value = jnp.where(materials == index, tables_ref[row : row + 1, :], value)
    return value


def column_onehot(cells):
    cross = jnp.broadcast_to(cells & (CY - 1), (LANES, LANES))
    column = iota((LANES, LANES), 0)
    return [(column == cross + b).astype(F32).astype(BF16) for b in range(4)]


def row_masks(cells):
    depth = jnp.broadcast_to(cells >> 5, (SUB, LANES))
    return [depth == index for index in range(CX)]


def node_terms(load, chunks, rho):
    sub = iota((SUB, LANES), 0)
    scale = jnp.where(sub < 3, jnp.broadcast_to(rho * VOLUME, (SUB, LANES)), -VOLUME)
    scale = jnp.where(sub < 5, scale, 0.0)
    stencils = [(stencil(load(0, k)), stencil(load(1, k))) for k in range(chunks)]
    terms = [[None] * 4 for _ in range(4)]
    for b in range(4):
        acc = [[None] * 5 for _ in range(4)]
        for k in range(chunks):
            (weight_x, slope_x), (weight_y, slope_y) = stencils[k]
            wy, dy = weight_y[b], slope_y[b]
            sxy = load(6, k)
            y1 = wy * load(2, k)
            y2 = wy * load(3, k)
            y3 = wy * load(4, k)
            y4 = wy * sxy
            y5 = dy * sxy
            y6 = dy * load(5, k)
            for a in range(4):
                wx, dx = weight_x[a], slope_x[a]
                new = (wx * wy, wx * y1, wx * y2, dx * y3 + wx * y5, dx * y4 + wx * y6)
                acc[a] = [n if o is None else o + n for o, n in zip(acc[a], new)]
        for a in range(4):
            packed = jnp.zeros((SUB, LANES), F32)
            for q in range(5):
                total = jnp.sum(acc[a][q], axis=0, keepdims=True)
                packed = jnp.where(sub == q, jnp.broadcast_to(total, (SUB, LANES)), packed)
            terms[a][b] = packed * scale
    return terms


def spread_rows(terms, masks, left_ref, lane):
    zero = jnp.zeros((SUB, LANES), F32)
    for b in range(4):
        for x in range(ROWS // SUB):
            total = zero
            for a in range(4):
                if 0 <= x - a < CX:
                    total = total + jnp.where(masks[x - a], terms[a][b], zero)
            left_ref[x * SUB : (x + 1) * SUB, lane + b * LANES : lane + (b + 1) * LANES] = total


def parity(axis):
    return (lax.axis_index(axis) & 1) == 1


def emit_sums(left_ref, onehots, more_ref, sums_ref, inner_ref, outer_ref):
    sums = product(thirds(left_ref[...]), jnp.concatenate(onehots, axis=1), NT)
    if more_ref is not None:
        sums = sums + more_ref[...]
    sums_ref[...] = sums
    odd = parity("gx")
    bottom, top = (sums[0:HALO], sums[TOP : TOP + HALO])
    inner_ref[...] = jnp.where(odd, bottom, top)
    outer_ref[...] = jnp.where(odd, top, bottom)


def turn(points_ref, turned_ref):
    turned_ref[...] = points_ref[...].T


def sums_one(
    turned_ref, cells_ref, mats_ref, density_ref, shear_ref, lame_ref,
    sums_ref, inner_ref, outer_ref, tables_ref, meta_ref,
    left_ref,
):
    for which, table_ref in enumerate((density_ref, shear_ref, lame_ref)):
        table = table_ref[...]
        for index in range(NMAT):
            row = which * NMAT + index
            tables_ref[row : row + 1, :] = jnp.broadcast_to(table[:, index : index + 1], (1, LANES))
    cells, materials = (cells_ref[...], mats_ref[...])
    meta_ref[0:1, :] = cells
    meta_ref[1:2, :] = materials
    rho = by_material(materials, tables_ref, 0)
    load = lambda c, k: turned_ref[c * BLOCK + k * SUB : c * BLOCK + (k + 1) * SUB, :]
    terms = node_terms(load, BLOCK // SUB, rho)
    spread_rows(terms, row_masks(cells), left_ref, 0)
    emit_sums(left_ref, column_onehot(cells), None, sums_ref, inner_ref, outer_ref)


def join_lists(*refs):
    *list_refs, lists_ref = refs
    for index, ref in enumerate(list_refs):
        row = ref[...]
        rest = jnp.full((1, LANES - row.shape[1]), -1, jnp.int32)
        lists_ref[index : index + 1, :] = jnp.concatenate([row, rest], axis=1)


def regions(from_inner_x, from_outer_x, from_inner_y, from_outer_y):
    odd_x, odd_y = (parity("gx"), parity("gy"))
    return (
        jnp.where(odd_x, from_inner_x, from_outer_x),
        jnp.where(odd_x, from_outer_x, from_inner_x),
        jnp.where(odd_y, from_inner_y, from_outer_y),
        jnp.where(odd_y, from_outer_y, from_inner_y),
    )


def arrived_meta(boxes):
    packed = boxes[0]
    for index in range(1, 4):
        packed = packed + pltpu.roll(boxes[index], MCAP * index, 1)
    packed = packed + pltpu.roll(packed, 4 * MCAP, 1)
    sub = iota((SUB, LANES), 0)
    return packed.astype(jnp.int32) - (sub == 1).astype(jnp.int32)


def sums_kept(fresh_ref, kept_meta_ref, tables_ref, sums_ref, kept_ref, left_ref):
    cells, materials = (kept_meta_ref[0:1, :], kept_meta_ref[1:2, :])
    alive = jnp.broadcast_to(materials, fresh_ref.shape) >= 0
    kept_ref[...] = jnp.where(alive, fresh_ref[...], 0.0)
    load = lambda c, k: kept_ref[c * BLOCK + k * SUB : c * BLOCK + (k + 1) * SUB, :]
    terms = node_terms(load, BLOCK // SUB, by_material(materials, tables_ref, 0))
    spread_rows(terms, row_masks(cells), left_ref, 0)
    sums_ref[...] = product(thirds(left_ref[...]), jnp.concatenate(column_onehot(cells), axis=1), NT)


def sums_two(
    kept_sums_ref, xo_ref, yo_ref, yi_ref, xi_ref, tables_ref,
    sums_ref, inner_ref, outer_ref, turned_ref, new_meta_ref,
    left_ref, wide_ref,
):
    boxes = regions(xi_ref[...], xo_ref[...], yi_ref[...], yo_ref[...])
    new_meta = arrived_meta([box[MCAP:MSG, 0:LANES] for box in boxes])
    new_meta_ref[...] = new_meta
    rows = jnp.concatenate([box[0:MCAP] for box in boxes], axis=0)
    wide_ref[...] = jnp.concatenate([rows, jnp.zeros_like(rows)], axis=0).T
    half = BLOCK // 2
    for c in range(8):
        first = wide_ref[c * BLOCK : c * BLOCK + half, :]
        second = wide_ref[c * BLOCK + half : (c + 1) * BLOCK, :]
        turned_ref[c * half : (c + 1) * half, :] = first + pltpu.roll(second, BLOCK, 1)
    cells, materials = (new_meta[0:1], new_meta[1:2])
    load = lambda c, k: turned_ref[c * half + k * SUB : c * half + (k + 1) * SUB, :]
    terms = node_terms(load, half // SUB, by_material(materials, tables_ref, 0))
    spread_rows(terms, row_masks(cells), left_ref, 0)
    emit_sums(left_ref, column_onehot(cells), kept_sums_ref, sums_ref, inner_ref, outer_ref)


def merge_depth(sums_ref, from_outer_ref, from_inner_ref, merged_ref, inner_ref, outer_ref):
    odd = parity("gx")
    from_inner, from_outer = (from_inner_ref[...], from_outer_ref[...])
    merged_ref[...] = sums_ref[...]
    merged_ref[0:HALO] = sums_ref[0:HALO] + jnp.where(odd, from_inner, from_outer)
    merged_ref[TOP : TOP + HALO] = sums_ref[TOP : TOP + HALO] + jnp.where(odd, from_outer, from_inner)
    lane = iota((SUB, LANES), 1)
    low = jnp.zeros((SUB, LANES), F32)
    high = jnp.zeros((SUB, LANES), F32)
    for x in range(CX + 3):
        row = merged_ref[x * SUB : (x + 1) * SUB, :]
        here = (lane >= 3 * x) & (lane < 3 * x + 3)
        shift = 3 * x
        low = jnp.where(here, pltpu.roll(row, shift, 1) if shift else row, low)
        high = jnp.where(here, pltpu.roll(row, (shift - CY) % LANES, 1), high)
    odd_y = parity("gy")
    inner_ref[...] = jnp.where(odd_y, low, high)
    outer_ref[...] = jnp.where(odd_y, high, low)


def node_velocity(merged_ref, from_inner_ref, from_outer_ref, velocity_ref):
    odd_y = parity("gy")
    from_inner, from_outer = (from_inner_ref[...], from_outer_ref[...])
    low = jnp.where(odd_y, from_inner, from_outer)
    high = jnp.where(odd_y, from_outer, from_inner)
    lane = iota((SUB, LANES), 1)
    total_x = CX * lax.axis_size("gx")
    total_y = CY * lax.axis_size("gy")
    base_x = lax.axis_index("gx") * CX - 1
    node_y = lax.axis_index("gy") * CY - 1 + lane
    inside_y = (node_y > 0) & (node_y < total_y - 1)
    for x in range(ROWS // SUB):
        row = merged_ref[x * SUB : (x + 1) * SUB, :]
        if x < CX + 3:
            shift = 3 * x
            row = row + jnp.where(lane < 3, pltpu.roll(low, (-shift) % LANES, 1) if shift else low, 0.0)
            row = row + jnp.where(
                (lane >= CY) & (lane < CY + 3), pltpu.roll(high, (CY - shift) % LANES, 1), 0.0
            )
        mass = jnp.maximum(jnp.broadcast_to(row[0:1], (SUB, LANES)), MASS_FLOOR)
        value = (row + TIME_STEP * pltpu.roll(row, SUB - 2, 0)) / mass
        node_x = base_x + x
        inside_x = (node_x > 0) & (node_x < total_x - 1)
        velocity_ref[x * SUB : (x + 1) * SUB, :] = jnp.where(inside_y & inside_x, value, 0.0)


def gathered(velocity_parts, cells):
    masks = row_masks(cells)
    near = [[None] * 4 for _ in range(4)]
    for b, onehot in enumerate(column_onehot(cells)):
        column = product(velocity_parts, onehot, NN)
        for a in range(4):
            total = jnp.zeros((SUB, LANES), F32)
            for x in range(CX):
                total = jnp.where(masks[x], column[(x + a) * SUB : (x + a + 1) * SUB], total)
            near[a][b] = total
    return near


def move_points(load, store, chunks, near, materials, tables_ref):
    wide = lambda row: jnp.broadcast_to(row, (SUB, LANES))
    twice_shear = wide(2.0 * by_material(materials, tables_ref, 1))
    lame = wide(by_material(materials, tables_ref, 2))
    alive = wide(materials) >= 0
    for k in range(chunks):
        u, v = (load(0, k), load(1, k))
        weight_x, slope_x = stencil(u)
        weight_y, slope_y = stencil(v)
        speed, along, across = ([], [], [])
        for row in (1, 2):
            value = rate_x = rate_y = None
            for a in range(4):
                inner = slant = None
                for b in range(4):
                    node = wide(near[a][b][row : row + 1])
                    term, tilt = (weight_y[b] * node, slope_y[b] * node)
                    inner = term if b == 0 else inner + term
                    slant = tilt if b == 0 else slant + tilt
                add = (weight_x[a] * inner, slope_x[a] * inner, weight_x[a] * slant)
                if a == 0:
                    value, rate_x, rate_y = add
                else:
                    value, rate_x, rate_y = (value + add[0], rate_x + add[1], rate_y + add[2])
            speed.append(value)
            along.append(rate_x)
            across.append(rate_y)
        rate_xx, rate_yy = (along[0], across[1])
        rate_xy = 0.5 * (across[0] + along[1])
        spherical = lame * (rate_xx + rate_yy)
        stress_xx = load(4, k) + TIME_STEP * (twice_shear * rate_xx + spherical)
        stress_yy = load(5, k) + TIME_STEP * (twice_shear * rate_yy + spherical)
        stress_xy = load(6, k) + TIME_STEP * twice_shear * rate_xy
        fresh = (
            jnp.clip(u + TIME_STEP * speed[0], 0.0, 1.0),
            jnp.clip(v + TIME_STEP * speed[1], 0.0, 1.0),
            speed[0],
            speed[1],
            stress_xx,
            stress_yy,
            stress_xy,
            jnp.maximum(load(7, k), -0.5 * (stress_xx + stress_yy)),
        )
        for c in range(8):
            store(c, k, jnp.where(alive, fresh[c], 0.0))


def outgoing(fresh, materials, lists, message_refs):
    across = lax.axis_size("gy")
    gx, gy = (lax.axis_index("gx"), lax.axis_index("gy"))
    home = gx * across + gy
    step_x = across - 2 * across * (gx & 1)
    step_y = 1 - 2 * (gy & 1)
    slots, dests, places = (lists[0:1], lists[1:2], lists[2:3])
    dest = jnp.broadcast_to(dests, (2 * SUB, LANES))
    sub = iota((2 * SUB, LANES), 0)
    matched = jnp.zeros((2 * SUB, LANES), F32)
    for o, target in enumerate((home + step_x, home - step_x, home + step_y, home - step_y)):
        matched = jnp.where((sub == o) & (dest == target), 1.0, matched)
    square = (LANES, LANES)
    earlier = (iota(square, 0) < iota(square, 1)).astype(F32).astype(BF16)
    rank = lax.dot_general(matched.astype(BF16), earlier, NN, preferred_element_type=F32)
    place_rank = iota((MCAP, LANES), 0).astype(F32)
    placing = []
    for o in range(4):
        hit = jnp.broadcast_to(rank[o : o + 1], (MCAP, LANES)) == place_rank
        placing.append(jnp.where(hit, jnp.broadcast_to(matched[o : o + 1], (MCAP, LANES)), 0.0))
    placing.append(jnp.zeros((LANES - 4 * MCAP, LANES), F32))
    placing = jnp.concatenate(placing, axis=0).astype(BF16)
    holds = (iota(square, 0) == jnp.broadcast_to(slots, square)).astype(F32).astype(BF16)
    moving = jnp.where((dest >= 0) & (dest != home), 1.0, 0.0).astype(BF16)
    vacated = lax.dot_general(moving, holds, NT, preferred_element_type=F32)[0:1] > 0.5
    chosen = lax.dot_general(placing, holds, NT, preferred_element_type=F32).astype(BF16)
    listed = jnp.where(sub == 0, jnp.broadcast_to(places >> 5, dest.shape), 0)
    listed = jnp.where(sub == 1, jnp.broadcast_to(places & (CY - 1), dest.shape), listed)
    listed = lax.dot_general(listed.astype(F32).astype(BF16), placing, NT, preferred_element_type=F32)
    kinds = jnp.broadcast_to(materials + 1, dest.shape).astype(F32).astype(BF16)
    kinds = lax.dot_general(kinds, chosen, NT, preferred_element_type=F32)
    new_cells = jnp.broadcast_to(listed[0:1] * float(CY) + listed[1:2], (SUB, LANES))
    new_kinds = jnp.broadcast_to(kinds[0:1], (SUB, LANES))
    low_sub, lane = (iota((SUB, LANES), 0), iota((SUB, LANES), 1))
    tags = jnp.where(low_sub == 0, new_cells, jnp.where(low_sub == 1, new_kinds, 0.0))
    total = None
    for part in thirds(fresh):
        term = lax.dot_general(chosen[0 : 4 * MCAP], part, NN, preferred_element_type=F32)
        total = term if total is None else total + term
    for o, ref in enumerate(message_refs):
        ref[0:MCAP, :] = total[o * MCAP : (o + 1) * MCAP]
        tag = pltpu.roll(tags, LANES - o * MCAP, 1) if o else tags
        ref[MCAP:MSG, 0:LANES] = jnp.where(lane < MCAP, tag, 0.0)
        ref[MCAP:MSG, LANES:] = jnp.zeros((SUB, 8 * BLOCK - LANES), F32)
    return vacated


def vacate(cells, materials, vacated):
    first = iota((SUB, LANES), 0) == 0
    gone = jnp.broadcast_to(vacated.astype(F32), (SUB, LANES)) > 0.5
    meta = jnp.where(first, jnp.broadcast_to(cells, gone.shape), jnp.broadcast_to(materials, gone.shape))
    return jnp.where(gone, jnp.where(first, 0, -1), meta)


def advance_old(load, meta_ref, lists, merged_ref, yo_ref, yi_ref, tables_ref, outs, velocity_ref):
    fresh_ref, kept_meta_ref, *message_refs = outs
    cells, materials = (meta_ref[0:1, :], meta_ref[1:2, :])
    node_velocity(merged_ref, yi_ref, yo_ref, velocity_ref)
    at = lambda c, k: slice(c * BLOCK + k * SUB, c * BLOCK + (k + 1) * SUB)

    def store(c, k, value):
        fresh_ref[at(c, k), :] = value

    near = gathered(thirds(velocity_ref[...]), cells)
    move_points(lambda c, k: load(at(c, k)), store, BLOCK // SUB, near, materials, tables_ref)
    vacated = outgoing(fresh_ref[...].T, materials, lists, message_refs)
    kept_meta_ref[...] = vacate(cells, materials, vacated)


def advance_one(
    turned_ref, meta_ref, lists_ref, merged_ref, yo_ref, yi_ref, tables_ref,
    fresh_ref, kept_meta_ref, m0_ref, m1_ref, m2_ref, m3_ref,
    velocity_ref,
):
    advance_old(
        lambda rows: turned_ref[rows, :], meta_ref, lists_ref[0:3, :], merged_ref, yo_ref, yi_ref, tables_ref,
        (fresh_ref, kept_meta_ref, m0_ref, m1_ref, m2_ref, m3_ref), velocity_ref,
    )


def advance_two(
    kept_ref, meta_ref, lists_ref, merged_ref, yo_ref, yi_ref, tables_ref,
    fresh_ref, old_meta_ref, velocity_ref, m0_ref, m1_ref, m2_ref, m3_ref,
):
    advance_old(
        lambda rows: kept_ref[rows, :], meta_ref, lists_ref[3:6, :], merged_ref, yo_ref, yi_ref, tables_ref,
        (fresh_ref, old_meta_ref, m0_ref, m1_ref, m2_ref, m3_ref), velocity_ref,
    )


def settle(
    fresh_ref, old_meta_ref, velocity_ref, turned_ref, new_meta_ref, tables_ref,
    points_ref,
    old_ref, wide_ref, new_ref, sems,
):
    alive = jnp.broadcast_to(old_meta_ref[1:2, :], fresh_ref.shape) >= 0
    old_ref[...] = jnp.where(alive, fresh_ref[...], 0.0).T
    old, new = (LANES, 4 * MCAP)
    first = pltpu.make_async_copy(old_ref, points_ref.at[0:old], sems.at[0])
    first.start()
    half = BLOCK // 2
    cells, materials = (new_meta_ref[0:1, :], new_meta_ref[1:2, :])

    def store(c, k, value):
        wide_ref[c * BLOCK + k * SUB : c * BLOCK + (k + 1) * SUB, :] = value
        wide_ref[c * BLOCK + half + k * SUB : c * BLOCK + half + (k + 1) * SUB, :] = pltpu.roll(value, BLOCK, 1)

    load = lambda c, k: turned_ref[c * half + k * SUB : c * half + (k + 1) * SUB, :]
    near = gathered(thirds(velocity_ref[...]), cells)
    move_points(load, store, half // SUB, near, materials, tables_ref)
    new_ref[...] = wide_ref[...].T[0:new]
    second = pltpu.make_async_copy(new_ref, points_ref.at[old : old + new], sems.at[1])
    second.start()
    first.wait()
    second.wait()


def assemble(
    part_ref, old_meta_ref, new_meta_ref, xo_ref, yo_ref, yi_ref, xi_ref,
    points_ref, cells_ref, mats_ref,
    tags_ref, sems,
):
    del part_ref
    new = 4 * MCAP
    base = points_ref.shape[0] - new
    odd_x, odd_y = (lax.axis_index("gx") & 1, lax.axis_index("gy") & 1)
    copies = []
    for index, (ref, region) in enumerate(
        ((xo_ref, odd_x), (yo_ref, 2 + odd_y), (yi_ref, 3 - odd_y), (xi_ref, 1 - odd_x))
    ):
        start = pl.multiple_of(base + region * MCAP, MCAP)
        copies.append(
            pltpu.make_async_copy(ref.at[0:MCAP, :], points_ref.at[pl.ds(start, MCAP), :], sems.at[index])
        )
        copies[-1].start()
    tiles = [ref[MCAP:MSG, 0:LANES] for ref in (xi_ref, xo_ref, yi_ref, yo_ref)]
    last_meta = arrived_meta(regions(*tiles))
    lane = iota((1, LANES), 1)
    for row, ref in ((0, cells_ref), (1, mats_ref)):
        tags_ref[row, 0:1, :] = old_meta_ref[row : row + 1, :]
        tags_ref[row, 1:2, :] = jnp.where(lane < new, new_meta_ref[row : row + 1, :], last_meta[row : row + 1])
        copies.append(pltpu.make_async_copy(tags_ref.at[row], ref, sems.at[4 + row]))
        copies[-1].start()
    for copy in copies:
        copy.wait()


def shards(
    points,
    block_cell,
    block_mat,
    density,
    shear_modulus,
    lame_modulus,
    mig_slot_a,
    mig_dest_a,
    mig_cell_a,
    mig_slot_b,
    mig_dest_b,
    mig_cell_b,
):
    wide = 8 * BLOCK
    I32 = jnp.int32
    row = lambda value: value.reshape(1, -1)
    cells, mats = (row(block_cell), row(block_mat))
    list_a = (row(mig_slot_a), row(mig_dest_a), row(mig_cell_a))
    list_b = (row(mig_slot_b), row(mig_dest_b), row(mig_cell_b))

    halo = ((HALO, LANES), F32)
    tile = ((SUB, LANES), F32)
    tags = ((SUB, LANES), I32)
    grid = ((ROWS, LANES), F32)
    message = ((MSG, wide), F32)
    turned_form = ((wide, LANES), F32)
    half_form = ((wide // 2, LANES), F32)
    scratch = lambda form: pltpu.VMEM(*form)
    left = pltpu.VMEM((ROWS, 4 * LANES), F32)

    def exchange_sums(sums, inner, outer):
        from_outer = swap(outer, "gx", 1)
        from_inner = swap(inner, "gx", 0)
        merged, inner, outer = call(
            merge_depth, (grid, tile, tile), (), (IN_VMEM,) * 3, sums, from_outer, from_inner
        )
        from_outer = swap(outer, "gy", 1)
        from_inner = swap(inner, "gy", 0)
        return (merged, from_outer, from_inner)

    def exchange_blocks(messages):
        xi, xo, yi, yo = messages
        xo = swap(xo, "gx", 1)
        yo = swap(yo, "gy", 1)
        yi = swap(yi, "gy", 0)
        xi = swap(xi, "gx", 0)
        return (xo, yo, yi, xi)

    (lists,) = call(join_lists, (tags,), (), (IN_VMEM,) * 6, *list_a, *list_b)
    (turned,) = call(turn, (turned_form,), (), (IN_VMEM,), points)
    sums, inner, outer, tables, meta = call(
        sums_one,
        (grid, halo, halo, ((3 * NMAT, LANES), F32), tags),
        (left,),
        (IN_VMEM,) * 6,
        turned, cells, mats, row(density), row(shear_modulus), row(lame_modulus),
    )
    merged, from_outer, from_inner = exchange_sums(sums, inner, outer)
    fresh, kept_meta, *messages = call(
        advance_one,
        (turned_form, tags) + (message,) * 4,
        (scratch(grid),),
        (IN_VMEM,) * 7,
        turned, meta, lists, merged, from_outer, from_inner, tables,
    )
    arrived = exchange_blocks(messages)
    kept_sums, kept = call(
        sums_kept, (grid, turned_form), (left,), (IN_VMEM,) * 3, fresh, kept_meta, tables
    )
    sums, inner, outer, turned, new_meta = call(
        sums_two,
        (grid, halo, halo, half_form, tags),
        (left, scratch(turned_form)),
        (IN_VMEM,) * 6,
        kept_sums, *arrived, tables,
    )
    merged, from_outer, from_inner = exchange_sums(sums, inner, outer)
    fresh, old_meta, velocity, *messages = call(
        advance_two,
        (turned_form, tags, grid) + (message,) * 4,
        (),
        (IN_VMEM,) * 7,
        kept, kept_meta, lists, merged, from_outer, from_inner, tables,
    )
    arrived = exchange_blocks(messages)
    final_form = ((2 * LANES, wide), F32)
    (part,) = call(
        settle,
        (final_form,),
        (
            pltpu.VMEM((LANES, wide), F32),
            scratch(turned_form),
            pltpu.VMEM((4 * MCAP, wide), F32),
            pltpu.SemaphoreType.DMA((2,)),
        ),
        (IN_VMEM,) * 6,
        fresh, old_meta, velocity, turned, new_meta, tables,
        out_specs=(IN_HBM,),
    )
    final_points, final_cells, final_mats = call(
        assemble,
        (final_form, ((2, LANES), I32), ((2, LANES), I32)),
        (pltpu.VMEM((2, 2, LANES), I32), pltpu.SemaphoreType.DMA((6,))),
        (IN_HBM,) + (IN_VMEM,) * 6,
        part, old_meta, new_meta, *arrived,
        out_specs=(IN_HBM,) * 3,
        aliases={0: 0},
    )
    return (final_points, final_cells.reshape(-1), final_mats.reshape(-1))


def solution(mesh):
    split = P(("gx", "gy"))
    rows = P(("gx", "gy"), None)
    return jax.shard_map(
        shards,
        mesh=mesh,
        in_specs=(rows, split, split, P(), P(), P()) + (split,) * 6,
        out_specs=(rows, split, split),
        check_vma=False,
    )
```

```python
import jax
import jax.numpy as jnp
from jax import lax
from jax.experimental import pallas as pl
from jax.experimental.pallas import tpu as pltpu
from jax.sharding import PartitionSpec as P

CX = 16
CY = 32
BLOCK = 64
NMAT = 8
MCAP = 16
LANES = 128
SUB = 8
ROWS = 160
HALO = 24
TOP = CX * SUB
MSG = MCAP + SUB
DEPTHS = CX + 3
PACK = 96
NEAR = 16
SLOT = PACK + NEAR
CROSS_MSG = SUB + 2 * MCAP
SPAN = 3 * CY + 3

TIME_STEP = 0.2
MASS_FLOOR = 0.25
VOLUME = 1.0 / BLOCK
VMEM_LIMIT = 12 * 1024 * 1024

IN_VMEM = pl.BlockSpec(memory_space=pltpu.VMEM)
IN_HBM = pl.BlockSpec(memory_space=pltpu.HBM)
F32 = jnp.float32
BF16 = jnp.bfloat16
NN = (((1,), (0,)), ((), ()))
NT = (((1,), (1,)), ((), ()))


def call(kernel, outs, scratch, in_specs, *operands, out_specs=None, aliases=None):
    return pl.pallas_call(
        kernel,
        out_shape=tuple(jax.ShapeDtypeStruct(shape, dtype) for shape, dtype in outs),
        in_specs=in_specs,
        out_specs=out_specs or tuple(IN_VMEM for _ in outs),
        scratch_shapes=scratch,
        input_output_aliases=aliases or {},
        compiler_params=pltpu.CompilerParams(vmem_limit_bytes=VMEM_LIMIT),
        cost_estimate=pl.CostEstimate(flops=1 << 22, bytes_accessed=1 << 19, transcendentals=0),
    )(*operands)


def swap(value, axis, first):
    count = lax.axis_size(axis)
    pairs = []
    for low in range(first, count - 1, 2):
        pairs += [(low, low + 1), (low + 1, low)]
    return lax.ppermute(value, axis, pairs)


def iota(shape, dim):
    return lax.broadcasted_iota(jnp.int32, shape, dim)


def thirds(value):
    high = value.astype(BF16)
    rest = value - high.astype(F32)
    middle = rest.astype(BF16)
    low = (rest - middle.astype(F32)).astype(BF16)
    return (high, middle, low)


def product(parts, onehot, dims):
    total = None
    for part in parts:
        term = lax.dot_general(part, onehot, dims, preferred_element_type=F32)
        total = term if total is None else total + term
    return total


def stencil(u):
    p = jnp.maximum(0.25 - u, 0.0)
    q = jnp.maximum(u - 0.75, 0.0)
    p2 = p * p
    q2 = q * q
    weight = (p2, (1.0 - u) - 2.0 * p2 + q2, u + p2 - 2.0 * q2, q2)
    slope = (-2.0 * p, 4.0 * p + 2.0 * q - 1.0, 1.0 - 2.0 * p - 4.0 * q, 2.0 * q)
    return (weight, slope)


def by_material(materials, tables_ref, which):
    value = jnp.zeros(materials.shape, F32)
    for index in range(NMAT):
        row = which * NMAT + index
        value = jnp.where(materials == index, tables_ref[row : row + 1, :], value)
    return value


def column_onehot(column_of):
    first = jnp.broadcast_to(column_of, (LANES, LANES))
    column = iota((LANES, LANES), 0)
    return [(column == first + b).astype(F32).astype(BF16) for b in range(4)]


def row_masks(depth_of):
    depth = jnp.broadcast_to(depth_of, (SUB, LANES))
    return [depth == index for index in range(CX)]


def node_terms(load, chunks, rho, alive):
    sub = iota((SUB, LANES), 0)
    scale = jnp.where(sub < 3, jnp.broadcast_to(rho * VOLUME, (SUB, LANES)), -VOLUME)
    scale = jnp.where((sub < 5) & jnp.broadcast_to(alive, (SUB, LANES)), scale, 0.0)
    stencils = [(stencil(load(0, k)), stencil(load(1, k))) for k in range(chunks)]
    terms = [[None] * 4 for _ in range(4)]
    for b in range(4):
        acc = [[None] * 5 for _ in range(4)]
        for k in range(chunks):
            (weight_x, slope_x), (weight_y, slope_y) = stencils[k]
            wy, dy = weight_y[b], slope_y[b]
            sxy = load(6, k)
            y1 = wy * load(2, k)
            y2 = wy * load(3, k)
            y3 = wy * load(4, k)
            y4 = wy * sxy
            y5 = dy * sxy
            y6 = dy * load(5, k)
            for a in range(4):
                wx, dx = weight_x[a], slope_x[a]
                new = (wx * wy, wx * y1, wx * y2, dx * y3 + wx * y5, dx * y4 + wx * y6)
                acc[a] = [n if o is None else o + n for o, n in zip(acc[a], new)]
        for a in range(4):
            packed = jnp.zeros((SUB, LANES), F32)
            for q in range(5):
                total = jnp.sum(acc[a][q], axis=0, keepdims=True)
                packed = jnp.where(sub == q, jnp.broadcast_to(total, (SUB, LANES)), packed)
            terms[a][b] = packed * scale
    return terms


def spread_rows(terms, masks, left_ref):
    zero = jnp.zeros((SUB, LANES), F32)
    for b in range(4):
        for x in range(ROWS // SUB):
            total = zero
            for a in range(4):
                if 0 <= x - a < CX:
                    total = total + jnp.where(masks[x - a], terms[a][b], zero)
            left_ref[x * SUB : (x + 1) * SUB, b * LANES : (b + 1) * LANES] = total


def parity(axis):
    return (lax.axis_index(axis) & 1) == 1


def emit_sums(left_ref, onehots, more_ref, sums_ref, inner_ref, outer_ref):
    sums = product(thirds(left_ref[...]), jnp.concatenate(onehots, axis=1), NT)
    if more_ref is not None:
        sums = sums + more_ref[...]
    sums_ref[...] = sums
    odd = parity("gx")
    bottom, top = (sums[0:HALO], sums[TOP : TOP + HALO])
    inner_ref[...] = jnp.where(odd, bottom, top)
    outer_ref[...] = jnp.where(odd, top, bottom)


def turn(points_ref, turned_ref):
    turned_ref[...] = points_ref[...].T


def sums_one(
    turned_ref, cells_ref, mats_ref, density_ref, shear_ref, lame_ref,
    sums_ref, inner_ref, outer_ref, tables_ref, meta_ref,
    left_ref,
):
    for which, table_ref in enumerate((density_ref, shear_ref, lame_ref)):
        table = table_ref[...]
        for index in range(NMAT):
            row = which * NMAT + index
            tables_ref[row : row + 1, :] = jnp.broadcast_to(table[:, index : index + 1], (1, LANES))
    cells, materials = (cells_ref[...], mats_ref[...])
    meta_ref[0:1, :] = cells
    meta_ref[1:2, :] = materials
    rho = by_material(materials, tables_ref, 0)
    load = lambda c, k: turned_ref[c * BLOCK + k * SUB : c * BLOCK + (k + 1) * SUB, :]
    terms = node_terms(load, BLOCK // SUB, rho, materials >= 0)
    spread_rows(terms, row_masks(cells >> 5), left_ref)
    emit_sums(left_ref, column_onehot(cells & (CY - 1)), None, sums_ref, inner_ref, outer_ref)


def join_lists(*refs):
    *list_refs, lists_ref = refs
    for index, ref in enumerate(list_refs):
        row = ref[...]
        rest = jnp.full((1, LANES - row.shape[1]), -1, jnp.int32)
        lists_ref[index : index + 1, :] = jnp.concatenate([row, rest], axis=1)


def by_side(inner, outer, odd):
    return (jnp.where(odd, inner, outer), jnp.where(odd, outer, inner))


def matches(dests, targets):
    dest = jnp.broadcast_to(dests, (2 * SUB, LANES))
    sub = iota(dest.shape, 0)
    matched = jnp.zeros(dest.shape, F32)
    for o, target in enumerate(targets):
        matched = jnp.where((sub == o) & (dest == target), 1.0, matched)
    square = (LANES, LANES)
    earlier = (iota(square, 0) < iota(square, 1)).astype(F32).astype(BF16)
    rank = lax.dot_general(matched.astype(BF16), earlier, NN, preferred_element_type=F32)
    return (matched, rank)


def placing_rows(matched, rank, groups):
    blank = jnp.zeros((MCAP, LANES), F32)
    place = iota((MCAP, LANES), 0).astype(F32)
    rows = []
    for o in groups:
        if o is None:
            rows.append(blank)
            continue
        hit = jnp.broadcast_to(rank[o : o + 1], blank.shape) == place
        rows.append(jnp.where(hit, jnp.broadcast_to(matched[o : o + 1], blank.shape), 0.0))
    rows += [blank] * (LANES // MCAP - len(groups))
    return jnp.concatenate(rows, axis=0).astype(BF16)


def holding(slots):
    square = (LANES, LANES)
    return (iota(square, 0) == jnp.broadcast_to(slots, square)).astype(F32).astype(BF16)


def small_rows(*rows):
    sub = iota((2 * SUB, LANES), 0)
    value = jnp.zeros((2 * SUB, LANES), F32)
    for index, row in enumerate(rows):
        value = jnp.where(sub == index, jnp.broadcast_to(row.astype(F32), value.shape), value)
    return value.astype(BF16)


def turned_to(small, onehot):
    return lax.dot_general(small, onehot, NT, preferred_element_type=F32)


def tag_tile(*rows):
    sub = iota((SUB, LANES), 0)
    tile = jnp.zeros((SUB, LANES), F32)
    for index, row in enumerate(rows):
        tile = jnp.where(sub == index, jnp.broadcast_to(row, tile.shape), tile)
    return tile


def home_and_steps():
    across = lax.axis_size("gy")
    gx, gy = (lax.axis_index("gx"), lax.axis_index("gy"))
    return (gx * across + gy, across - 2 * across * (gx & 1), 1 - 2 * (gy & 1))


def pick_cross(points_ref, meta_ref, lists_ref, rows_ref, tags_ref, chosen_ref):
    home, _, step_y = home_and_steps()
    chosen = places = None
    for first, groups in ((0, (0, None, 1, None)), (3, (None, 0, None, 1))):
        matched, rank = matches(lists_ref[first + 1 : first + 2, :], (home + step_y, home - step_y))
        placing = placing_rows(matched, rank, groups)
        part = turned_to(placing, holding(lists_ref[first : first + 1, :]))
        cell = lists_ref[first + 2 : first + 3, :]
        place = turned_to(small_rows(cell >> 5, cell & (CY - 1)), placing)
        chosen = part if chosen is None else chosen + part
        places = place if places is None else places + place
    chosen_ref[...] = chosen
    onehot = chosen.astype(BF16)
    cells, materials = (meta_ref[0:1, :], meta_ref[1:2, :])
    found = turned_to(small_rows(materials + 1, cells >> 5, cells & (CY - 1)), onehot)
    tags_ref[...] = tag_tile(
        places[0:1] * float(CY) + places[1:2], found[0:1], found[1:2] * float(CY) + found[2:3]
    )
    total = None
    for part in thirds(points_ref[...]):
        term = lax.dot_general(onehot[0 : 4 * MCAP], part, NN, preferred_element_type=F32)
        total = term if total is None else total + term
    rows_ref[...] = total


def merge_rows(sums_ref, from_outer_ref, from_inner_ref, merged_ref):
    from_low, from_high = by_side(from_inner_ref[...], from_outer_ref[...], parity("gx"))
    merged_ref[...] = sums_ref[...]
    merged_ref[0:HALO] = sums_ref[0:HALO] + from_low
    merged_ref[TOP : TOP + HALO] = sums_ref[TOP : TOP + HALO] + from_high


def merge_one(
    sums_ref, from_outer_ref, from_inner_ref, rows_ref, tags_ref,
    merged_ref, inner_ref, outer_ref,
):
    merge_rows(sums_ref, from_outer_ref, from_inner_ref, merged_ref)
    lane = iota((SUB, LANES), 1)
    low = jnp.zeros((SUB, LANES), F32)
    high = jnp.zeros((SUB, LANES), F32)
    for x in range(DEPTHS):
        row = merged_ref[x * SUB : (x + 1) * SUB, :]
        here = (lane >= 3 * x) & (lane < 3 * x + 3)
        shift = 3 * x
        low = jnp.where(here, pltpu.roll(row, shift, 1) if shift else row, low)
        high = jnp.where(here, pltpu.roll(row, (shift - CY) % LANES, 1), high)
    to_inner, to_outer = by_side(low, high, parity("gy"))
    movers = 2 * MCAP
    tags = tags_ref[...]
    for ref, halo, tag, first in (
        (inner_ref, to_inner, tags, 0),
        (outer_ref, to_outer, pltpu.roll(tags, LANES - movers, 1), movers),
    ):
        ref[0:SUB, 0:LANES] = halo
        ref[0:SUB, LANES : 2 * LANES] = jnp.where(lane < movers, tag, 0.0)
        ref[0:SUB, 2 * LANES :] = jnp.zeros((SUB, 8 * BLOCK - 2 * LANES), F32)
        ref[SUB:CROSS_MSG, :] = rows_ref[first : first + movers, :]


def merge_two(sums_ref, from_outer_ref, from_inner_ref, near_ref, slots_ref, merged_ref, slot_ref):
    merge_rows(sums_ref, from_outer_ref, from_inner_ref, merged_ref)
    slot_ref[PACK - SUB : PACK, :] = jnp.zeros((SUB, LANES), F32)
    for x in range(DEPTHS):
        slot_ref[5 * x : 5 * x + 5, :] = merged_ref[x * SUB : x * SUB + 5, :]
    slot_ref[PACK:SLOT, :] = near_ref[...]
    value = slot_ref[...]
    for index in range(slots_ref.shape[0]):
        slots_ref[index] = value


def put_velocity(row, x, node_y, velocity_ref):
    node_x = lax.axis_index("gx") * CX - 1 + x
    inside_x = (node_x > 0) & (node_x < CX * lax.axis_size("gx") - 1)
    inside_y = (node_y > 0) & (node_y < CY * lax.axis_size("gy") - 1)
    mass = jnp.maximum(jnp.broadcast_to(row[0:1], (SUB, LANES)), MASS_FLOOR)
    value = (row + TIME_STEP * pltpu.roll(row, SUB - 2, 0)) / mass
    velocity_ref[x * SUB : (x + 1) * SUB, :] = jnp.where(inside_y & inside_x, value, 0.0)


def velocity_one(merged_ref, from_inner, from_outer, velocity_ref):
    low, high = by_side(from_inner, from_outer, parity("gy"))
    lane = iota((SUB, LANES), 1)
    node_y = lax.axis_index("gy") * CY - 1 + lane
    for x in range(DEPTHS):
        row = merged_ref[x * SUB : (x + 1) * SUB, :]
        shift = 3 * x
        row = row + jnp.where(lane < 3, pltpu.roll(low, LANES - shift, 1) if shift else low, 0.0)
        row = row + jnp.where(
            (lane >= CY) & (lane < CY + 3), pltpu.roll(high, (CY - shift) % LANES, 1), 0.0
        )
        put_velocity(row, x, node_y, velocity_ref)
    velocity_ref[DEPTHS * SUB :, :] = jnp.zeros((ROWS - DEPTHS * SUB, LANES), F32)


def velocity_two(slots_ref, packed_ref, velocity_ref):
    gy = lax.axis_index("gy")
    lane = iota((PACK, LANES), 1)
    total = jnp.zeros((PACK, LANES), F32)
    for index in range(slots_ref.shape[0]):
        shift = CY * (index - gy)
        moved = pltpu.roll(slots_ref[index, 0:PACK, :], shift & (LANES - 1), 1)
        valid = (lane >= shift) & (lane < SPAN + shift) & (lane < SPAN)
        total = total + jnp.where(valid, moved, 0.0)
    packed_ref[0:PACK, :] = total
    packed_ref[PACK:, :] = jnp.zeros((packed_ref.shape[0] - PACK, LANES), F32)
    node_y = (gy - 1) * CY - 1 + iota((SUB, LANES), 1)
    for x in range(DEPTHS):
        put_velocity(packed_ref[5 * x : 5 * x + SUB, :], x, node_y, velocity_ref)
    velocity_ref[DEPTHS * SUB :, :] = jnp.zeros((ROWS - DEPTHS * SUB, LANES), F32)


def gathered(velocity_parts, depth_of, column_of):
    masks = row_masks(depth_of)
    near = [[None] * 4 for _ in range(4)]
    for b, onehot in enumerate(column_onehot(column_of)):
        column = product(velocity_parts, onehot, NN)
        for a in range(4):
            total = jnp.zeros((SUB, LANES), F32)
            for x in range(CX):
                total = jnp.where(masks[x], column[(x + a) * SUB : (x + a + 1) * SUB], total)
            near[a][b] = total
    return near


def move_points(load, store, chunks, node_of, materials, tables_ref):
    wide = lambda row: jnp.broadcast_to(row, (SUB, LANES))
    twice_shear = wide(2.0 * by_material(materials, tables_ref, 1))
    lame = wide(by_material(materials, tables_ref, 2))
    alive = wide(materials) >= 0
    for k in range(chunks):
        u, v = (load(0, k), load(1, k))
        weight_x, slope_x = stencil(u)
        weight_y, slope_y = stencil(v)
        speed, along, across = ([], [], [])
        for component in range(2):
            value = rate_x = rate_y = None
            for a in range(4):
                inner = slant = None
                for b in range(4):
                    node = wide(node_of(a, b, component))
                    term, tilt = (weight_y[b] * node, slope_y[b] * node)
                    inner = term if b == 0 else inner + term
                    slant = tilt if b == 0 else slant + tilt
                add = (weight_x[a] * inner, slope_x[a] * inner, weight_x[a] * slant)
                if a == 0:
                    value, rate_x, rate_y = add
                else:
                    value, rate_x, rate_y = (value + add[0], rate_x + add[1], rate_y + add[2])
            speed.append(value)
            along.append(rate_x)
            across.append(rate_y)
        rate_xx, rate_yy = (along[0], across[1])
        rate_xy = 0.5 * (across[0] + along[1])
        spherical = lame * (rate_xx + rate_yy)
        stress_xx = load(4, k) + TIME_STEP * (twice_shear * rate_xx + spherical)
        stress_yy = load(5, k) + TIME_STEP * (twice_shear * rate_yy + spherical)
        stress_xy = load(6, k) + TIME_STEP * twice_shear * rate_xy
        fresh = (
            jnp.clip(u + TIME_STEP * speed[0], 0.0, 1.0),
            jnp.clip(v + TIME_STEP * speed[1], 0.0, 1.0),
            speed[0],
            speed[1],
            stress_xx,
            stress_yy,
            stress_xy,
            jnp.maximum(load(7, k), -0.5 * (stress_xx + stress_yy)),
        )
        for c in range(8):
            store(c, k, jnp.where(alive, fresh[c], 0.0))


def node_getter(near):
    return lambda a, b, component: near[a][b][component + 1 : component + 2]


def emit_movers(fresh, materials, lists, far_ref, near_ref):
    home, step_x, _ = home_and_steps()
    slots, dests, cell = (lists[0:1], lists[1:2], lists[2:3])
    matched, rank = matches(dests, (home - step_x, home + step_x))
    placing = placing_rows(matched, rank, (0, 1))
    chosen = turned_to(placing, holding(slots)).astype(BF16)
    places = turned_to(small_rows(cell >> 5, cell & (CY - 1)), placing)
    kinds = turned_to(small_rows(materials + 1), chosen)
    tags = tag_tile(places[0:1] * float(CY) + places[1:2], kinds[0:1])
    total = None
    for part in thirds(fresh):
        term = lax.dot_general(chosen[0 : 2 * MCAP], part, NN, preferred_element_type=F32)
        total = term if total is None else total + term
    lane = iota((SUB, LANES), 1)
    for o, ref in enumerate((far_ref, near_ref)):
        ref[0:MCAP, :] = total[o * MCAP : (o + 1) * MCAP]
        tag = pltpu.roll(tags, LANES - o * MCAP, 1) if o else tags
        ref[MCAP:MSG, 0:LANES] = jnp.where(lane < MCAP, tag, 0.0)
        ref[MCAP:MSG, LANES:] = jnp.zeros((SUB, 8 * BLOCK - LANES), F32)


def departures(cells, materials, lists):
    home, _, _ = home_and_steps()
    slots, dests, cell = (lists[0:1], lists[1:2], lists[2:3])
    moving = (dests >= 0) & (dests != home)
    low, high = (dests == home - 1, dests == home + 1)
    cross = jnp.where(low | high, 1, 0)
    column = (cell & (CY - 1)) + jnp.where(high, 2 * CY, 0)
    entries = small_rows(jnp.where(moving, 1, 0), cross, cross * (cell >> 5), cross * column)
    found = turned_to(entries, holding(slots)).astype(jnp.int32)
    gone, across = (found[0:1] > 0, found[1:2] > 0)
    sub = iota((SUB, LANES), 0)
    wide = lambda value: jnp.broadcast_to(value, (SUB, LANES))
    kept = jnp.where(
        sub == 0,
        wide(jnp.where(gone, 0, cells)),
        wide(jnp.where(gone, -1, materials)),
    )
    target = jnp.where(
        sub == 0,
        wide(jnp.where(across, found[2:3], cells >> 5)),
        jnp.where(
            sub == 1,
            wide(jnp.where(across, found[3:4], (cells & (CY - 1)) + CY)),
            wide(jnp.where(gone & ~across, -1, materials)),
        ),
    )
    return (kept, target)


def rows_at(ref, c, k, stride):
    return ref[c * stride + k * SUB : c * stride + (k + 1) * SUB, :]


def advance_one(
    turned_ref, meta_ref, lists_ref, merged_ref, yo_ref, yi_ref, tables_ref, chosen_ref,
    fresh_ref, kept_meta_ref, target_ref, near_ref, far_message_ref, near_message_ref,
    velocity_ref, nodes_ref,
):
    velocity_one(merged_ref, yi_ref[0:SUB, 0:LANES], yo_ref[0:SUB, 0:LANES], velocity_ref)
    cells, materials = (meta_ref[0:1, :], meta_ref[1:2, :])

    def store(c, k, value):
        fresh_ref[c * BLOCK + k * SUB : c * BLOCK + (k + 1) * SUB, :] = value

    near = gathered(thirds(velocity_ref[...]), cells >> 5, cells & (CY - 1))
    load = lambda c, k: rows_at(turned_ref, c, k, BLOCK)
    move_points(load, store, BLOCK // SUB, node_getter(near), materials, tables_ref)
    emit_movers(fresh_ref[...].T, materials, lists_ref[0:3, :], far_message_ref, near_message_ref)
    kept, target = departures(cells, materials, lists_ref[0:3, :])
    kept_meta_ref[...] = kept
    target_ref[...] = target
    for a in range(4):
        for b in range(4):
            row = 2 * (4 * a + b)
            nodes_ref[row : row + 2, :] = near[a][b][1:3]
    nodes = product(thirds(nodes_ref[...]), chosen_ref[...].astype(BF16), NT)
    near_ref[...] = nodes[0:NEAR] + pltpu.roll(nodes[NEAR:], LANES // 2, 1)


def sums_kept(fresh_ref, target_ref, tables_ref, sums_ref, left_ref):
    depth, column, materials = (target_ref[0:1, :], target_ref[1:2, :], target_ref[2:3, :])
    load = lambda c, k: rows_at(fresh_ref, c, k, BLOCK)
    rho = by_material(materials, tables_ref, 0)
    terms = node_terms(load, BLOCK // SUB, rho, materials >= 0)
    spread_rows(terms, row_masks(depth), left_ref)
    sums_ref[...] = product(thirds(left_ref[...]), jnp.concatenate(column_onehot(column), axis=1), NT)


def packed_blocks(rows, wide_ref, turned_ref):
    count = rows.shape[0]
    fill = jnp.zeros((LANES - count, rows.shape[1]), F32)
    wide_ref[...] = jnp.concatenate([rows, fill], axis=0).T
    stride = BLOCK * count // LANES
    for c in range(8):
        total = wide_ref[c * BLOCK : c * BLOCK + stride, :]
        for group in range(1, LANES // count):
            start = c * BLOCK + group * stride
            total = total + pltpu.roll(wide_ref[start : start + stride, :], count * group, 1)
        turned_ref[c * stride : (c + 1) * stride, :] = total


def unpacked_blocks(turned_ref, count, wide_ref):
    stride = BLOCK * count // LANES
    for c in range(8):
        value = turned_ref[c * stride : (c + 1) * stride, :]
        for group in range(LANES // count):
            start = c * BLOCK + group * stride
            shift = (LANES - count * group) % LANES
            wide_ref[start : start + stride, :] = pltpu.roll(value, shift, 1) if shift else value
    return wide_ref[...].T[0:count]


def repeated(tile, count):
    while count < LANES:
        tile = tile + pltpu.roll(tile, count, 1)
        count *= 2
    return tile


def arrived_tags(from_inner, from_outer):
    low, high = by_side(from_inner, from_outer, parity("gx"))
    packed = repeated(low + pltpu.roll(high, MCAP, 1), 2 * MCAP)
    return packed.astype(jnp.int32) - (iota((SUB, LANES), 0) == 1).astype(jnp.int32)


def sums_two(
    kept_sums_ref, xo_ref, xi_ref, tables_ref,
    sums_ref, inner_ref, outer_ref, turned_ref, new_meta_ref,
    left_ref, wide_ref,
):
    new_meta = arrived_tags(xi_ref[MCAP:MSG, 0:LANES], xo_ref[MCAP:MSG, 0:LANES])
    new_meta_ref[...] = new_meta
    low, high = by_side(xi_ref[0:MCAP, :], xo_ref[0:MCAP, :], parity("gx"))
    packed_blocks(jnp.concatenate([low, high], axis=0), wide_ref, turned_ref)
    cells, materials = (new_meta[0:1], new_meta[1:2])
    stride = turned_ref.shape[0] // 8
    load = lambda c, k: rows_at(turned_ref, c, k, stride)
    rho = by_material(materials, tables_ref, 0)
    terms = node_terms(load, stride // SUB, rho, materials >= 0)
    spread_rows(terms, row_masks(cells >> 5), left_ref)
    onehots = column_onehot((cells & (CY - 1)) + CY)
    emit_sums(left_ref, onehots, kept_sums_ref, sums_ref, inner_ref, outer_ref)


def advance_two(
    kept_ref, meta_ref, lists_ref, slots_ref, tables_ref,
    fresh_ref, old_meta_ref, velocity_ref, far_message_ref, near_message_ref,
    packed_ref,
):
    velocity_two(slots_ref, packed_ref, velocity_ref)
    cells, materials = (meta_ref[0:1, :], meta_ref[1:2, :])

    def store(c, k, value):
        fresh_ref[c * BLOCK + k * SUB : c * BLOCK + (k + 1) * SUB, :] = value

    near = gathered(thirds(velocity_ref[...]), cells >> 5, (cells & (CY - 1)) + CY)
    load = lambda c, k: rows_at(kept_ref, c, k, BLOCK)
    move_points(load, store, BLOCK // SUB, node_getter(near), materials, tables_ref)
    emit_movers(fresh_ref[...].T, materials, lists_ref[3:6, :], far_message_ref, near_message_ref)
    kept, _ = departures(cells, materials, lists_ref[3:6, :])
    old_meta_ref[...] = kept


def settle(
    fresh_ref, old_meta_ref, velocity_ref, turned_ref, new_meta_ref, tables_ref, slots_ref, yo_ref, yi_ref,
    points_ref, tail_ref,
    old_ref, wide_ref, new_ref, cross_ref, middle_ref, out_ref, small_ref, last_ref, sems,
):
    alive = jnp.broadcast_to(old_meta_ref[1:2, :], fresh_ref.shape) >= 0
    old_ref[...] = jnp.where(alive, fresh_ref[...], 0.0).T
    old = LANES
    copies = [pltpu.make_async_copy(old_ref, points_ref.at[0:old], sems.at[0])]
    copies[0].start()
    parts = thirds(velocity_ref[...])

    stride = turned_ref.shape[0] // 8
    cells, materials = (new_meta_ref[0:1, :], new_meta_ref[1:2, :])

    def store_small(c, k, value):
        small_ref[c * stride + k * SUB : c * stride + (k + 1) * SUB, :] = value

    load = lambda c, k: rows_at(turned_ref, c, k, stride)
    near = gathered(parts, cells >> 5, (cells & (CY - 1)) + CY)
    move_points(load, store_small, stride // SUB, node_getter(near), materials, tables_ref)
    new_ref[...] = unpacked_blocks(small_ref, 2 * MCAP, wide_ref)
    copies.append(pltpu.make_async_copy(new_ref, points_ref.at[old : old + 2 * MCAP], sems.at[1]))
    copies[1].start()

    gy = lax.axis_index("gy")
    odd = parity("gy")
    low, high = by_side(yi_ref[...], yo_ref[...], odd)
    lane = iota((SUB, LANES), 1)
    tags = low[0:SUB, LANES : 2 * LANES] + pltpu.roll(high[0:SUB, LANES : 2 * LANES], 2 * MCAP, 1)
    tail = jnp.zeros((SUB, LANES), F32)
    for start, shift in ((32, 32), (48, 16), (96, 80), (112, 64)):
        tail = jnp.where((lane >= start) & (lane < start + MCAP), pltpu.roll(tags, shift, 1), tail)
    materials_row = (iota((SUB, LANES), 0) == 1).astype(jnp.int32)
    tail = tail.astype(jnp.int32) - materials_row
    tail_ref[...] = jnp.where(lane < 2 * MCAP, new_meta_ref[...], tail)
    tags = repeated(tags, 4 * MCAP).astype(jnp.int32) - materials_row

    last = slots_ref.shape[0] - 1
    below = slots_ref[jnp.maximum(gy - 1, 0), PACK:SLOT, :]
    above = slots_ref[jnp.minimum(gy + 1, last), PACK:SLOT, :]
    below = jnp.where(odd, below, pltpu.roll(below, LANES - 2 * MCAP, 1))
    above = jnp.where(odd, above, pltpu.roll(above, 2 * MCAP, 1))
    many = iota((NEAR, LANES), 1)
    nodes = jnp.where((many & (4 * MCAP - 1)) < 2 * MCAP, below, above)
    turned_nodes = pltpu.roll(nodes, LANES // 2, 1)
    halves = (jnp.where(many < LANES // 2, nodes, turned_nodes), jnp.where(many < LANES // 2, turned_nodes, nodes))

    def node_of(a, b, component):
        row = 2 * (4 * a + b) + component
        return halves[row // NEAR][row % NEAR : row % NEAR + 1]

    packed_blocks(jnp.concatenate([low[SUB:], high[SUB:]], axis=0), wide_ref, cross_ref)
    half = cross_ref.shape[0] // 8
    kinds = tags[1:2]

    def store_middle(c, k, value):
        middle_ref[c * half + k * SUB : c * half + (k + 1) * SUB, :] = value

    move_points(lambda c, k: rows_at(cross_ref, c, k, half), store_middle, half // SUB, node_of, kinds, tables_ref)
    row_lane = lane[0:1]
    second = (row_lane & MCAP) != 0
    cell = jnp.where(second, tags[2:3], tags[0:1])
    side = jnp.where((row_lane & (2 * MCAP)) != 0, 2 * CY, 0)
    near = gathered(parts, cell >> 5, (cell & (CY - 1)) + jnp.where(second, side, CY))

    def store_out(c, k, value):
        out_ref[c * half + k * SUB : c * half + (k + 1) * SUB, :] = value

    move_points(
        lambda c, k: rows_at(middle_ref, c, k, half), store_out, half // SUB, node_getter(near), kinds, tables_ref
    )
    last_ref[...] = unpacked_blocks(out_ref, 4 * MCAP, wide_ref)
    region = lambda index: points_ref.at[old + index * MCAP : old + (index + 1) * MCAP]
    for group, index in enumerate((2, 6, 3, 7)):
        source = last_ref.at[group * MCAP : (group + 1) * MCAP]
        copies.append(pltpu.make_async_copy(source, region(index), sems.at[2 + group]))
        copies[-1].start()
    for copy in copies:
        copy.wait()


def assemble(
    part_ref, old_meta_ref, tail_ref, xo_ref, xi_ref,
    points_ref, cells_ref, mats_ref,
    tags_ref, sems,
):
    del part_ref
    base = points_ref.shape[0] - 4 * MCAP
    odd = lax.axis_index("gx") & 1
    copies = []
    for index, (ref, region) in enumerate(((xo_ref, odd), (xi_ref, 1 - odd))):
        start = pl.multiple_of(base + region * MCAP, MCAP)
        copies.append(
            pltpu.make_async_copy(ref.at[0:MCAP, :], points_ref.at[pl.ds(start, MCAP), :], sems.at[index])
        )
        copies[-1].start()
    arrived = arrived_tags(xi_ref[MCAP:MSG, 0:LANES], xo_ref[MCAP:MSG, 0:LANES])
    lane = iota((1, LANES), 1)
    here = (lane >= 4 * MCAP) & (lane < 6 * MCAP)
    for row, ref in ((0, cells_ref), (1, mats_ref)):
        tags_ref[row, 0:1, :] = old_meta_ref[row : row + 1, :]
        tags_ref[row, 1:2, :] = jnp.where(here, arrived[row : row + 1], tail_ref[row : row + 1, :])
        copies.append(pltpu.make_async_copy(tags_ref.at[row], ref, sems.at[2 + row]))
        copies[-1].start()
    for copy in copies:
        copy.wait()


def shards(
    points,
    block_cell,
    block_mat,
    density,
    shear_modulus,
    lame_modulus,
    mig_slot_a,
    mig_dest_a,
    mig_cell_a,
    mig_slot_b,
    mig_dest_b,
    mig_cell_b,
):
    wide = 8 * BLOCK
    I32 = jnp.int32
    row = lambda value: value.reshape(1, -1)
    cells, mats = (row(block_cell), row(block_mat))
    list_a = (row(mig_slot_a), row(mig_dest_a), row(mig_cell_a))
    list_b = (row(mig_slot_b), row(mig_dest_b), row(mig_cell_b))

    halo = ((HALO, LANES), F32)
    tile = ((SUB, LANES), F32)
    tags = ((SUB, LANES), I32)
    grid = ((ROWS, LANES), F32)
    message = ((MSG, wide), F32)
    cross_message = ((CROSS_MSG, wide), F32)
    turned_form = ((wide, LANES), F32)
    half_form = ((wide // 2, LANES), F32)
    quarter_form = ((wide // 4, LANES), F32)
    near_form = ((NEAR, LANES), F32)
    slots_form = ((lax.axis_size("gy"), SLOT, LANES), F32)
    scratch = lambda form: pltpu.VMEM(*form)
    left = pltpu.VMEM((ROWS, 4 * LANES), F32)

    def along_depth(far, near):
        return (swap(far, "gx", 1), swap(near, "gx", 0))

    (lists,) = call(join_lists, (tags,), (), (IN_VMEM,) * 6, *list_a, *list_b)
    (turned,) = call(turn, (turned_form,), (), (IN_VMEM,), points)
    sums, inner, outer, tables, meta = call(
        sums_one,
        (grid, halo, halo, ((3 * NMAT, LANES), F32), tags),
        (left,),
        (IN_VMEM,) * 6,
        turned, cells, mats, row(density), row(shear_modulus), row(lame_modulus),
    )
    picked, picked_tags, chosen = call(
        pick_cross,
        (((4 * MCAP, wide), F32), tile, ((LANES, LANES), F32)),
        (),
        (IN_VMEM,) * 3,
        points, meta, lists,
    )
    merged, inner, outer = call(
        merge_one,
        (grid, cross_message, cross_message),
        (),
        (IN_VMEM,) * 5,
        sums, *along_depth(outer, inner), picked, picked_tags,
    )
    cross_far, cross_near = (swap(outer, "gy", 1), swap(inner, "gy", 0))
    fresh, kept_meta, target, near_nodes, far, near = call(
        advance_one,
        (turned_form, tags, tags, near_form, message, message),
        (scratch(grid), pltpu.VMEM((2 * NEAR, LANES), F32)),
        (IN_VMEM,) * 8,
        turned, meta, lists, merged, cross_far, cross_near, tables, chosen,
    )
    arrived = along_depth(far, near)
    (kept_sums,) = call(sums_kept, (grid,), (left,), (IN_VMEM,) * 3, fresh, target, tables)
    sums, inner, outer, turned, new_meta = call(
        sums_two,
        (grid, halo, halo, quarter_form, tags),
        (left, scratch(turned_form)),
        (IN_VMEM,) * 4,
        kept_sums, *arrived, tables,
    )
    (slots,) = call(
        merge_two,
        (slots_form,),
        (scratch(grid), pltpu.VMEM((SLOT, LANES), F32)),
        (IN_VMEM,) * 4,
        sums, *along_depth(outer, inner), near_nodes,
    )
    slots = lax.all_to_all(slots, "gy", 0, 0)
    fresh, old_meta, velocity, far, near = call(
        advance_two,
        (turned_form, tags, grid, message, message),
        (pltpu.VMEM((PACK + SUB, LANES), F32),),
        (IN_VMEM,) * 5,
        fresh, kept_meta, lists, slots, tables,
    )
    arrived = along_depth(far, near)
    final_form = ((2 * LANES, wide), F32)
    part, tail = call(
        settle,
        (final_form, tags),
        (
            pltpu.VMEM((LANES, wide), F32),
            scratch(turned_form),
            pltpu.VMEM((2 * MCAP, wide), F32),
            scratch(half_form),
            scratch(half_form),
            scratch(half_form),
            scratch(quarter_form),
            pltpu.VMEM((4 * MCAP, wide), F32),
            pltpu.SemaphoreType.DMA((6,)),
        ),
        (IN_VMEM,) * 9,
        fresh, old_meta, velocity, turned, new_meta, tables, slots, cross_far, cross_near,
        out_specs=(IN_HBM, IN_VMEM),
    )
    final_points, final_cells, final_mats = call(
        assemble,
        (final_form, ((2, LANES), I32), ((2, LANES), I32)),
        (pltpu.VMEM((2, 2, LANES), I32), pltpu.SemaphoreType.DMA((4,))),
        (IN_HBM,) + (IN_VMEM,) * 4,
        part, old_meta, tail, *arrived,
        out_specs=(IN_HBM,) * 3,
        aliases={0: 0},
    )
    return (final_points, final_cells.reshape(-1), final_mats.reshape(-1))


def solution(mesh):
    split = P(("gx", "gy"))
    rows = P(("gx", "gy"), None)
    return jax.shard_map(
        shards,
        mesh=mesh,
        in_specs=(rows, split, split, P(), P(), P()) + (split,) * 6,
        out_specs=(rows, split, split),
        check_vma=False,
    )
```

```python
import jax
import jax.numpy as jnp
from jax import lax
from jax.experimental import pallas as pl
from jax.experimental.pallas import tpu as pltpu
from jax.sharding import PartitionSpec as P

CX = 16
CY = 32
BLOCK = 64
NMAT = 8
MCAP = 16
LANES = 128
SUB = 8
ROWS = 160
HALO = 24
TOP = CX * SUB
PIECES = 8 * BLOCK // LANES
MSG = PIECES * MCAP + SUB
DEPTHS = CX + 3
PACK = 96
NEAR = 32
SHARE = 22
CROSS_MSG = 2 * SUB + PIECES * 2 * MCAP
SPAN = 3 * CY + 3

TIME_STEP = 0.2
MASS_FLOOR = 0.25
VOLUME = 1.0 / BLOCK
VMEM_LIMIT = 12 * 1024 * 1024

IN_VMEM = pl.BlockSpec(memory_space=pltpu.VMEM)
IN_HBM = pl.BlockSpec(memory_space=pltpu.HBM)
F32 = jnp.float32
BF16 = jnp.bfloat16
NN = (((1,), (0,)), ((), ()))
NT = (((1,), (1,)), ((), ()))


def call(kernel, outs, scratch, in_specs, *operands, out_specs=None, flops=1 << 22, bytes_accessed=1 << 19):
    return pl.pallas_call(
        kernel,
        out_shape=tuple(jax.ShapeDtypeStruct(shape, dtype) for shape, dtype in outs),
        in_specs=in_specs,
        out_specs=out_specs or tuple(IN_VMEM for _ in outs),
        scratch_shapes=scratch,
        compiler_params=pltpu.CompilerParams(vmem_limit_bytes=VMEM_LIMIT),
        cost_estimate=pl.CostEstimate(flops=flops, bytes_accessed=bytes_accessed, transcendentals=0),
    )(*operands)


def swap(value, axis, first):
    count = lax.axis_size(axis)
    pairs = []
    for low in range(first, count - 1, 2):
        pairs += [(low, low + 1), (low + 1, low)]
    return lax.ppermute(value, axis, pairs)


def iota(shape, dim):
    return lax.broadcasted_iota(jnp.int32, shape, dim)


def halves(value):
    high = value.astype(BF16)
    return (high, (value - high.astype(F32)).astype(BF16))


def product(parts, onehot, dims):
    rows = parts[0].shape[0]
    stacked = lax.dot_general(jnp.concatenate(parts, axis=0), onehot, dims, preferred_element_type=F32)
    total = stacked[0:rows]
    for index in range(1, len(parts)):
        total = total + stacked[index * rows : (index + 1) * rows]
    return total


def select_rows(onehot, rows):
    high, low = halves(rows)
    twice = jnp.concatenate([onehot, onehot], axis=1)
    return lax.dot_general(twice, jnp.concatenate([high, low], axis=0), NN, preferred_element_type=F32)


def stencil(u):
    p = jnp.maximum(0.25 - u, 0.0)
    q = jnp.maximum(u - 0.75, 0.0)
    p2 = p * p
    q2 = q * q
    weight = (p2, (1.0 - u) - 2.0 * p2 + q2, u + p2 - 2.0 * q2, q2)
    slope = (-2.0 * p, 4.0 * p + 2.0 * q - 1.0, 1.0 - 2.0 * p - 4.0 * q, 2.0 * q)
    return (weight, slope)


def by_material(materials, tables_ref, which):
    value = jnp.zeros(materials.shape, F32)
    for index in range(NMAT):
        row = which * NMAT + index
        value = jnp.where(materials == index, tables_ref[row : row + 1, :], value)
    return value


def column_onehot(column_of):
    first = jnp.broadcast_to(column_of, (LANES, LANES))
    column = iota((LANES, LANES), 0)
    return [(column == first + b).astype(F32).astype(BF16) for b in range(4)]


def row_masks(depth_of):
    depth = jnp.broadcast_to(depth_of, (SUB, LANES))
    return [depth == index for index in range(CX)]


def scaled(terms, materials, tables_ref):
    sub = iota((SUB, LANES), 0)
    wide = lambda row: jnp.broadcast_to(row, (SUB, LANES))
    scale = jnp.where(sub < 3, wide(by_material(materials, tables_ref, 0) * VOLUME), -VOLUME)
    scale = jnp.where((sub < 5) & (wide(materials) >= 0), scale, 0.0)
    return [[term * scale for term in row] for row in terms]


def node_terms(load, chunks):
    sub = iota((SUB, LANES), 0)
    stencils = [(stencil(load(0, k)), stencil(load(1, k))) for k in range(chunks)]
    terms = [[None] * 4 for _ in range(4)]
    for b in range(4):
        acc = [[None] * 5 for _ in range(4)]
        for k in range(chunks):
            (weight_x, slope_x), (weight_y, slope_y) = stencils[k]
            wy, dy = weight_y[b], slope_y[b]
            sxy = load(6, k)
            y1 = wy * load(2, k)
            y2 = wy * load(3, k)
            y3 = wy * load(4, k)
            y4 = wy * sxy
            y5 = dy * sxy
            y6 = dy * load(5, k)
            for a in range(4):
                wx, dx = weight_x[a], slope_x[a]
                new = (wx * wy, wx * y1, wx * y2, dx * y3 + wx * y5, dx * y4 + wx * y6)
                acc[a] = [n if o is None else o + n for o, n in zip(acc[a], new)]
        for a in range(4):
            packed = jnp.zeros((SUB, LANES), F32)
            for q in range(5):
                total = jnp.sum(acc[a][q], axis=0, keepdims=True)
                packed = jnp.where(sub == q, jnp.broadcast_to(total, (SUB, LANES)), packed)
            terms[a][b] = packed
    return terms


def spread_rows(terms, masks, left_ref):
    zero = jnp.zeros((SUB, LANES), F32)
    for b in range(4):
        for x in range(ROWS // SUB):
            total = zero
            for a in range(4):
                if 0 <= x - a < CX:
                    total = total + jnp.where(masks[x - a], terms[a][b], zero)
            left_ref[x * SUB : (x + 1) * SUB, b * LANES : (b + 1) * LANES] = total


def parity(axis):
    return (lax.axis_index(axis) & 1) == 1


def emit_sums(left_ref, onehots, more_ref, sums_ref, inner_ref, outer_ref):
    sums = product(halves(left_ref[...]), jnp.concatenate(onehots, axis=1), NT)
    if more_ref is not None:
        sums = sums + more_ref[...]
    sums_ref[...] = sums
    odd = parity("gx")
    bottom, top = (sums[0:HALO], sums[TOP : TOP + HALO])
    inner_ref[...] = jnp.where(odd, bottom, top)
    outer_ref[...] = jnp.where(odd, top, bottom)


def spread_table(table_ref, rows_ref, first):
    table = table_ref[...]
    for index in range(NMAT):
        row = first + index
        rows_ref[row : row + 1, :] = jnp.broadcast_to(table[:, index : index + 1], (1, LANES))


def terms_one(points_ref, turned_ref, terms_ref):
    turned_ref[...] = points_ref[...].T
    load = lambda c, k: rows_at(turned_ref, c, k, BLOCK)
    terms = node_terms(load, BLOCK // SUB)
    for a in range(4):
        for b in range(4):
            row = (4 * a + b) * SUB
            terms_ref[row : row + SUB, :] = terms[a][b]


def sums_one(
    terms_ref, cells_ref, mats_ref, density_ref,
    sums_ref, inner_ref, outer_ref, meta_ref,
    left_ref, density_rows_ref,
):
    spread_table(density_ref, density_rows_ref, 0)
    cells, materials = (cells_ref[...], mats_ref[...])
    meta_ref[0:1, :] = cells
    meta_ref[1:2, :] = materials
    terms = [[terms_ref[(4 * a + b) * SUB : (4 * a + b + 1) * SUB, :] for b in range(4)] for a in range(4)]
    terms = scaled(terms, materials, density_rows_ref)
    spread_rows(terms, row_masks(cells >> 5), left_ref)
    emit_sums(left_ref, column_onehot(cells & (CY - 1)), None, sums_ref, inner_ref, outer_ref)


def join_lists(*refs):
    *list_refs, density_ref, shear_ref, lame_ref, lists_ref, tables_ref = refs
    for which, table_ref in enumerate((density_ref, shear_ref, lame_ref)):
        spread_table(table_ref, tables_ref, which * NMAT)
    for index, ref in enumerate(list_refs):
        row = ref[...]
        rest = jnp.full((1, LANES - row.shape[1]), -1, jnp.int32)
        lists_ref[index : index + 1, :] = jnp.concatenate([row, rest], axis=1)


def by_side(inner, outer, odd):
    return (jnp.where(odd, inner, outer), jnp.where(odd, outer, inner))


def put_pieces(ref, first, rows):
    count = rows.shape[0]
    for piece in range(PIECES):
        start = first + piece * count
        ref[start : start + count, :] = rows[:, piece * LANES : (piece + 1) * LANES]


def joined(pieces):
    count = pieces.shape[0] // PIECES
    return jnp.concatenate([pieces[piece * count : (piece + 1) * count] for piece in range(PIECES)], axis=1)


def matches(dests, targets):
    dest = jnp.broadcast_to(dests, (2 * SUB, LANES))
    sub = iota(dest.shape, 0)
    matched = jnp.zeros(dest.shape, F32)
    for o, target in enumerate(targets):
        matched = jnp.where((sub == o) & (dest == target), 1.0, matched)
    square = (LANES, LANES)
    earlier = (iota(square, 0) < iota(square, 1)).astype(F32).astype(BF16)
    rank = lax.dot_general(matched.astype(BF16), earlier, NN, preferred_element_type=F32)
    return (matched, rank)


def placing_rows(matched, rank, groups):
    blank = jnp.zeros((MCAP, LANES), F32)
    place = iota((MCAP, LANES), 0).astype(F32)
    rows = []
    for o in groups:
        if o is None:
            rows.append(blank)
            continue
        hit = jnp.broadcast_to(rank[o : o + 1], blank.shape) == place
        rows.append(jnp.where(hit, jnp.broadcast_to(matched[o : o + 1], blank.shape), 0.0))
    rows += [blank] * (LANES // MCAP - len(groups))
    return jnp.concatenate(rows, axis=0).astype(BF16)


def holding(slots):
    square = (LANES, LANES)
    return (iota(square, 0) == jnp.broadcast_to(slots, square)).astype(F32).astype(BF16)


def small_rows(*rows):
    sub = iota((2 * SUB, LANES), 0)
    value = jnp.zeros((2 * SUB, LANES), F32)
    for index, row in enumerate(rows):
        value = jnp.where(sub == index, jnp.broadcast_to(row.astype(F32), value.shape), value)
    return value.astype(BF16)


def turned_to(small, onehot):
    return lax.dot_general(small, onehot, NT, preferred_element_type=F32)


def tag_tile(*rows):
    sub = iota((SUB, LANES), 0)
    tile = jnp.zeros((SUB, LANES), F32)
    for index, row in enumerate(rows):
        tile = jnp.where(sub == index, jnp.broadcast_to(row, tile.shape), tile)
    return tile


def home_and_steps():
    across = lax.axis_size("gy")
    gx, gy = (lax.axis_index("gx"), lax.axis_index("gy"))
    return (gx * across + gy, across - 2 * across * (gx & 1), 1 - 2 * (gy & 1))


def pick_cross(points_ref, meta_ref, lists_ref, rows_ref, tags_ref, chosen_ref):
    home, _, step_y = home_and_steps()
    chosen = places = None
    for first, groups in ((0, (0, None, 1, None)), (3, (None, 0, None, 1))):
        matched, rank = matches(lists_ref[first + 1 : first + 2, :], (home + step_y, home - step_y))
        placing = placing_rows(matched, rank, groups)
        part = turned_to(placing, holding(lists_ref[first : first + 1, :]))
        cell = lists_ref[first + 2 : first + 3, :]
        place = turned_to(small_rows(cell >> 5, cell & (CY - 1)), placing)
        chosen = part if chosen is None else chosen + part
        places = place if places is None else places + place
    chosen_ref[...] = chosen
    onehot = chosen.astype(BF16)
    cells, materials = (meta_ref[0:1, :], meta_ref[1:2, :])
    found = turned_to(small_rows(materials + 1, cells >> 5, cells & (CY - 1)), onehot)
    tags_ref[...] = tag_tile(
        places[0:1] * float(CY) + places[1:2], found[0:1], found[1:2] * float(CY) + found[2:3]
    )
    rows_ref[...] = select_rows(onehot[0 : 4 * MCAP], points_ref[...])


def merge_rows(sums_ref, from_outer_ref, from_inner_ref, merged_ref):
    from_low, from_high = by_side(from_inner_ref[...], from_outer_ref[...], parity("gx"))
    merged_ref[...] = sums_ref[...]
    merged_ref[0:HALO] = sums_ref[0:HALO] + from_low
    merged_ref[TOP : TOP + HALO] = sums_ref[TOP : TOP + HALO] + from_high


def merge_one(
    sums_ref, from_outer_ref, from_inner_ref, rows_ref, tags_ref,
    merged_ref, inner_ref, outer_ref,
):
    merge_rows(sums_ref, from_outer_ref, from_inner_ref, merged_ref)
    lane = iota((SUB, LANES), 1)
    low = jnp.zeros((SUB, LANES), F32)
    high = jnp.zeros((SUB, LANES), F32)
    for x in range(DEPTHS):
        row = merged_ref[x * SUB : (x + 1) * SUB, :]
        here = (lane >= 3 * x) & (lane < 3 * x + 3)
        shift = 3 * x
        low = jnp.where(here, pltpu.roll(row, shift, 1) if shift else row, low)
        high = jnp.where(here, pltpu.roll(row, (shift - CY) % LANES, 1), high)
    to_inner, to_outer = by_side(low, high, parity("gy"))
    movers = 2 * MCAP
    tags = tags_ref[...]
    for ref, halo, tag, first in (
        (inner_ref, to_inner, tags, 0),
        (outer_ref, to_outer, pltpu.roll(tags, LANES - movers, 1), movers),
    ):
        ref[0:SUB, :] = halo
        ref[SUB : 2 * SUB, :] = jnp.where(lane < movers, tag, 0.0)
        put_pieces(ref, 2 * SUB, rows_ref[first : first + movers, :])


def merge_two(sums_ref, from_outer_ref, from_inner_ref, near_ref, slots_ref, merged_ref, slot_ref):
    merge_rows(sums_ref, from_outer_ref, from_inner_ref, merged_ref)
    slot_ref[PACK - SUB : PACK, :] = jnp.zeros((SUB, LANES), F32)
    for x in range(DEPTHS):
        slot_ref[5 * x : 5 * x + 5, :] = merged_ref[x * SUB : x * SUB + 5, :]
    lane = iota((NEAR, LANES), 1)
    near = near_ref[...]
    for third in range(PACK // NEAR):
        start = third * NEAR
        moved = pltpu.roll(near, SPAN - SHARE * third, 1)
        here = (lane >= SPAN) & (lane < SPAN + SHARE)
        slot_ref[start : start + NEAR, :] = jnp.where(here, moved, slot_ref[start : start + NEAR, :])
    value = slot_ref[...]
    for index in range(slots_ref.shape[0]):
        slots_ref[index] = value


def put_velocity(row, x, node_y, velocity_ref):
    node_x = lax.axis_index("gx") * CX - 1 + x
    inside_x = (node_x > 0) & (node_x < CX * lax.axis_size("gx") - 1)
    inside_y = (node_y > 0) & (node_y < CY * lax.axis_size("gy") - 1)
    mass = jnp.maximum(jnp.broadcast_to(row[0:1], (SUB, LANES)), MASS_FLOOR)
    value = (row + TIME_STEP * pltpu.roll(row, SUB - 2, 0)) / mass
    velocity_ref[x * SUB : (x + 1) * SUB, :] = jnp.where(inside_y & inside_x, value, 0.0)


def velocity_one(merged_ref, from_inner, from_outer, velocity_ref):
    low, high = by_side(from_inner, from_outer, parity("gy"))
    lane = iota((SUB, LANES), 1)
    node_y = lax.axis_index("gy") * CY - 1 + lane
    for x in range(DEPTHS):
        row = merged_ref[x * SUB : (x + 1) * SUB, :]
        shift = 3 * x
        row = row + jnp.where(lane < 3, pltpu.roll(low, LANES - shift, 1) if shift else low, 0.0)
        row = row + jnp.where(
            (lane >= CY) & (lane < CY + 3), pltpu.roll(high, (CY - shift) % LANES, 1), 0.0
        )
        put_velocity(row, x, node_y, velocity_ref)
    velocity_ref[DEPTHS * SUB :, :] = jnp.zeros((ROWS - DEPTHS * SUB, LANES), F32)


def velocity_two(slots_ref, packed_ref, velocity_ref):
    gy = lax.axis_index("gy")
    lane = iota((PACK, LANES), 1)
    total = jnp.zeros((PACK, LANES), F32)
    for index in range(slots_ref.shape[0]):
        shift = CY * (index - gy)
        moved = pltpu.roll(slots_ref[index, 0:PACK, :], shift & (LANES - 1), 1)
        valid = (lane >= shift) & (lane < SPAN + shift) & (lane < SPAN)
        total = total + jnp.where(valid, moved, 0.0)
    packed_ref[0:PACK, :] = total
    packed_ref[PACK:, :] = jnp.zeros((packed_ref.shape[0] - PACK, LANES), F32)
    node_y = (gy - 1) * CY - 1 + iota((SUB, LANES), 1)
    for x in range(DEPTHS):
        put_velocity(packed_ref[5 * x : 5 * x + SUB, :], x, node_y, velocity_ref)
    velocity_ref[DEPTHS * SUB :, :] = jnp.zeros((ROWS - DEPTHS * SUB, LANES), F32)


def gathered(velocity_parts, depth_of, column_of):
    masks = row_masks(depth_of)
    near = [[None] * 4 for _ in range(4)]
    columns = product(velocity_parts, jnp.concatenate(column_onehot(column_of), axis=1), NN)
    for b in range(4):
        column = columns[:, b * LANES : (b + 1) * LANES]
        for a in range(4):
            total = jnp.zeros((SUB, LANES), F32)
            for x in range(CX):
                total = jnp.where(masks[x], column[(x + a) * SUB : (x + a + 1) * SUB], total)
            near[a][b] = total
    return near


def move_points(load, store, chunks, node_of, materials, tables_ref):
    wide = lambda row: jnp.broadcast_to(row, (SUB, LANES))
    twice_shear = wide(2.0 * by_material(materials, tables_ref, 1))
    lame = wide(by_material(materials, tables_ref, 2))
    alive = wide(materials) >= 0
    for k in range(chunks):
        u, v = (load(0, k), load(1, k))
        weight_x, slope_x = stencil(u)
        weight_y, slope_y = stencil(v)
        speed, along, across = ([], [], [])
        for component in range(2):
            value = rate_x = rate_y = None
            for a in range(4):
                inner = slant = None
                for b in range(4):
                    node = wide(node_of(a, b, component))
                    term, tilt = (weight_y[b] * node, slope_y[b] * node)
                    inner = term if b == 0 else inner + term
                    slant = tilt if b == 0 else slant + tilt
                add = (weight_x[a] * inner, slope_x[a] * inner, weight_x[a] * slant)
                if a == 0:
                    value, rate_x, rate_y = add
                else:
                    value, rate_x, rate_y = (value + add[0], rate_x + add[1], rate_y + add[2])
            speed.append(value)
            along.append(rate_x)
            across.append(rate_y)
        rate_xx, rate_yy = (along[0], across[1])
        rate_xy = 0.5 * (across[0] + along[1])
        spherical = lame * (rate_xx + rate_yy)
        stress_xx = load(4, k) + TIME_STEP * (twice_shear * rate_xx + spherical)
        stress_yy = load(5, k) + TIME_STEP * (twice_shear * rate_yy + spherical)
        stress_xy = load(6, k) + TIME_STEP * twice_shear * rate_xy
        fresh = (
            jnp.clip(u + TIME_STEP * speed[0], 0.0, 1.0),
            jnp.clip(v + TIME_STEP * speed[1], 0.0, 1.0),
            speed[0],
            speed[1],
            stress_xx,
            stress_yy,
            stress_xy,
            jnp.maximum(load(7, k), -0.5 * (stress_xx + stress_yy)),
        )
        for c in range(8):
            store(c, k, jnp.where(alive, fresh[c], 0.0))


def node_getter(near):
    return lambda a, b, component: near[a][b][component + 1 : component + 2]


def emit_movers(fresh, chosen_ref, tags_ref, far_ref, near_ref):
    rows = select_rows(chosen_ref[...].astype(BF16), fresh.T)
    tags = tags_ref[...]
    lane = iota((SUB, LANES), 1)
    for o, ref in enumerate((far_ref, near_ref)):
        put_pieces(ref, 0, rows[o * MCAP : (o + 1) * MCAP])
        tag = pltpu.roll(tags, LANES - o * MCAP, 1) if o else tags
        ref[MSG - SUB : MSG, :] = jnp.where(lane < MCAP, tag, 0.0)


def departures(cells, materials, lists):
    home, _, _ = home_and_steps()
    slots, dests, cell = (lists[0:1], lists[1:2], lists[2:3])
    moving = (dests >= 0) & (dests != home)
    low, high = (dests == home - 1, dests == home + 1)
    cross = jnp.where(low | high, 1, 0)
    column = (cell & (CY - 1)) + jnp.where(high, 2 * CY, 0)
    entries = small_rows(jnp.where(moving, 1, 0), cross, cross * (cell >> 5), cross * column)
    found = turned_to(entries, holding(slots)).astype(jnp.int32)
    gone, across = (found[0:1] > 0, found[1:2] > 0)
    sub = iota((SUB, LANES), 0)
    wide = lambda value: jnp.broadcast_to(value, (SUB, LANES))
    kept = jnp.where(
        sub == 0,
        wide(jnp.where(gone, 0, cells)),
        wide(jnp.where(gone, -1, materials)),
    )
    target = jnp.where(
        sub == 0,
        wide(jnp.where(across, found[2:3], cells >> 5)),
        jnp.where(
            sub == 1,
            wide(jnp.where(across, found[3:4], (cells & (CY - 1)) + CY)),
            wide(jnp.where(gone & ~across, -1, materials)),
        ),
    )
    return (kept, target)


def plan_depth(
    meta_ref, lists_ref,
    chosen_a_ref, chosen_b_ref, tags_a_ref, tags_b_ref, kept_a_ref, kept_b_ref, target_ref,
):
    home, step_x, _ = home_and_steps()
    cells, materials = (meta_ref[0:1, :], meta_ref[1:2, :])
    for first, chosen_ref, tags_ref in ((0, chosen_a_ref, tags_a_ref), (3, chosen_b_ref, tags_b_ref)):
        matched, rank = matches(lists_ref[first + 1 : first + 2, :], (home - step_x, home + step_x))
        placing = placing_rows(matched, rank, (0, 1))
        chosen = turned_to(placing, holding(lists_ref[first : first + 1, :]))
        chosen_ref[...] = chosen[0 : 2 * MCAP]
        cell = lists_ref[first + 2 : first + 3, :]
        places = turned_to(small_rows(cell >> 5, cell & (CY - 1)), placing)
        kinds = turned_to(small_rows(materials + 1), chosen.astype(BF16))
        tags_ref[...] = tag_tile(places[0:1] * float(CY) + places[1:2], kinds[0:1])
    kept, target = departures(cells, materials, lists_ref[0:3, :])
    kept_a_ref[...] = kept
    target_ref[...] = target
    kept, _ = departures(kept[0:1], kept[1:2], lists_ref[3:6, :])
    kept_b_ref[...] = kept


def rows_at(ref, c, k, stride):
    return ref[c * stride + k * SUB : c * stride + (k + 1) * SUB, :]


def advance_one(
    turned_ref, meta_ref, merged_ref, yo_ref, yi_ref, tables_ref, chosen_ref, tags_ref,
    fresh_ref, nodes_ref, far_message_ref, near_message_ref,
    velocity_ref,
):
    velocity_one(merged_ref, yi_ref[0:SUB, :], yo_ref[0:SUB, :], velocity_ref)
    cells, materials = (meta_ref[0:1, :], meta_ref[1:2, :])

    def store(c, k, value):
        fresh_ref[c * BLOCK + k * SUB : c * BLOCK + (k + 1) * SUB, :] = value

    near = gathered(halves(velocity_ref[...]), cells >> 5, cells & (CY - 1))
    load = lambda c, k: rows_at(turned_ref, c, k, BLOCK)
    move_points(load, store, BLOCK // SUB, node_getter(near), materials, tables_ref)
    emit_movers(fresh_ref[...], chosen_ref, tags_ref, far_message_ref, near_message_ref)
    for a in range(4):
        for b in range(4):
            row = 2 * (4 * a + b)
            nodes_ref[row : row + 2, :] = near[a][b][1:3]


def sums_kept(fresh_ref, target_ref, tables_ref, nodes_ref, chosen_ref, sums_ref, near_ref, left_ref):
    depth, column, materials = (target_ref[0:1, :], target_ref[1:2, :], target_ref[2:3, :])
    load = lambda c, k: rows_at(fresh_ref, c, k, BLOCK)
    terms = scaled(node_terms(load, BLOCK // SUB), materials, tables_ref)
    spread_rows(terms, row_masks(depth), left_ref)
    sums_ref[...] = product(halves(left_ref[...]), jnp.concatenate(column_onehot(column), axis=1), NT)
    near_ref[...] = product(halves(nodes_ref[...]), chosen_ref[...].astype(BF16), NT)


def packed_blocks(rows, wide_ref, turned_ref):
    count = rows.shape[0]
    fill = jnp.zeros((LANES - count, rows.shape[1]), F32)
    wide_ref[...] = jnp.concatenate([rows, fill], axis=0).T
    stride = BLOCK * count // LANES
    for c in range(8):
        total = wide_ref[c * BLOCK : c * BLOCK + stride, :]
        for group in range(1, LANES // count):
            start = c * BLOCK + group * stride
            total = total + pltpu.roll(wide_ref[start : start + stride, :], count * group, 1)
        turned_ref[c * stride : (c + 1) * stride, :] = total


def unpacked_blocks(turned_ref, count, wide_ref):
    stride = BLOCK * count // LANES
    for c in range(8):
        value = turned_ref[c * stride : (c + 1) * stride, :]
        for group in range(LANES // count):
            start = c * BLOCK + group * stride
            shift = (LANES - count * group) % LANES
            wide_ref[start : start + stride, :] = pltpu.roll(value, shift, 1) if shift else value
    return wide_ref[...].T[0:count]


def repeated(tile, count):
    while count < LANES:
        tile = tile + pltpu.roll(tile, count, 1)
        count *= 2
    return tile


def arrived_tags(from_inner, from_outer):
    low, high = by_side(from_inner, from_outer, parity("gx"))
    packed = repeated(low + pltpu.roll(high, MCAP, 1), 2 * MCAP)
    return packed.astype(jnp.int32) - (iota((SUB, LANES), 0) == 1).astype(jnp.int32)


def sums_two(
    kept_sums_ref, xo_ref, xi_ref, tables_ref,
    sums_ref, inner_ref, outer_ref, turned_ref, new_meta_ref,
    left_ref, wide_ref,
):
    new_meta = arrived_tags(xi_ref[MSG - SUB : MSG, :], xo_ref[MSG - SUB : MSG, :])
    new_meta_ref[...] = new_meta
    low, high = by_side(xi_ref[0 : MSG - SUB, :], xo_ref[0 : MSG - SUB, :], parity("gx"))
    packed_blocks(jnp.concatenate([joined(low), joined(high)], axis=0), wide_ref, turned_ref)
    cells, materials = (new_meta[0:1], new_meta[1:2])
    stride = turned_ref.shape[0] // 8
    load = lambda c, k: rows_at(turned_ref, c, k, stride)
    terms = scaled(node_terms(load, stride // SUB), materials, tables_ref)
    spread_rows(terms, row_masks(cells >> 5), left_ref)
    onehots = column_onehot((cells & (CY - 1)) + CY)
    emit_sums(left_ref, onehots, kept_sums_ref, sums_ref, inner_ref, outer_ref)


def advance_two(
    kept_ref, meta_ref, slots_ref, tables_ref, chosen_ref, tags_ref,
    fresh_ref, velocity_ref, far_message_ref, near_message_ref,
    packed_ref,
):
    velocity_two(slots_ref, packed_ref, velocity_ref)
    cells, materials = (meta_ref[0:1, :], meta_ref[1:2, :])

    def store(c, k, value):
        fresh_ref[c * BLOCK + k * SUB : c * BLOCK + (k + 1) * SUB, :] = value

    near = gathered(halves(velocity_ref[...]), cells >> 5, (cells & (CY - 1)) + CY)
    load = lambda c, k: rows_at(kept_ref, c, k, BLOCK)
    move_points(load, store, BLOCK // SUB, node_getter(near), materials, tables_ref)
    emit_movers(fresh_ref[...], chosen_ref, tags_ref, far_message_ref, near_message_ref)


def near_movers(slots_ref, index):
    lane = iota((NEAR, LANES), 1)
    nodes = jnp.zeros((NEAR, LANES), F32)
    for third in range(PACK // NEAR):
        first = SHARE * third
        part = slots_ref[index, third * NEAR : (third + 1) * NEAR, :]
        part = pltpu.roll(part, LANES - SPAN + first, 1)
        nodes = jnp.where((lane >= first) & (lane < first + SHARE), part, nodes)
    return nodes


def settle(
    fresh_ref, old_meta_ref, velocity_ref, turned_ref, new_meta_ref, tables_ref, slots_ref, yo_ref, yi_ref,
    rows_ref, tail_ref,
    wide_ref, cross_ref, middle_ref, out_ref, small_ref,
):
    alive = jnp.broadcast_to(old_meta_ref[1:2, :], fresh_ref.shape) >= 0
    rows_ref[0:LANES, :] = jnp.where(alive, fresh_ref[...], 0.0).T
    parts = halves(velocity_ref[...])

    stride = turned_ref.shape[0] // 8
    cells, materials = (new_meta_ref[0:1, :], new_meta_ref[1:2, :])

    def store_small(c, k, value):
        small_ref[c * stride + k * SUB : c * stride + (k + 1) * SUB, :] = value

    load = lambda c, k: rows_at(turned_ref, c, k, stride)
    near = gathered(parts, cells >> 5, (cells & (CY - 1)) + CY)
    move_points(load, store_small, stride // SUB, node_getter(near), materials, tables_ref)
    rows_ref[LANES : LANES + 2 * MCAP, :] = unpacked_blocks(small_ref, 2 * MCAP, wide_ref)

    gy = lax.axis_index("gy")
    odd = parity("gy")
    low, high = by_side(yi_ref[...], yo_ref[...], odd)
    lane = iota((SUB, LANES), 1)
    tags = low[SUB : 2 * SUB] + pltpu.roll(high[SUB : 2 * SUB], 2 * MCAP, 1)
    tail = jnp.zeros((SUB, LANES), F32)
    for start, shift in ((32, 32), (48, 16), (96, 80), (112, 64)):
        tail = jnp.where((lane >= start) & (lane < start + MCAP), pltpu.roll(tags, shift, 1), tail)
    materials_row = (iota((SUB, LANES), 0) == 1).astype(jnp.int32)
    tail = tail.astype(jnp.int32) - materials_row
    tail_ref[...] = jnp.where(lane < 2 * MCAP, new_meta_ref[...], tail)
    tags = repeated(tags, 4 * MCAP).astype(jnp.int32) - materials_row

    last = slots_ref.shape[0] - 1
    below = near_movers(slots_ref, jnp.maximum(gy - 1, 0))
    above = near_movers(slots_ref, jnp.minimum(gy + 1, last))
    below = jnp.where(odd, below, pltpu.roll(below, LANES - 2 * MCAP, 1))
    above = jnp.where(odd, above, pltpu.roll(above, 2 * MCAP, 1))
    many = iota((NEAR, LANES), 1)
    nodes = jnp.where(many < 2 * MCAP, below, jnp.where(many < 4 * MCAP, above, 0.0))
    nodes = nodes + pltpu.roll(nodes, 4 * MCAP, 1)

    def node_of(a, b, component):
        row = 2 * (4 * a + b) + component
        return nodes[row : row + 1]

    rows = jnp.concatenate([joined(low[2 * SUB :]), joined(high[2 * SUB :])], axis=0)
    packed_blocks(rows, wide_ref, cross_ref)
    half = cross_ref.shape[0] // 8
    kinds = tags[1:2]

    def store_middle(c, k, value):
        middle_ref[c * half + k * SUB : c * half + (k + 1) * SUB, :] = value

    move_points(lambda c, k: rows_at(cross_ref, c, k, half), store_middle, half // SUB, node_of, kinds, tables_ref)
    row_lane = lane[0:1]
    second = (row_lane & MCAP) != 0
    cell = jnp.where(second, tags[2:3], tags[0:1])
    side = jnp.where((row_lane & (2 * MCAP)) != 0, 2 * CY, 0)
    near = gathered(parts, cell >> 5, (cell & (CY - 1)) + jnp.where(second, side, CY))

    def store_out(c, k, value):
        out_ref[c * half + k * SUB : c * half + (k + 1) * SUB, :] = value

    move_points(
        lambda c, k: rows_at(middle_ref, c, k, half), store_out, half // SUB, node_getter(near), kinds, tables_ref
    )
    last = unpacked_blocks(out_ref, 4 * MCAP, wide_ref)
    for group, index in enumerate((2, 6, 3, 7)):
        start = LANES + index * MCAP
        rows_ref[start : start + MCAP, :] = last[group * MCAP : (group + 1) * MCAP]


def assemble(
    part_ref, old_meta_ref, tail_ref, xo_ref, xi_ref,
    points_ref, cells_ref, mats_ref,
    tags_ref, rows_ref, sems,
):
    base = points_ref.shape[0] - 4 * MCAP
    odd = lax.axis_index("gx") & 1
    copies = []
    for index, (first, last) in enumerate(((0, base), (base + 2 * MCAP, base + 4 * MCAP))):
        copies.append(pltpu.make_async_copy(part_ref.at[first:last], points_ref.at[first:last], sems.at[index]))
        copies[-1].start()
    for index, (ref, region) in enumerate(((xo_ref, odd), (xi_ref, 1 - odd))):
        start = pl.multiple_of(base + region * MCAP, MCAP)
        rows_ref[index] = joined(ref[0 : MSG - SUB, :])
        copies.append(
            pltpu.make_async_copy(rows_ref.at[index], points_ref.at[pl.ds(start, MCAP), :], sems.at[2 + index])
        )
        copies[-1].start()
    arrived = arrived_tags(xi_ref[MSG - SUB : MSG, :], xo_ref[MSG - SUB : MSG, :])
    lane = iota((1, LANES), 1)
    here = (lane >= 4 * MCAP) & (lane < 6 * MCAP)
    for row, ref in ((0, cells_ref), (1, mats_ref)):
        tags_ref[row, 0:1, :] = old_meta_ref[row : row + 1, :]
        tags_ref[row, 1:2, :] = jnp.where(here, arrived[row : row + 1], tail_ref[row : row + 1, :])
        copies.append(pltpu.make_async_copy(tags_ref.at[row], ref, sems.at[4 + row]))
        copies[-1].start()
    for copy in copies:
        copy.wait()


def shards(
    points,
    block_cell,
    block_mat,
    density,
    shear_modulus,
    lame_modulus,
    mig_slot_a,
    mig_dest_a,
    mig_cell_a,
    mig_slot_b,
    mig_dest_b,
    mig_cell_b,
):
    wide = 8 * BLOCK
    I32 = jnp.int32
    row = lambda value: value.reshape(1, -1)
    cells, mats = (row(block_cell), row(block_mat))
    list_a = (row(mig_slot_a), row(mig_dest_a), row(mig_cell_a))
    list_b = (row(mig_slot_b), row(mig_dest_b), row(mig_cell_b))

    halo = ((HALO, LANES), F32)
    tile = ((SUB, LANES), F32)
    tags = ((SUB, LANES), I32)
    grid = ((ROWS, LANES), F32)
    message = ((MSG, LANES), F32)
    cross_message = ((CROSS_MSG, LANES), F32)
    turned_form = ((wide, LANES), F32)
    half_form = ((wide // 2, LANES), F32)
    quarter_form = ((wide // 4, LANES), F32)
    near_form = ((NEAR, LANES), F32)
    slots_form = ((lax.axis_size("gy"), PACK, LANES), F32)
    scratch = lambda form: pltpu.VMEM(*form)
    left = pltpu.VMEM((ROWS, 4 * LANES), F32)

    def along_depth(far, near):
        return (swap(far, "gx", 1), swap(near, "gx", 0))

    small = (row(density), row(shear_modulus), row(lame_modulus))
    lists, tables = call(
        join_lists, (tags, ((3 * NMAT, LANES), F32)), (), (IN_VMEM,) * 9, *list_a, *list_b, *small
    )
    turned, terms = call(
        terms_one, (turned_form, ((16 * SUB, LANES), F32)), (), (IN_VMEM,), points
    )
    sums, inner, outer, meta = call(
        sums_one,
        (grid, halo, halo, tags),
        (left, pltpu.VMEM((NMAT, LANES), F32)),
        (IN_VMEM,) * 4,
        terms, cells, mats, small[0],
    )
    picked, picked_tags, chosen = call(
        pick_cross,
        (((4 * MCAP, wide), F32), tile, ((LANES, LANES), F32)),
        (),
        (IN_VMEM,) * 3,
        points, meta, lists,
    )
    merged, inner, outer = call(
        merge_one,
        (grid, cross_message, cross_message),
        (),
        (IN_VMEM,) * 5,
        sums, *along_depth(outer, inner), picked, picked_tags,
    )
    cross_far, cross_near = (swap(outer, "gy", 1), swap(inner, "gy", 0))
    chosen_form = ((2 * MCAP, LANES), F32)
    chosen_a, chosen_b, tags_a, tags_b, kept_a, kept_b, target = call(
        plan_depth,
        (chosen_form, chosen_form, tile, tile, tags, tags, tags),
        (),
        (IN_VMEM,) * 2,
        meta, lists,
    )
    fresh, nodes, far, near = call(
        advance_one,
        (turned_form, near_form, message, message),
        (scratch(grid),),
        (IN_VMEM,) * 8,
        turned, meta, merged, cross_far, cross_near, tables, chosen_a, tags_a,
    )
    arrived = along_depth(far, near)
    kept_sums, near_nodes = call(
        sums_kept, (grid, near_form), (left,), (IN_VMEM,) * 5, fresh, target, tables, nodes, chosen
    )
    sums, inner, outer, turned, new_meta = call(
        sums_two,
        (grid, halo, halo, quarter_form, tags),
        (left, scratch(turned_form)),
        (IN_VMEM,) * 4,
        kept_sums, *arrived, tables,
    )
    (slots,) = call(
        merge_two,
        (slots_form,),
        (scratch(grid), pltpu.VMEM((PACK, LANES), F32)),
        (IN_VMEM,) * 4,
        sums, *along_depth(outer, inner), near_nodes,
    )
    slots = lax.all_to_all(slots, "gy", 0, 0)
    fresh, velocity, far, near = call(
        advance_two,
        (turned_form, grid, message, message),
        (pltpu.VMEM((PACK + SUB, LANES), F32),),
        (IN_VMEM,) * 6,
        fresh, kept_a, slots, tables, chosen_b, tags_b,
    )
    arrived = along_depth(far, near)
    final_form = ((2 * LANES, wide), F32)
    part, tail = call(
        settle,
        (final_form, tags),
        (
            scratch(turned_form),
            scratch(half_form),
            scratch(half_form),
            scratch(half_form),
            scratch(quarter_form),
        ),
        (IN_VMEM,) * 9,
        fresh, kept_b, velocity, turned, new_meta, tables, slots, cross_far, cross_near,
    )
    final_points, final_cells, final_mats = call(
        assemble,
        (final_form, ((2, LANES), I32), ((2, LANES), I32)),
        (pltpu.VMEM((2, 2, LANES), I32), pltpu.VMEM((2, MCAP, wide), F32), pltpu.SemaphoreType.DMA((6,))),
        (IN_VMEM,) * 5,
        part, kept_b, tail, *arrived,
        out_specs=(IN_HBM,) * 3,
    )
    return (final_points, final_cells.reshape(-1), final_mats.reshape(-1))


def solution(mesh):
    split = P(("gx", "gy"))
    rows = P(("gx", "gy"), None)
    return jax.shard_map(
        shards,
        mesh=mesh,
        in_specs=(rows, split, split, P(), P(), P()) + (split,) * 6,
        out_specs=(rows, split, split),
        check_vma=False,
    )
```

```python
import jax
import jax.numpy as jnp
from jax import lax
from jax.experimental import pallas as pl
from jax.experimental.pallas import tpu as pltpu
from jax.sharding import PartitionSpec as P

CX = 16
CY = 32
BLOCK = 64
NMAT = 8
MCAP = 16
LANES = 128
SUB = 8
ROWS = 160
HALO = 24
TOP = CX * SUB
PIECES = 8 * BLOCK // LANES
MSG = PIECES * MCAP + SUB
DEPTHS = CX + 3
BRICK = DEPTHS * SUB
PAIR = (2 * CX + 4) * SUB
PACK = 96
NEAR = 32
SHARE = 22
CROSS_MSG = 2 * SUB + PIECES * 2 * MCAP
SPAN = 3 * CY + 3

TIME_STEP = 0.2
MASS_FLOOR = 0.25
VOLUME = 1.0 / BLOCK
VMEM_LIMIT = 12 * 1024 * 1024

IN_VMEM = pl.BlockSpec(memory_space=pltpu.VMEM)
IN_HBM = pl.BlockSpec(memory_space=pltpu.HBM)
F32 = jnp.float32
BF16 = jnp.bfloat16
NN = (((1,), (0,)), ((), ()))
NT = (((1,), (1,)), ((), ()))


def call(kernel, outs, scratch, in_specs, *operands, out_specs=None, flops=1 << 22, bytes_accessed=1 << 19):
    return pl.pallas_call(
        kernel,
        out_shape=tuple(jax.ShapeDtypeStruct(shape, dtype) for shape, dtype in outs),
        in_specs=in_specs,
        out_specs=out_specs or tuple(IN_VMEM for _ in outs),
        scratch_shapes=scratch,
        compiler_params=pltpu.CompilerParams(vmem_limit_bytes=VMEM_LIMIT),
        cost_estimate=pl.CostEstimate(flops=flops, bytes_accessed=bytes_accessed, transcendentals=0),
    )(*operands)


def swap(value, axis, first):
    count = lax.axis_size(axis)
    pairs = []
    for low in range(first, count - 1, 2):
        pairs += [(low, low + 1), (low + 1, low)]
    return lax.ppermute(value, axis, pairs)


def iota(shape, dim):
    return lax.broadcasted_iota(jnp.int32, shape, dim)


def halves(value):
    high = value.astype(BF16)
    return (high, (value - high.astype(F32)).astype(BF16))


def product(parts, onehot, dims):
    rows = parts[0].shape[0]
    stacked = lax.dot_general(jnp.concatenate(parts, axis=0), onehot, dims, preferred_element_type=F32)
    total = stacked[0:rows]
    for index in range(1, len(parts)):
        total = total + stacked[index * rows : (index + 1) * rows]
    return total


def select_rows(onehot, rows):
    high, low = halves(rows)
    twice = jnp.concatenate([onehot, onehot], axis=1)
    return lax.dot_general(twice, jnp.concatenate([high, low], axis=0), NN, preferred_element_type=F32)


def stencil(u):
    p = jnp.maximum(0.25 - u, 0.0)
    q = jnp.maximum(u - 0.75, 0.0)
    p2 = p * p
    q2 = q * q
    weight = (p2, (1.0 - u) - 2.0 * p2 + q2, u + p2 - 2.0 * q2, q2)
    slope = (-2.0 * p, 4.0 * p + 2.0 * q - 1.0, 1.0 - 2.0 * p - 4.0 * q, 2.0 * q)
    return (weight, slope)


def by_material(materials, tables_ref, which):
    value = jnp.zeros(materials.shape, F32)
    for index in range(NMAT):
        row = which * NMAT + index
        value = jnp.where(materials == index, tables_ref[row : row + 1, :], value)
    return value


def column_onehot(column_of):
    first = jnp.broadcast_to(column_of, (LANES, LANES))
    column = iota((LANES, LANES), 0)
    return [(column == first + b).astype(F32).astype(BF16) for b in range(4)]


def row_masks(depth_of, count=CX):
    depth = jnp.broadcast_to(depth_of, (SUB, LANES))
    return [depth == index for index in range(count)]


def scaled(terms, materials, tables_ref):
    sub = iota((SUB, LANES), 0)
    wide = lambda row: jnp.broadcast_to(row, (SUB, LANES))
    scale = jnp.where(sub < 3, wide(by_material(materials, tables_ref, 0) * VOLUME), -VOLUME)
    scale = jnp.where((sub < 5) & (wide(materials) >= 0), scale, 0.0)
    return [[term * scale for term in row] for row in terms]


def node_terms(load, chunks):
    sub = iota((SUB, LANES), 0)
    stencils = [(stencil(load(0, k)), stencil(load(1, k))) for k in range(chunks)]
    terms = [[None] * 4 for _ in range(4)]
    for b in range(4):
        acc = [[None] * 5 for _ in range(4)]
        for k in range(chunks):
            (weight_x, slope_x), (weight_y, slope_y) = stencils[k]
            wy, dy = weight_y[b], slope_y[b]
            sxy = load(6, k)
            y1 = wy * load(2, k)
            y2 = wy * load(3, k)
            y3 = wy * load(4, k)
            y4 = wy * sxy
            y5 = dy * sxy
            y6 = dy * load(5, k)
            for a in range(4):
                wx, dx = weight_x[a], slope_x[a]
                new = (wx * wy, wx * y1, wx * y2, dx * y3 + wx * y5, dx * y4 + wx * y6)
                acc[a] = [n if o is None else o + n for o, n in zip(acc[a], new)]
        for a in range(4):
            packed = jnp.zeros((SUB, LANES), F32)
            for q in range(5):
                total = jnp.sum(acc[a][q], axis=0, keepdims=True)
                packed = jnp.where(sub == q, jnp.broadcast_to(total, (SUB, LANES)), packed)
            terms[a][b] = packed
    return terms


def spread_rows(terms, masks, left_ref):
    zero = jnp.zeros((SUB, LANES), F32)
    for b in range(4):
        for x in range(left_ref.shape[0] // SUB):
            total = zero
            for a in range(4):
                if 0 <= x - a < len(masks):
                    total = total + jnp.where(masks[x - a], terms[a][b], zero)
            left_ref[x * SUB : (x + 1) * SUB, b * LANES : (b + 1) * LANES] = total


def parity(axis):
    return (lax.axis_index(axis) & 1) == 1


def spread_table(table_ref, rows_ref, first):
    table = table_ref[...]
    for index in range(NMAT):
        row = first + index
        rows_ref[row : row + 1, :] = jnp.broadcast_to(table[:, index : index + 1], (1, LANES))


def terms_one(points_ref, turned_ref, terms_ref):
    turned_ref[...] = points_ref[...].T
    load = lambda c, k: rows_at(turned_ref, c, k, BLOCK)
    terms = node_terms(load, BLOCK // SUB)
    for a in range(4):
        for b in range(4):
            row = (4 * a + b) * SUB
            terms_ref[row : row + SUB, :] = terms[a][b]


def sums_one(
    terms_ref, cells_ref, mats_ref, density_ref,
    sums_ref, inner_ref, outer_ref, meta_ref,
    left_ref, density_rows_ref,
):
    spread_table(density_ref, density_rows_ref, 0)
    cells, materials = (cells_ref[...], mats_ref[...])
    meta_ref[0:1, :] = cells
    meta_ref[1:2, :] = materials
    terms = [[terms_ref[(4 * a + b) * SUB : (4 * a + b + 1) * SUB, :] for b in range(4)] for a in range(4)]
    terms = scaled(terms, materials, density_rows_ref)
    spread_rows(terms, row_masks(cells >> 5), left_ref)
    sums = product(halves(left_ref[...]), jnp.concatenate(column_onehot(cells & (CY - 1)), axis=1), NT)
    sums_ref[...] = sums
    to_inner, to_outer = by_side(sums[0:HALO], sums[TOP : TOP + HALO], parity("gx"))
    inner_ref[...] = to_inner
    outer_ref[...] = to_outer


def join_lists(*refs):
    *list_refs, density_ref, shear_ref, lame_ref, lists_ref, tables_ref = refs
    for which, table_ref in enumerate((density_ref, shear_ref, lame_ref)):
        spread_table(table_ref, tables_ref, which * NMAT)
    for index, ref in enumerate(list_refs):
        row = ref[...]
        rest = jnp.full((1, LANES - row.shape[1]), -1, jnp.int32)
        lists_ref[index : index + 1, :] = jnp.concatenate([row, rest], axis=1)


def by_side(inner, outer, odd):
    return (jnp.where(odd, inner, outer), jnp.where(odd, outer, inner))


def put_pieces(ref, first, rows):
    count = rows.shape[0]
    for piece in range(PIECES):
        start = first + piece * count
        ref[start : start + count, :] = rows[:, piece * LANES : (piece + 1) * LANES]


def joined(pieces):
    count = pieces.shape[0] // PIECES
    return jnp.concatenate([pieces[piece * count : (piece + 1) * count] for piece in range(PIECES)], axis=1)


def matches(dests, targets):
    dest = jnp.broadcast_to(dests, (2 * SUB, LANES))
    sub = iota(dest.shape, 0)
    matched = jnp.zeros(dest.shape, F32)
    for o, target in enumerate(targets):
        matched = jnp.where((sub == o) & (dest == target), 1.0, matched)
    square = (LANES, LANES)
    earlier = (iota(square, 0) < iota(square, 1)).astype(F32).astype(BF16)
    rank = lax.dot_general(matched.astype(BF16), earlier, NN, preferred_element_type=F32)
    return (matched, rank)


def placing_rows(matched, rank, groups):
    blank = jnp.zeros((MCAP, LANES), F32)
    place = iota((MCAP, LANES), 0).astype(F32)
    rows = []
    for o in groups:
        if o is None:
            rows.append(blank)
            continue
        hit = jnp.broadcast_to(rank[o : o + 1], blank.shape) == place
        rows.append(jnp.where(hit, jnp.broadcast_to(matched[o : o + 1], blank.shape), 0.0))
    rows += [blank] * (LANES // MCAP - len(groups))
    return jnp.concatenate(rows, axis=0).astype(BF16)


def holding(slots):
    square = (LANES, LANES)
    return (iota(square, 0) == jnp.broadcast_to(slots, square)).astype(F32).astype(BF16)


def small_rows(*rows):
    sub = iota((2 * SUB, LANES), 0)
    value = jnp.zeros((2 * SUB, LANES), F32)
    for index, row in enumerate(rows):
        value = jnp.where(sub == index, jnp.broadcast_to(row.astype(F32), value.shape), value)
    return value.astype(BF16)


def turned_to(small, onehot):
    return lax.dot_general(small, onehot, NT, preferred_element_type=F32)


def tag_tile(*rows):
    sub = iota((SUB, LANES), 0)
    tile = jnp.zeros((SUB, LANES), F32)
    for index, row in enumerate(rows):
        tile = jnp.where(sub == index, jnp.broadcast_to(row, tile.shape), tile)
    return tile


def home_and_steps():
    across = lax.axis_size("gy")
    gx, gy = (lax.axis_index("gx"), lax.axis_index("gy"))
    return (gx * across + gy, across - 2 * across * (gx & 1), 1 - 2 * (gy & 1))


def pick_cross(points_ref, meta_ref, lists_ref, rows_ref, tags_ref, chosen_ref):
    home, _, step_y = home_and_steps()
    chosen = places = None
    for first, groups in ((0, (0, None, 1, None)), (3, (None, 0, None, 1))):
        matched, rank = matches(lists_ref[first + 1 : first + 2, :], (home + step_y, home - step_y))
        placing = placing_rows(matched, rank, groups)
        part = turned_to(placing, holding(lists_ref[first : first + 1, :]))
        cell = lists_ref[first + 2 : first + 3, :]
        place = turned_to(small_rows(cell >> 5, cell & (CY - 1)), placing)
        chosen = part if chosen is None else chosen + part
        places = place if places is None else places + place
    chosen_ref[...] = chosen
    onehot = chosen.astype(BF16)
    cells, materials = (meta_ref[0:1, :], meta_ref[1:2, :])
    found = turned_to(small_rows(materials + 1, cells >> 5, cells & (CY - 1)), onehot)
    tags_ref[...] = tag_tile(
        places[0:1] * float(CY) + places[1:2], found[0:1], found[1:2] * float(CY) + found[2:3]
    )
    rows_ref[...] = select_rows(onehot[0 : 4 * MCAP], points_ref[...])


def merge_rows(sums_ref, from_outer_ref, from_inner_ref, merged_ref):
    from_low, from_high = by_side(from_inner_ref[...], from_outer_ref[...], parity("gx"))
    merged_ref[...] = sums_ref[...]
    merged_ref[0:HALO] = sums_ref[0:HALO] + from_low
    merged_ref[TOP : TOP + HALO] = sums_ref[TOP : TOP + HALO] + from_high


def merge_one(
    sums_ref, from_outer_ref, from_inner_ref, rows_ref, tags_ref,
    merged_ref, inner_ref, outer_ref,
):
    merge_rows(sums_ref, from_outer_ref, from_inner_ref, merged_ref)
    lane = iota((SUB, LANES), 1)
    low = jnp.zeros((SUB, LANES), F32)
    high = jnp.zeros((SUB, LANES), F32)
    for x in range(DEPTHS):
        row = merged_ref[x * SUB : (x + 1) * SUB, :]
        here = (lane >= 3 * x) & (lane < 3 * x + 3)
        shift = 3 * x
        low = jnp.where(here, pltpu.roll(row, shift, 1) if shift else row, low)
        high = jnp.where(here, pltpu.roll(row, (shift - CY) % LANES, 1), high)
    to_inner, to_outer = by_side(low, high, parity("gy"))
    movers = 2 * MCAP
    tags = tags_ref[...]
    for ref, halo, tag, first in (
        (inner_ref, to_inner, tags, 0),
        (outer_ref, to_outer, pltpu.roll(tags, LANES - movers, 1), movers),
    ):
        ref[0:SUB, :] = halo
        ref[SUB : 2 * SUB, :] = jnp.where(lane < movers, tag, 0.0)
        put_pieces(ref, 2 * SUB, rows_ref[first : first + movers, :])


def merge_far(own_ref, from_far_ref, near_nodes_ref, cross_tags_ref, merged_ref, halo_ref):
    del near_nodes_ref, cross_tags_ref
    merged = own_ref[...] + from_far_ref[0:PACK, :]
    merged_ref[...] = merged
    low = jnp.where(iota((2 * SUB, LANES), 0) < 15, merged[0 : 2 * SUB], 0.0)
    halo_ref[...] = jnp.where(parity("gx"), low, merged[PACK - 2 * SUB : PACK])


def merge_two(sums_ref, from_near_ref, near_ref, new_meta_ref, slots_ref, slot_ref):
    del new_meta_ref
    odd = parity("gx")
    from_near = from_near_ref[...]
    slot_ref[...] = sums_ref[...]
    last = PACK - 2 * SUB
    slot_ref[0 : 2 * SUB] = sums_ref[0 : 2 * SUB] + jnp.where(odd, from_near, 0.0)
    slot_ref[last:PACK] = sums_ref[last:PACK] + jnp.where(odd, 0.0, from_near)
    lane = iota((NEAR, LANES), 1)
    near = near_ref[...]
    for third in range(PACK // NEAR):
        start = third * NEAR
        moved = pltpu.roll(near, SPAN - SHARE * third, 1)
        here = (lane >= SPAN) & (lane < SPAN + SHARE)
        slot_ref[start : start + NEAR, :] = jnp.where(here, moved, slot_ref[start : start + NEAR, :])
    value = slot_ref[...]
    for index in range(slots_ref.shape[0]):
        slots_ref[index] = value


def put_velocity(row, x, node_y, velocity_ref):
    node_x = lax.axis_index("gx") * CX - 1 + x
    inside_x = (node_x > 0) & (node_x < CX * lax.axis_size("gx") - 1)
    inside_y = (node_y > 0) & (node_y < CY * lax.axis_size("gy") - 1)
    mass = jnp.maximum(jnp.broadcast_to(row[0:1], (SUB, LANES)), MASS_FLOOR)
    value = (row + TIME_STEP * pltpu.roll(row, SUB - 2, 0)) / mass
    velocity_ref[x * SUB : (x + 1) * SUB, :] = jnp.where(inside_y & inside_x, value, 0.0)


def velocity_one(merged_ref, from_inner, from_outer, velocity_ref):
    low, high = by_side(from_inner, from_outer, parity("gy"))
    lane = iota((SUB, LANES), 1)
    node_y = lax.axis_index("gy") * CY - 1 + lane
    for x in range(DEPTHS):
        row = merged_ref[x * SUB : (x + 1) * SUB, :]
        shift = 3 * x
        row = row + jnp.where(lane < 3, pltpu.roll(low, LANES - shift, 1) if shift else low, 0.0)
        row = row + jnp.where(
            (lane >= CY) & (lane < CY + 3), pltpu.roll(high, (CY - shift) % LANES, 1), 0.0
        )
        put_velocity(row, x, node_y, velocity_ref)
    velocity_ref[DEPTHS * SUB :, :] = jnp.zeros((ROWS - DEPTHS * SUB, LANES), F32)


def velocity_two(slots_ref, packed_ref, velocity_ref):
    gy = lax.axis_index("gy")
    lane = iota((PACK, LANES), 1)
    total = jnp.zeros((PACK, LANES), F32)
    for index in range(slots_ref.shape[0]):
        shift = CY * (index - gy)
        moved = pltpu.roll(slots_ref[index, 0:PACK, :], shift & (LANES - 1), 1)
        valid = (lane >= shift) & (lane < SPAN + shift) & (lane < SPAN)
        total = total + jnp.where(valid, moved, 0.0)
    packed_ref[0:PACK, :] = total
    packed_ref[PACK:, :] = jnp.zeros((packed_ref.shape[0] - PACK, LANES), F32)
    node_y = (gy - 1) * CY - 1 + iota((SUB, LANES), 1)
    for x in range(DEPTHS):
        put_velocity(packed_ref[5 * x : 5 * x + SUB, :], x, node_y, velocity_ref)
    velocity_ref[DEPTHS * SUB :, :] = jnp.zeros((ROWS - DEPTHS * SUB, LANES), F32)


def gathered(velocity_parts, depth_of, column_of):
    masks = row_masks(depth_of)
    near = [[None] * 4 for _ in range(4)]
    columns = product(velocity_parts, jnp.concatenate(column_onehot(column_of), axis=1), NN)
    for b in range(4):
        column = columns[:, b * LANES : (b + 1) * LANES]
        for a in range(4):
            total = jnp.zeros((SUB, LANES), F32)
            for x in range(CX):
                total = jnp.where(masks[x], column[(x + a) * SUB : (x + a + 1) * SUB], total)
            near[a][b] = total
    return near


def move_points(load, store, chunks, node_of, materials, tables_ref):
    wide = lambda row: jnp.broadcast_to(row, (SUB, LANES))
    twice_shear = wide(2.0 * by_material(materials, tables_ref, 1))
    lame = wide(by_material(materials, tables_ref, 2))
    alive = wide(materials) >= 0
    for k in range(chunks):
        u, v = (load(0, k), load(1, k))
        weight_x, slope_x = stencil(u)
        weight_y, slope_y = stencil(v)
        speed, along, across = ([], [], [])
        for component in range(2):
            value = rate_x = rate_y = None
            for a in range(4):
                inner = slant = None
                for b in range(4):
                    node = wide(node_of(a, b, component))
                    term, tilt = (weight_y[b] * node, slope_y[b] * node)
                    inner = term if b == 0 else inner + term
                    slant = tilt if b == 0 else slant + tilt
                add = (weight_x[a] * inner, slope_x[a] * inner, weight_x[a] * slant)
                if a == 0:
                    value, rate_x, rate_y = add
                else:
                    value, rate_x, rate_y = (value + add[0], rate_x + add[1], rate_y + add[2])
            speed.append(value)
            along.append(rate_x)
            across.append(rate_y)
        rate_xx, rate_yy = (along[0], across[1])
        rate_xy = 0.5 * (across[0] + along[1])
        spherical = lame * (rate_xx + rate_yy)
        stress_xx = load(4, k) + TIME_STEP * (twice_shear * rate_xx + spherical)
        stress_yy = load(5, k) + TIME_STEP * (twice_shear * rate_yy + spherical)
        stress_xy = load(6, k) + TIME_STEP * twice_shear * rate_xy
        fresh = (
            jnp.clip(u + TIME_STEP * speed[0], 0.0, 1.0),
            jnp.clip(v + TIME_STEP * speed[1], 0.0, 1.0),
            speed[0],
            speed[1],
            stress_xx,
            stress_yy,
            stress_xy,
            jnp.maximum(load(7, k), -0.5 * (stress_xx + stress_yy)),
        )
        for c in range(8):
            store(c, k, jnp.where(alive, fresh[c], 0.0))


def node_getter(near):
    return lambda a, b, component: near[a][b][component + 1 : component + 2]


def emit_movers(fresh, chosen_ref, tags_ref, far_ref, near_ref):
    rows = select_rows(chosen_ref[...].astype(BF16), fresh.T)
    tags = tags_ref[...]
    lane = iota((SUB, LANES), 1)
    for o, ref in enumerate((far_ref, near_ref)):
        put_pieces(ref, 0, rows[o * MCAP : (o + 1) * MCAP])
        tag = pltpu.roll(tags, LANES - o * MCAP, 1) if o else tags
        ref[MSG - SUB : MSG, :] = jnp.where(lane < MCAP, tag, 0.0)


def own_and_far_depth():
    odd = lax.axis_index("gx") & 1
    return (CX - CX * odd, CX * odd)


def departures(cells, materials, lists):
    home, step_x, _ = home_and_steps()
    slots, dests, cell = (lists[0:1], lists[1:2], lists[2:3])
    moving = (dests >= 0) & (dests != home)
    low, high, far = (dests == home - 1, dests == home + 1, dests == home - step_x)
    carried = jnp.where(low | high | far, 1, 0)
    own, other = own_and_far_depth()
    depth = (cell >> 5) + jnp.where(far, other, own)
    column = (cell & (CY - 1)) + jnp.where(high, 2 * CY, jnp.where(far, CY, 0))
    entries = small_rows(jnp.where(moving, 1, 0), carried, carried * depth, carried * column)
    found = turned_to(entries, holding(slots)).astype(jnp.int32)
    gone, across = (found[0:1] > 0, found[1:2] > 0)
    sub = iota((SUB, LANES), 0)
    wide = lambda value: jnp.broadcast_to(value, (SUB, LANES))
    kept = jnp.where(
        sub == 0,
        wide(jnp.where(gone, 0, cells)),
        wide(jnp.where(gone, -1, materials)),
    )
    target = jnp.where(
        sub == 0,
        wide(jnp.where(across, found[2:3], (cells >> 5) + own)),
        jnp.where(
            sub == 1,
            wide(jnp.where(across, found[3:4], (cells & (CY - 1)) + CY)),
            wide(jnp.where(gone & ~across, -1, materials)),
        ),
    )
    return (kept, target)


def plan_depth(
    meta_ref, lists_ref,
    chosen_a_ref, chosen_b_ref, tags_a_ref, tags_b_ref, kept_a_ref, kept_b_ref, target_ref,
):
    home, step_x, _ = home_and_steps()
    cells, materials = (meta_ref[0:1, :], meta_ref[1:2, :])
    for first, chosen_ref, tags_ref in ((0, chosen_a_ref, tags_a_ref), (3, chosen_b_ref, tags_b_ref)):
        matched, rank = matches(lists_ref[first + 1 : first + 2, :], (home - step_x, home + step_x))
        placing = placing_rows(matched, rank, (0, 1))
        chosen = turned_to(placing, holding(lists_ref[first : first + 1, :]))
        chosen_ref[...] = chosen[0 : 2 * MCAP]
        cell = lists_ref[first + 2 : first + 3, :]
        places = turned_to(small_rows(cell >> 5, cell & (CY - 1)), placing)
        kinds = turned_to(small_rows(materials + 1), chosen.astype(BF16))
        tags_ref[...] = tag_tile(places[0:1] * float(CY) + places[1:2], kinds[0:1])
    kept, target = departures(cells, materials, lists_ref[0:3, :])
    kept_a_ref[...] = kept
    target_ref[...] = target
    kept, _ = departures(kept[0:1], kept[1:2], lists_ref[3:6, :])
    kept_b_ref[...] = kept


def rows_at(ref, c, k, stride):
    return ref[c * stride + k * SUB : c * stride + (k + 1) * SUB, :]


def advance_one(
    turned_ref, meta_ref, merged_ref, yo_ref, yi_ref, tables_ref, chosen_ref, tags_ref,
    fresh_ref, nodes_ref, far_message_ref, near_message_ref,
    velocity_ref,
):
    velocity_one(merged_ref, yi_ref[0:SUB, :], yo_ref[0:SUB, :], velocity_ref)
    cells, materials = (meta_ref[0:1, :], meta_ref[1:2, :])

    def store(c, k, value):
        fresh_ref[c * BLOCK + k * SUB : c * BLOCK + (k + 1) * SUB, :] = value

    near = gathered(halves(velocity_ref[...]), cells >> 5, cells & (CY - 1))
    load = lambda c, k: rows_at(turned_ref, c, k, BLOCK)
    move_points(load, store, BLOCK // SUB, node_getter(near), materials, tables_ref)
    emit_movers(fresh_ref[...], chosen_ref, tags_ref, far_message_ref, near_message_ref)
    for a in range(4):
        for b in range(4):
            row = 2 * (4 * a + b)
            nodes_ref[row : row + 2, :] = near[a][b][1:3]


def sums_kept(fresh_ref, target_ref, tables_ref, sums_ref, left_ref):
    depth, column, materials = (target_ref[0:1, :], target_ref[1:2, :], target_ref[2:3, :])
    load = lambda c, k: rows_at(fresh_ref, c, k, BLOCK)
    terms = scaled(node_terms(load, BLOCK // SUB), materials, tables_ref)
    spread_rows(terms, row_masks(depth, 2 * CX), left_ref)
    sums_ref[...] = product(halves(left_ref[...]), jnp.concatenate(column_onehot(column), axis=1), NT)


def near_cross(nodes_ref, chosen_ref, near_ref):
    near_ref[...] = product(halves(nodes_ref[...]), chosen_ref[...].astype(BF16), NT)


def packed_blocks(rows, wide_ref, turned_ref):
    count = rows.shape[0]
    fill = jnp.zeros((LANES - count, rows.shape[1]), F32)
    wide_ref[...] = jnp.concatenate([rows, fill], axis=0).T
    stride = BLOCK * count // LANES
    for c in range(8):
        total = wide_ref[c * BLOCK : c * BLOCK + stride, :]
        for group in range(1, LANES // count):
            start = c * BLOCK + group * stride
            total = total + pltpu.roll(wide_ref[start : start + stride, :], count * group, 1)
        turned_ref[c * stride : (c + 1) * stride, :] = total


def unpacked_blocks(turned_ref, count, wide_ref):
    stride = BLOCK * count // LANES
    for c in range(8):
        value = turned_ref[c * stride : (c + 1) * stride, :]
        for group in range(LANES // count):
            start = c * BLOCK + group * stride
            shift = (LANES - count * group) % LANES
            wide_ref[start : start + stride, :] = pltpu.roll(value, shift, 1) if shift else value
    return wide_ref[...].T[0:count]


def repeated(tile, count):
    while count < LANES:
        tile = tile + pltpu.roll(tile, count, 1)
        count *= 2
    return tile


def arrived_tags(from_inner, from_outer):
    low, high = by_side(from_inner, from_outer, parity("gx"))
    packed = repeated(low + pltpu.roll(high, MCAP, 1), 2 * MCAP)
    return packed.astype(jnp.int32) - (iota((SUB, LANES), 0) == 1).astype(jnp.int32)


def put_packed(ref, sums):
    ref[PACK - SUB : PACK, :] = jnp.zeros((SUB, LANES), F32)
    for x in range(DEPTHS):
        ref[5 * x : 5 * x + 5, :] = sums[x * SUB : x * SUB + 5]


def sums_two(
    kept_sums_ref, from_near_ref, to_far_ref, tables_ref,
    own_ref, message_ref,
    left_ref, wide_ref, turned_ref,
):
    tags = repeated(from_near_ref[MSG - SUB : MSG, :], MCAP).astype(jnp.int32)
    cells, materials = (tags[0:1], tags[1:2] - 1)
    packed_blocks(joined(from_near_ref[0 : MSG - SUB, :]), wide_ref, turned_ref)
    stride = turned_ref.shape[0] // 8
    load = lambda c, k: rows_at(turned_ref, c, k, stride)
    terms = scaled(node_terms(load, stride // SUB), materials, tables_ref)
    own, _ = own_and_far_depth()
    spread_rows(terms, row_masks((cells >> 5) + own, 2 * CX), left_ref)
    onehots = jnp.concatenate(column_onehot((cells & (CY - 1)) + CY), axis=1)
    sums = product(halves(left_ref[...]), onehots, NT) + kept_sums_ref[...]
    odd = parity("gx")
    first, second = (sums[0:BRICK], sums[CX * SUB : CX * SUB + BRICK])
    put_packed(own_ref, jnp.where(odd, first, second))
    put_packed(message_ref, jnp.where(odd, second, first))
    message_ref[PACK : PACK + MSG, :] = to_far_ref[...]


def arrange_depth(from_near_ref, from_far_ref, turned_ref, new_meta_ref, wide_ref):
    rows, tags = (slice(0, MSG - SUB), slice(MSG - SUB, MSG))
    far = from_far_ref[PACK : PACK + MSG, :]
    new_meta_ref[...] = arrived_tags(from_near_ref[tags, :], far[tags])
    low, high = by_side(from_near_ref[rows, :], far[rows], parity("gx"))
    packed_blocks(jnp.concatenate([joined(low), joined(high)], axis=0), wide_ref, turned_ref)


def arrange_cross(yo_ref, yi_ref, cross_ref, tags_ref, wide_ref):
    low, high = by_side(yi_ref[...], yo_ref[...], parity("gy"))
    tags_ref[...] = low[SUB : 2 * SUB] + pltpu.roll(high[SUB : 2 * SUB], 2 * MCAP, 1)
    rows = jnp.concatenate([joined(low[2 * SUB :]), joined(high[2 * SUB :])], axis=0)
    packed_blocks(rows, wide_ref, cross_ref)


def advance_two(
    kept_ref, meta_ref, slots_ref, tables_ref, chosen_ref, tags_ref,
    fresh_ref, velocity_ref, far_message_ref, near_message_ref,
    packed_ref,
):
    velocity_two(slots_ref, packed_ref, velocity_ref)
    cells, materials = (meta_ref[0:1, :], meta_ref[1:2, :])

    def store(c, k, value):
        fresh_ref[c * BLOCK + k * SUB : c * BLOCK + (k + 1) * SUB, :] = value

    near = gathered(halves(velocity_ref[...]), cells >> 5, (cells & (CY - 1)) + CY)
    load = lambda c, k: rows_at(kept_ref, c, k, BLOCK)
    move_points(load, store, BLOCK // SUB, node_getter(near), materials, tables_ref)
    emit_movers(fresh_ref[...], chosen_ref, tags_ref, far_message_ref, near_message_ref)


def near_movers(slots_ref, index):
    lane = iota((NEAR, LANES), 1)
    nodes = jnp.zeros((NEAR, LANES), F32)
    for third in range(PACK // NEAR):
        first = SHARE * third
        part = slots_ref[index, third * NEAR : (third + 1) * NEAR, :]
        part = pltpu.roll(part, LANES - SPAN + first, 1)
        nodes = jnp.where((lane >= first) & (lane < first + SHARE), part, nodes)
    return nodes


def settle(
    fresh_ref, old_meta_ref, velocity_ref, turned_ref, new_meta_ref, tables_ref, slots_ref, cross_ref, tags_ref,
    rows_ref, tail_ref,
    wide_ref, middle_ref, out_ref, small_ref,
):
    alive = jnp.broadcast_to(old_meta_ref[1:2, :], fresh_ref.shape) >= 0
    rows_ref[0:LANES, :] = jnp.where(alive, fresh_ref[...], 0.0).T
    parts = halves(velocity_ref[...])

    stride = turned_ref.shape[0] // 8
    cells, materials = (new_meta_ref[0:1, :], new_meta_ref[1:2, :])

    def store_small(c, k, value):
        small_ref[c * stride + k * SUB : c * stride + (k + 1) * SUB, :] = value

    load = lambda c, k: rows_at(turned_ref, c, k, stride)
    near = gathered(parts, cells >> 5, (cells & (CY - 1)) + CY)
    move_points(load, store_small, stride // SUB, node_getter(near), materials, tables_ref)
    rows_ref[LANES : LANES + 2 * MCAP, :] = unpacked_blocks(small_ref, 2 * MCAP, wide_ref)

    gy = lax.axis_index("gy")
    odd = parity("gy")
    lane = iota((SUB, LANES), 1)
    tags = tags_ref[...]
    tail = jnp.zeros((SUB, LANES), F32)
    for start, shift in ((32, 32), (48, 16), (96, 80), (112, 64)):
        tail = jnp.where((lane >= start) & (lane < start + MCAP), pltpu.roll(tags, shift, 1), tail)
    materials_row = (iota((SUB, LANES), 0) == 1).astype(jnp.int32)
    tail = tail.astype(jnp.int32) - materials_row
    tail_ref[...] = jnp.where(lane < 2 * MCAP, new_meta_ref[...], tail)
    tags = repeated(tags, 4 * MCAP).astype(jnp.int32) - materials_row

    last = slots_ref.shape[0] - 1
    below = near_movers(slots_ref, jnp.maximum(gy - 1, 0))
    above = near_movers(slots_ref, jnp.minimum(gy + 1, last))
    below = jnp.where(odd, below, pltpu.roll(below, LANES - 2 * MCAP, 1))
    above = jnp.where(odd, above, pltpu.roll(above, 2 * MCAP, 1))
    many = iota((NEAR, LANES), 1)
    nodes = jnp.where(many < 2 * MCAP, below, jnp.where(many < 4 * MCAP, above, 0.0))
    nodes = nodes + pltpu.roll(nodes, 4 * MCAP, 1)

    def node_of(a, b, component):
        row = 2 * (4 * a + b) + component
        return nodes[row : row + 1]

    half = cross_ref.shape[0] // 8
    kinds = tags[1:2]

    def store_middle(c, k, value):
        middle_ref[c * half + k * SUB : c * half + (k + 1) * SUB, :] = value

    move_points(lambda c, k: rows_at(cross_ref, c, k, half), store_middle, half // SUB, node_of, kinds, tables_ref)
    row_lane = lane[0:1]
    second = (row_lane & MCAP) != 0
    cell = jnp.where(second, tags[2:3], tags[0:1])
    side = jnp.where((row_lane & (2 * MCAP)) != 0, 2 * CY, 0)
    near = gathered(parts, cell >> 5, (cell & (CY - 1)) + jnp.where(second, side, CY))

    def store_out(c, k, value):
        out_ref[c * half + k * SUB : c * half + (k + 1) * SUB, :] = value

    move_points(
        lambda c, k: rows_at(middle_ref, c, k, half), store_out, half // SUB, node_getter(near), kinds, tables_ref
    )
    last = unpacked_blocks(out_ref, 4 * MCAP, wide_ref)
    for group, index in enumerate((2, 6, 3, 7)):
        start = LANES + index * MCAP
        rows_ref[start : start + MCAP, :] = last[group * MCAP : (group + 1) * MCAP]


def assemble(
    part_ref, old_meta_ref, tail_ref, xo_ref, xi_ref,
    points_ref, cells_ref, mats_ref,
    tags_ref, rows_ref, sems,
):
    base = points_ref.shape[0] - 4 * MCAP
    odd = lax.axis_index("gx") & 1
    copies = []
    for index, (first, last) in enumerate(((0, base), (base + 2 * MCAP, base + 4 * MCAP))):
        copies.append(pltpu.make_async_copy(part_ref.at[first:last], points_ref.at[first:last], sems.at[index]))
        copies[-1].start()
    for index, (ref, region) in enumerate(((xo_ref, odd), (xi_ref, 1 - odd))):
        start = pl.multiple_of(base + region * MCAP, MCAP)
        rows_ref[index] = joined(ref[0 : MSG - SUB, :])
        copies.append(
            pltpu.make_async_copy(rows_ref.at[index], points_ref.at[pl.ds(start, MCAP), :], sems.at[2 + index])
        )
        copies[-1].start()
    arrived = arrived_tags(xi_ref[MSG - SUB : MSG, :], xo_ref[MSG - SUB : MSG, :])
    lane = iota((1, LANES), 1)
    here = (lane >= 4 * MCAP) & (lane < 6 * MCAP)
    for row, ref in ((0, cells_ref), (1, mats_ref)):
        tags_ref[row, 0:1, :] = old_meta_ref[row : row + 1, :]
        tags_ref[row, 1:2, :] = jnp.where(here, arrived[row : row + 1], tail_ref[row : row + 1, :])
        copies.append(pltpu.make_async_copy(tags_ref.at[row], ref, sems.at[4 + row]))
        copies[-1].start()
    for copy in copies:
        copy.wait()


def shards(
    points,
    block_cell,
    block_mat,
    density,
    shear_modulus,
    lame_modulus,
    mig_slot_a,
    mig_dest_a,
    mig_cell_a,
    mig_slot_b,
    mig_dest_b,
    mig_cell_b,
):
    wide = 8 * BLOCK
    I32 = jnp.int32
    row = lambda value: value.reshape(1, -1)
    cells, mats = (row(block_cell), row(block_mat))
    list_a = (row(mig_slot_a), row(mig_dest_a), row(mig_cell_a))
    list_b = (row(mig_slot_b), row(mig_dest_b), row(mig_cell_b))

    halo = ((HALO, LANES), F32)
    tile = ((SUB, LANES), F32)
    tags = ((SUB, LANES), I32)
    grid = ((ROWS, LANES), F32)
    message = ((MSG, LANES), F32)
    cross_message = ((CROSS_MSG, LANES), F32)
    turned_form = ((wide, LANES), F32)
    half_form = ((wide // 2, LANES), F32)
    quarter_form = ((wide // 4, LANES), F32)
    near_form = ((NEAR, LANES), F32)
    slots_form = ((lax.axis_size("gy"), PACK, LANES), F32)
    scratch = lambda form: pltpu.VMEM(*form)
    left = pltpu.VMEM((ROWS, 4 * LANES), F32)

    def along_depth(far, near):
        return (swap(far, "gx", 1), swap(near, "gx", 0))

    small = (row(density), row(shear_modulus), row(lame_modulus))
    lists, tables = call(
        join_lists, (tags, ((3 * NMAT, LANES), F32)), (), (IN_VMEM,) * 9, *list_a, *list_b, *small
    )
    turned, terms = call(
        terms_one, (turned_form, ((16 * SUB, LANES), F32)), (), (IN_VMEM,), points
    )
    sums, inner, outer, meta = call(
        sums_one,
        (grid, halo, halo, tags),
        (left, pltpu.VMEM((NMAT, LANES), F32)),
        (IN_VMEM,) * 4,
        terms, cells, mats, small[0],
    )
    picked, picked_tags, chosen = call(
        pick_cross,
        (((4 * MCAP, wide), F32), tile, ((LANES, LANES), F32)),
        (),
        (IN_VMEM,) * 3,
        points, meta, lists,
    )
    merged, inner, outer = call(
        merge_one,
        (grid, cross_message, cross_message),
        (),
        (IN_VMEM,) * 5,
        sums, *along_depth(outer, inner), picked, picked_tags,
    )
    cross_far, cross_near = (swap(outer, "gy", 1), swap(inner, "gy", 0))
    chosen_form = ((2 * MCAP, LANES), F32)
    chosen_a, chosen_b, tags_a, tags_b, kept_a, kept_b, target = call(
        plan_depth,
        (chosen_form, chosen_form, tile, tile, tags, tags, tags),
        (),
        (IN_VMEM,) * 2,
        meta, lists,
    )
    fresh, nodes, far, near = call(
        advance_one,
        (turned_form, near_form, message, message),
        (scratch(grid),),
        (IN_VMEM,) * 8,
        turned, meta, merged, cross_far, cross_near, tables, chosen_a, tags_a,
    )
    from_near = swap(near, "gx", 0)
    pair_form = ((PAIR, LANES), F32)
    pair_left = pltpu.VMEM((PAIR, 4 * LANES), F32)
    (kept_sums,) = call(sums_kept, (pair_form,), (pair_left,), (IN_VMEM,) * 3, fresh, target, tables)
    (near_nodes,) = call(near_cross, (near_form,), (), (IN_VMEM,) * 2, nodes, chosen)
    packed_form = ((PACK, LANES), F32)
    own, far_message = call(
        sums_two,
        (packed_form, ((PACK + MSG, LANES), F32)),
        (pair_left, scratch(turned_form), pltpu.VMEM((wide // 8, LANES), F32)),
        (IN_VMEM,) * 4,
        kept_sums, from_near, far, tables,
    )
    from_far = swap(far_message, "gx", 1)
    cross, cross_tags = call(
        arrange_cross, (half_form, tile), (scratch(turned_form),), (IN_VMEM,) * 2, cross_far, cross_near
    )
    merged, halo_message = call(
        merge_far,
        (packed_form, ((2 * SUB, LANES), F32)),
        (),
        (IN_VMEM,) * 4,
        own, from_far, near_nodes, cross_tags,
    )
    turned, new_meta = call(
        arrange_depth, (quarter_form, tags), (scratch(turned_form),), (IN_VMEM,) * 2, from_near, from_far
    )
    (slots,) = call(
        merge_two,
        (slots_form,),
        (scratch(packed_form),),
        (IN_VMEM,) * 4,
        merged, swap(halo_message, "gx", 0), near_nodes, new_meta,
    )
    slots = lax.all_to_all(slots, "gy", 0, 0)
    fresh, velocity, far, near = call(
        advance_two,
        (turned_form, grid, message, message),
        (pltpu.VMEM((PACK + SUB, LANES), F32),),
        (IN_VMEM,) * 6,
        fresh, kept_a, slots, tables, chosen_b, tags_b,
    )
    arrived = along_depth(far, near)
    final_form = ((2 * LANES, wide), F32)
    part, tail = call(
        settle,
        (final_form, tags),
        (
            scratch(turned_form),
            scratch(half_form),
            scratch(half_form),
            scratch(quarter_form),
        ),
        (IN_VMEM,) * 9,
        fresh, kept_b, velocity, turned, new_meta, tables, slots, cross, cross_tags,
    )
    final_points, final_cells, final_mats = call(
        assemble,
        (final_form, ((2, LANES), I32), ((2, LANES), I32)),
        (pltpu.VMEM((2, 2, LANES), I32), pltpu.VMEM((2, MCAP, wide), F32), pltpu.SemaphoreType.DMA((6,))),
        (IN_VMEM,) * 5,
        part, kept_b, tail, *arrived,
        out_specs=(IN_HBM,) * 3,
    )
    return (final_points, final_cells.reshape(-1), final_mats.reshape(-1))


def solution(mesh):
    split = P(("gx", "gy"))
    rows = P(("gx", "gy"), None)
    return jax.shard_map(
        shards,
        mesh=mesh,
        in_specs=(rows, split, split, P(), P(), P()) + (split,) * 6,
        out_specs=(rows, split, split),
        check_vma=False,
    )
```

```python
import jax
import jax.numpy as jnp
from jax import lax
from jax.experimental import pallas as pl
from jax.experimental.pallas import tpu as pltpu
from jax.sharding import PartitionSpec as P

CX = 16
CY = 32
BLOCK = 64
NMAT = 8
MCAP = 16
LANES = 128
SUB = 8
ROWS = 160
HALO = 24
TOP = CX * SUB
PIECES = 8 * BLOCK // LANES
MSG = PIECES * MCAP + SUB
DEPTHS = CX + 3
BRICK = DEPTHS * SUB
PAIR = (2 * CX + 4) * SUB
KEPT = 3
PACK = 64
NEAR = 32
SHARE = 29
REST = 4 * MCAP - 2 * SHARE
SLOT = PACK + SUB
CROSS_MSG = 2 * SUB + PIECES * 2 * MCAP
SPAN = 3 * CY + 3

TIME_STEP = 0.2
MASS_FLOOR = 0.25
VOLUME = 1.0 / BLOCK
VMEM_LIMIT = 12 * 1024 * 1024

IN_VMEM = pl.BlockSpec(memory_space=pltpu.VMEM)
IN_HBM = pl.BlockSpec(memory_space=pltpu.HBM)
F32 = jnp.float32
BF16 = jnp.bfloat16
NN = (((1,), (0,)), ((), ()))
NT = (((1,), (1,)), ((), ()))


def call(kernel, outs, scratch, in_specs, *operands, out_specs=None, flops=1 << 22, bytes_accessed=1 << 19):
    return pl.pallas_call(
        kernel,
        out_shape=tuple(jax.ShapeDtypeStruct(shape, dtype) for shape, dtype in outs),
        in_specs=in_specs,
        out_specs=out_specs or tuple(IN_VMEM for _ in outs),
        scratch_shapes=scratch,
        compiler_params=pltpu.CompilerParams(vmem_limit_bytes=VMEM_LIMIT),
        cost_estimate=pl.CostEstimate(flops=flops, bytes_accessed=bytes_accessed, transcendentals=0),
    )(*operands)


def swap(value, axis, first):
    count = lax.axis_size(axis)
    pairs = []
    for low in range(first, count - 1, 2):
        pairs += [(low, low + 1), (low + 1, low)]
    return lax.ppermute(value, axis, pairs)


def iota(shape, dim):
    return lax.broadcasted_iota(jnp.int32, shape, dim)


def halves(value):
    high = value.astype(BF16)
    return (high, (value - high.astype(F32)).astype(BF16))


def product(parts, onehot, dims):
    rows = parts[0].shape[0]
    stacked = lax.dot_general(jnp.concatenate(parts, axis=0), onehot, dims, preferred_element_type=F32)
    total = stacked[0:rows]
    for index in range(1, len(parts)):
        total = total + stacked[index * rows : (index + 1) * rows]
    return total


def select_rows(onehot, rows):
    high, low = halves(rows)
    twice = jnp.concatenate([onehot, onehot], axis=1)
    return lax.dot_general(twice, jnp.concatenate([high, low], axis=0), NN, preferred_element_type=F32)


def stencil(u):
    p = jnp.maximum(0.25 - u, 0.0)
    q = jnp.maximum(u - 0.75, 0.0)
    p2 = p * p
    q2 = q * q
    weight = (p2, (1.0 - u) - 2.0 * p2 + q2, u + p2 - 2.0 * q2, q2)
    slope = (-2.0 * p, 4.0 * p + 2.0 * q - 1.0, 1.0 - 2.0 * p - 4.0 * q, 2.0 * q)
    return (weight, slope)


def by_material(materials, tables_ref, which):
    value = jnp.zeros(materials.shape, F32)
    for index in range(NMAT):
        row = which * NMAT + index
        value = jnp.where(materials == index, tables_ref[row : row + 1, :], value)
    return value


def column_onehot(column_of):
    first = jnp.broadcast_to(column_of, (LANES, LANES))
    column = iota((LANES, LANES), 0)
    return [(column == first + b).astype(F32).astype(BF16) for b in range(4)]


def row_masks(depth_of, count=CX):
    depth = jnp.broadcast_to(depth_of, (SUB, LANES))
    return [depth == index for index in range(count)]


def scaled(terms, materials, tables_ref):
    sub = iota((SUB, LANES), 0)
    wide = lambda row: jnp.broadcast_to(row, (SUB, LANES))
    mass = jnp.where((sub < KEPT) & (wide(materials) >= 0), wide(by_material(materials, tables_ref, 0) * VOLUME), 0.0)
    push = jnp.where((sub > 0) & (sub < KEPT) & (wide(materials) >= 0), -VOLUME * TIME_STEP, 0.0)
    return [[term * mass + pltpu.roll(term, SUB - 2, 0) * push for term in row] for row in terms]


def weighted_terms(load, chunks, materials, tables_ref):
    sub = iota((SUB, LANES), 0)
    wide = lambda row: jnp.broadcast_to(row, (SUB, LANES))
    rho = wide(by_material(materials, tables_ref, 0))
    scale = jnp.where(sub == 0, rho * VOLUME, VOLUME)
    scale = jnp.where((sub < KEPT) & (wide(materials) >= 0), scale, 0.0)
    stencils = [(stencil(load(0, k)), stencil(load(1, k))) for k in range(chunks)]
    points = [
        (rho * load(2, k), rho * load(3, k)) + tuple(-TIME_STEP * load(c, k) for c in (4, 5, 6))
        for k in range(chunks)
    ]
    terms = [[None] * 4 for _ in range(4)]
    for b in range(4):
        acc = [[None] * KEPT for _ in range(4)]
        for k in range(chunks):
            (weight_x, slope_x), (weight_y, slope_y) = stencils[k]
            wy, dy = weight_y[b], slope_y[b]
            px, py, sxx, syy, sxy = points[k]
            g1, h1 = (wy * px + dy * sxy, wy * sxx)
            g2, h2 = (wy * py + dy * syy, wy * sxy)
            for a in range(4):
                wx, dx = weight_x[a], slope_x[a]
                new = (wx * wy, wx * g1 + dx * h1, wx * g2 + dx * h2)
                acc[a] = [n if o is None else o + n for o, n in zip(acc[a], new)]
        for a in range(4):
            packed = jnp.zeros((SUB, LANES), F32)
            for q in range(KEPT):
                total = jnp.sum(acc[a][q], axis=0, keepdims=True)
                packed = jnp.where(sub == q, jnp.broadcast_to(total, (SUB, LANES)), packed)
            terms[a][b] = packed * scale
    return terms


def node_terms(load, chunks):
    sub = iota((SUB, LANES), 0)
    stencils = [(stencil(load(0, k)), stencil(load(1, k))) for k in range(chunks)]
    terms = [[None] * 4 for _ in range(4)]
    for b in range(4):
        acc = [[None] * 5 for _ in range(4)]
        for k in range(chunks):
            (weight_x, slope_x), (weight_y, slope_y) = stencils[k]
            wy, dy = weight_y[b], slope_y[b]
            sxy = load(6, k)
            y1 = wy * load(2, k)
            y2 = wy * load(3, k)
            y3 = wy * load(4, k)
            y4 = wy * sxy
            y5 = dy * sxy
            y6 = dy * load(5, k)
            for a in range(4):
                wx, dx = weight_x[a], slope_x[a]
                new = (wx * wy, wx * y1, wx * y2, dx * y3 + wx * y5, dx * y4 + wx * y6)
                acc[a] = [n if o is None else o + n for o, n in zip(acc[a], new)]
        for a in range(4):
            packed = jnp.zeros((SUB, LANES), F32)
            for q in range(5):
                total = jnp.sum(acc[a][q], axis=0, keepdims=True)
                packed = jnp.where(sub == q, jnp.broadcast_to(total, (SUB, LANES)), packed)
            terms[a][b] = packed
    return terms


def spread_rows(terms, masks, left_ref):
    zero = jnp.zeros((SUB, LANES), F32)
    for b in range(4):
        for x in range(left_ref.shape[0] // SUB):
            total = zero
            for a in range(4):
                if 0 <= x - a < len(masks):
                    total = total + jnp.where(masks[x - a], terms[a][b], zero)
            left_ref[x * SUB : (x + 1) * SUB, b * LANES : (b + 1) * LANES] = total


def parity(axis):
    return (lax.axis_index(axis) & 1) == 1


def spread_table(table_ref, rows_ref, first):
    table = table_ref[...]
    for index in range(NMAT):
        row = first + index
        rows_ref[row : row + 1, :] = jnp.broadcast_to(table[:, index : index + 1], (1, LANES))


def terms_one(points_ref, turned_ref, terms_ref):
    turned_ref[...] = points_ref[...].T
    load = lambda c, k: rows_at(turned_ref, c, k, BLOCK)
    terms = node_terms(load, BLOCK // SUB)
    for a in range(4):
        for b in range(4):
            row = (4 * a + b) * SUB
            terms_ref[row : row + SUB, :] = terms[a][b]


def sums_one(
    terms_ref, cells_ref, mats_ref, density_ref, shear_ref, lame_ref,
    slot_a_ref, dest_a_ref, cell_a_ref, slot_b_ref, dest_b_ref, cell_b_ref,
    sums_ref, inner_ref, outer_ref, meta_ref, lists_ref, tables_ref,
    left_ref,
):
    for which, table_ref in enumerate((density_ref, shear_ref, lame_ref)):
        spread_table(table_ref, tables_ref, which * NMAT)
    for index, ref in enumerate((slot_a_ref, dest_a_ref, cell_a_ref, slot_b_ref, dest_b_ref, cell_b_ref)):
        entries = ref[...]
        rest = jnp.full((1, LANES - entries.shape[1]), -1, jnp.int32)
        lists_ref[index : index + 1, :] = jnp.concatenate([entries, rest], axis=1)
    cells, materials = (cells_ref[...], mats_ref[...])
    meta_ref[0:1, :] = cells
    meta_ref[1:2, :] = materials
    terms = [[terms_ref[(4 * a + b) * SUB : (4 * a + b + 1) * SUB, :] for b in range(4)] for a in range(4)]
    terms = scaled(terms, materials, tables_ref)
    spread_rows(terms, row_masks(cells >> 5), left_ref)
    sums = product(halves(left_ref[...]), jnp.concatenate(column_onehot(cells & (CY - 1)), axis=1), NT)
    sums_ref[...] = sums
    to_inner, to_outer = by_side(sums[0:HALO], sums[TOP : TOP + HALO], parity("gx"))
    inner_ref[...] = to_inner
    outer_ref[...] = to_outer


def by_side(inner, outer, odd):
    return (jnp.where(odd, inner, outer), jnp.where(odd, outer, inner))


def put_pieces(ref, first, rows):
    count = rows.shape[0]
    for piece in range(PIECES):
        start = first + piece * count
        ref[start : start + count, :] = rows[:, piece * LANES : (piece + 1) * LANES]


def joined(pieces):
    count = pieces.shape[0] // PIECES
    return jnp.concatenate([pieces[piece * count : (piece + 1) * count] for piece in range(PIECES)], axis=1)


def matches(dests, targets):
    dest = jnp.broadcast_to(dests, (2 * SUB, LANES))
    sub = iota(dest.shape, 0)
    matched = jnp.zeros(dest.shape, F32)
    for o, target in enumerate(targets):
        matched = jnp.where((sub == o) & (dest == target), 1.0, matched)
    square = (LANES, LANES)
    earlier = (iota(square, 0) < iota(square, 1)).astype(F32).astype(BF16)
    rank = lax.dot_general(matched.astype(BF16), earlier, NN, preferred_element_type=F32)
    return (matched, rank)


def placing_rows(matched, rank, groups):
    blank = jnp.zeros((MCAP, LANES), F32)
    place = iota((MCAP, LANES), 0).astype(F32)
    rows = []
    for o in groups:
        if o is None:
            rows.append(blank)
            continue
        hit = jnp.broadcast_to(rank[o : o + 1], blank.shape) == place
        rows.append(jnp.where(hit, jnp.broadcast_to(matched[o : o + 1], blank.shape), 0.0))
    rows += [blank] * (LANES // MCAP - len(groups))
    return jnp.concatenate(rows, axis=0).astype(BF16)


def holding(slots):
    square = (LANES, LANES)
    return (iota(square, 0) == jnp.broadcast_to(slots, square)).astype(F32).astype(BF16)


def small_rows(*rows):
    sub = iota((2 * SUB, LANES), 0)
    value = jnp.zeros((2 * SUB, LANES), F32)
    for index, row in enumerate(rows):
        value = jnp.where(sub == index, jnp.broadcast_to(row.astype(F32), value.shape), value)
    return value.astype(BF16)


def turned_to(small, onehot):
    return lax.dot_general(small, onehot, NT, preferred_element_type=F32)


def tag_tile(*rows):
    sub = iota((SUB, LANES), 0)
    tile = jnp.zeros((SUB, LANES), F32)
    for index, row in enumerate(rows):
        tile = jnp.where(sub == index, jnp.broadcast_to(row, tile.shape), tile)
    return tile


def home_and_steps():
    across = lax.axis_size("gy")
    gx, gy = (lax.axis_index("gx"), lax.axis_index("gy"))
    return (gx * across + gy, across - 2 * across * (gx & 1), 1 - 2 * (gy & 1))


def pick_cross(points_ref, meta_ref, lists_ref, rows_ref, tags_ref, chosen_ref):
    home, _, step_y = home_and_steps()
    chosen = places = None
    for first, groups in ((0, (0, None, 1, None)), (3, (None, 0, None, 1))):
        matched, rank = matches(lists_ref[first + 1 : first + 2, :], (home + step_y, home - step_y))
        placing = placing_rows(matched, rank, groups)
        part = turned_to(placing, holding(lists_ref[first : first + 1, :]))
        cell = lists_ref[first + 2 : first + 3, :]
        place = turned_to(small_rows(cell >> 5, cell & (CY - 1)), placing)
        chosen = part if chosen is None else chosen + part
        places = place if places is None else places + place
    chosen_ref[...] = chosen
    onehot = chosen.astype(BF16)
    cells, materials = (meta_ref[0:1, :], meta_ref[1:2, :])
    found = turned_to(small_rows(materials + 1, cells >> 5, cells & (CY - 1)), onehot)
    tags_ref[...] = tag_tile(
        places[0:1] * float(CY) + places[1:2], found[0:1], found[1:2] * float(CY) + found[2:3]
    )
    rows_ref[...] = select_rows(onehot[0 : 4 * MCAP], points_ref[...])


def merge_rows(sums_ref, from_outer_ref, from_inner_ref, merged_ref):
    from_low, from_high = by_side(from_inner_ref[...], from_outer_ref[...], parity("gx"))
    merged_ref[...] = sums_ref[...]
    merged_ref[0:HALO] = sums_ref[0:HALO] + from_low
    merged_ref[TOP : TOP + HALO] = sums_ref[TOP : TOP + HALO] + from_high


def merge_one(
    sums_ref, from_outer_ref, from_inner_ref, rows_ref, tags_ref,
    merged_ref, inner_ref, outer_ref,
):
    merge_rows(sums_ref, from_outer_ref, from_inner_ref, merged_ref)
    lane = iota((SUB, LANES), 1)
    low = jnp.zeros((SUB, LANES), F32)
    high = jnp.zeros((SUB, LANES), F32)
    for x in range(DEPTHS):
        row = merged_ref[x * SUB : (x + 1) * SUB, :]
        here = (lane >= 3 * x) & (lane < 3 * x + 3)
        shift = 3 * x
        low = jnp.where(here, pltpu.roll(row, shift, 1) if shift else row, low)
        high = jnp.where(here, pltpu.roll(row, (shift - CY) % LANES, 1), high)
    to_inner, to_outer = by_side(low, high, parity("gy"))
    movers = 2 * MCAP
    tags = tags_ref[...]
    for ref, halo, tag, first in (
        (inner_ref, to_inner, tags, 0),
        (outer_ref, to_outer, pltpu.roll(tags, LANES - movers, 1), movers),
    ):
        ref[0:SUB, :] = halo
        ref[SUB : 2 * SUB, :] = jnp.where(lane < movers, tag, 0.0)
        put_pieces(ref, 2 * SUB, rows_ref[first : first + movers, :])


def merge_far(own_ref, from_far_ref, near_nodes_ref, cross_tags_ref, merged_ref, halo_ref):
    del near_nodes_ref, cross_tags_ref
    merged = own_ref[...] + from_far_ref[0:PACK, :]
    merged_ref[...] = merged
    low = jnp.where(iota((2 * SUB, LANES), 0) < 3 * KEPT, merged[0 : 2 * SUB], 0.0)
    halo_ref[...] = jnp.where(parity("gx"), low, merged[PACK - 2 * SUB : PACK])


def merge_two(sums_ref, from_near_ref, near_ref, new_meta_ref, slots_ref, slot_ref):
    del new_meta_ref
    odd = parity("gx")
    from_near = from_near_ref[...]
    slot_ref[0:PACK, :] = sums_ref[...]
    last = PACK - 2 * SUB
    slot_ref[0 : 2 * SUB] = sums_ref[0 : 2 * SUB] + jnp.where(odd, from_near, 0.0)
    slot_ref[last:PACK] = sums_ref[last:PACK] + jnp.where(odd, 0.0, from_near)
    lane = iota((NEAR, LANES), 1)
    near = near_ref[...]
    for half in range(2):
        start = half * NEAR
        moved = pltpu.roll(near, SPAN - SHARE * half, 1)
        slot_ref[start : start + NEAR, :] = jnp.where(lane >= SPAN, moved, slot_ref[start : start + NEAR, :])
    lane = iota((SUB, LANES), 1)
    rest = jnp.zeros((SUB, LANES), F32)
    for part in range(NEAR // SUB):
        moved = pltpu.roll(near[part * SUB : (part + 1) * SUB], LANES - 2 * SHARE + REST * part, 1)
        rest = jnp.where((lane >= REST * part) & (lane < REST * (part + 1)), moved, rest)
    slot_ref[PACK:SLOT, :] = rest
    value = slot_ref[...]
    for index in range(slots_ref.shape[0]):
        slots_ref[index] = value


def put_velocity(row, x, node_y, velocity_ref):
    node_x = lax.axis_index("gx") * CX - 1 + x
    inside_x = (node_x > 0) & (node_x < CX * lax.axis_size("gx") - 1)
    inside_y = (node_y > 0) & (node_y < CY * lax.axis_size("gy") - 1)
    mass = jnp.maximum(jnp.broadcast_to(row[0:1], (SUB, LANES)), MASS_FLOOR)
    value = row / mass
    velocity_ref[x * SUB : (x + 1) * SUB, :] = jnp.where(inside_y & inside_x, value, 0.0)


def velocity_one(merged_ref, from_inner, from_outer, velocity_ref):
    low, high = by_side(from_inner, from_outer, parity("gy"))
    lane = iota((SUB, LANES), 1)
    node_y = lax.axis_index("gy") * CY - 1 + lane
    for x in range(DEPTHS):
        row = merged_ref[x * SUB : (x + 1) * SUB, :]
        shift = 3 * x
        row = row + jnp.where(lane < 3, pltpu.roll(low, LANES - shift, 1) if shift else low, 0.0)
        row = row + jnp.where(
            (lane >= CY) & (lane < CY + 3), pltpu.roll(high, (CY - shift) % LANES, 1), 0.0
        )
        put_velocity(row, x, node_y, velocity_ref)
    velocity_ref[DEPTHS * SUB :, :] = jnp.zeros((ROWS - DEPTHS * SUB, LANES), F32)


def velocity_two(slots_ref, packed_ref, velocity_ref):
    gy = lax.axis_index("gy")
    lane = iota((PACK, LANES), 1)
    total = jnp.zeros((PACK, LANES), F32)
    for index in range(slots_ref.shape[0]):
        shift = CY * (index - gy)
        moved = pltpu.roll(slots_ref[index, 0:PACK, :], shift & (LANES - 1), 1)
        valid = (lane >= shift) & (lane < SPAN + shift) & (lane < SPAN)
        total = total + jnp.where(valid, moved, 0.0)
    packed_ref[...] = total
    node_y = (gy - 1) * CY - 1 + iota((SUB, LANES), 1)
    for x in range(DEPTHS):
        put_velocity(packed_ref[KEPT * x : KEPT * x + SUB, :], x, node_y, velocity_ref)
    velocity_ref[DEPTHS * SUB :, :] = jnp.zeros((ROWS - DEPTHS * SUB, LANES), F32)


def gathered(velocity_parts, depth_of, column_of):
    masks = row_masks(depth_of)
    near = [[None] * 4 for _ in range(4)]
    columns = product(velocity_parts, jnp.concatenate(column_onehot(column_of), axis=1), NN)
    for b in range(4):
        column = columns[:, b * LANES : (b + 1) * LANES]
        for a in range(4):
            total = jnp.zeros((SUB, LANES), F32)
            for x in range(CX):
                total = jnp.where(masks[x], column[(x + a) * SUB : (x + a + 1) * SUB], total)
            near[a][b] = total
    return near


def move_points(load, store, chunks, node_of, materials, tables_ref):
    wide = lambda row: jnp.broadcast_to(row, (SUB, LANES))
    twice_shear = wide(2.0 * by_material(materials, tables_ref, 1))
    lame = wide(by_material(materials, tables_ref, 2))
    alive = wide(materials) >= 0
    for k in range(chunks):
        u, v = (load(0, k), load(1, k))
        weight_x, slope_x = stencil(u)
        weight_y, slope_y = stencil(v)
        speed, along, across = ([], [], [])
        for component in range(2):
            value = rate_x = rate_y = None
            for a in range(4):
                inner = slant = None
                for b in range(4):
                    node = wide(node_of(a, b, component))
                    term, tilt = (weight_y[b] * node, slope_y[b] * node)
                    inner = term if b == 0 else inner + term
                    slant = tilt if b == 0 else slant + tilt
                add = (weight_x[a] * inner, slope_x[a] * inner, weight_x[a] * slant)
                if a == 0:
                    value, rate_x, rate_y = add
                else:
                    value, rate_x, rate_y = (value + add[0], rate_x + add[1], rate_y + add[2])
            speed.append(value)
            along.append(rate_x)
            across.append(rate_y)
        rate_xx, rate_yy = (along[0], across[1])
        rate_xy = 0.5 * (across[0] + along[1])
        spherical = lame * (rate_xx + rate_yy)
        stress_xx = load(4, k) + TIME_STEP * (twice_shear * rate_xx + spherical)
        stress_yy = load(5, k) + TIME_STEP * (twice_shear * rate_yy + spherical)
        stress_xy = load(6, k) + TIME_STEP * twice_shear * rate_xy
        fresh = (
            jnp.clip(u + TIME_STEP * speed[0], 0.0, 1.0),
            jnp.clip(v + TIME_STEP * speed[1], 0.0, 1.0),
            speed[0],
            speed[1],
            stress_xx,
            stress_yy,
            stress_xy,
            jnp.maximum(load(7, k), -0.5 * (stress_xx + stress_yy)),
        )
        for c in range(8):
            store(c, k, jnp.where(alive, fresh[c], 0.0))


def node_getter(near):
    return lambda a, b, component: near[a][b][component + 1 : component + 2]


def emit_movers(fresh, chosen_ref, tags_ref, far_ref, near_ref):
    rows = select_rows(chosen_ref[...].astype(BF16), fresh.T)
    tags = tags_ref[...]
    lane = iota((SUB, LANES), 1)
    for o, ref in enumerate((far_ref, near_ref)):
        put_pieces(ref, 0, rows[o * MCAP : (o + 1) * MCAP])
        tag = pltpu.roll(tags, LANES - o * MCAP, 1) if o else tags
        ref[MSG - SUB : MSG, :] = jnp.where(lane < MCAP, tag, 0.0)


def own_and_far_depth():
    odd = lax.axis_index("gx") & 1
    return (CX - CX * odd, CX * odd)


def departures(cells, materials, lists):
    home, step_x, _ = home_and_steps()
    slots, dests, cell = (lists[0:1], lists[1:2], lists[2:3])
    moving = (dests >= 0) & (dests != home)
    low, high, far = (dests == home - 1, dests == home + 1, dests == home - step_x)
    carried = jnp.where(low | high | far, 1, 0)
    own, other = own_and_far_depth()
    depth = (cell >> 5) + jnp.where(far, other, own)
    column = (cell & (CY - 1)) + jnp.where(high, 2 * CY, jnp.where(far, CY, 0))
    entries = small_rows(jnp.where(moving, 1, 0), carried, carried * depth, carried * column)
    found = turned_to(entries, holding(slots)).astype(jnp.int32)
    gone, across = (found[0:1] > 0, found[1:2] > 0)
    sub = iota((SUB, LANES), 0)
    wide = lambda value: jnp.broadcast_to(value, (SUB, LANES))
    kept = jnp.where(
        sub == 0,
        wide(jnp.where(gone, 0, cells)),
        wide(jnp.where(gone, -1, materials)),
    )
    target = jnp.where(
        sub == 0,
        wide(jnp.where(across, found[2:3], (cells >> 5) + own)),
        jnp.where(
            sub == 1,
            wide(jnp.where(across, found[3:4], (cells & (CY - 1)) + CY)),
            wide(jnp.where(gone & ~across, -1, materials)),
        ),
    )
    return (kept, target)


def plan_depth(
    meta_ref, lists_ref,
    chosen_a_ref, chosen_b_ref, tags_a_ref, tags_b_ref, kept_a_ref, kept_b_ref, target_ref,
):
    home, step_x, _ = home_and_steps()
    cells, materials = (meta_ref[0:1, :], meta_ref[1:2, :])
    for first, chosen_ref, tags_ref in ((0, chosen_a_ref, tags_a_ref), (3, chosen_b_ref, tags_b_ref)):
        matched, rank = matches(lists_ref[first + 1 : first + 2, :], (home - step_x, home + step_x))
        placing = placing_rows(matched, rank, (0, 1))
        chosen = turned_to(placing, holding(lists_ref[first : first + 1, :]))
        chosen_ref[...] = chosen[0 : 2 * MCAP]
        cell = lists_ref[first + 2 : first + 3, :]
        places = turned_to(small_rows(cell >> 5, cell & (CY - 1)), placing)
        kinds = turned_to(small_rows(materials + 1), chosen.astype(BF16))
        tags_ref[...] = tag_tile(places[0:1] * float(CY) + places[1:2], kinds[0:1])
    kept, target = departures(cells, materials, lists_ref[0:3, :])
    kept_a_ref[...] = kept
    target_ref[...] = target
    kept, _ = departures(kept[0:1], kept[1:2], lists_ref[3:6, :])
    kept_b_ref[...] = kept


def rows_at(ref, c, k, stride):
    return ref[c * stride + k * SUB : c * stride + (k + 1) * SUB, :]


def advance_one(
    turned_ref, meta_ref, merged_ref, yo_ref, yi_ref, tables_ref, chosen_ref, tags_ref,
    fresh_ref, nodes_ref, far_message_ref, near_message_ref,
    velocity_ref,
):
    velocity_one(merged_ref, yi_ref[0:SUB, :], yo_ref[0:SUB, :], velocity_ref)
    cells, materials = (meta_ref[0:1, :], meta_ref[1:2, :])

    def store(c, k, value):
        fresh_ref[c * BLOCK + k * SUB : c * BLOCK + (k + 1) * SUB, :] = value

    near = gathered(halves(velocity_ref[...]), cells >> 5, cells & (CY - 1))
    load = lambda c, k: rows_at(turned_ref, c, k, BLOCK)
    move_points(load, store, BLOCK // SUB, node_getter(near), materials, tables_ref)
    emit_movers(fresh_ref[...], chosen_ref, tags_ref, far_message_ref, near_message_ref)
    for a in range(4):
        for b in range(4):
            row = 2 * (4 * a + b)
            nodes_ref[row : row + 2, :] = near[a][b][1:3]


def sums_kept(fresh_ref, target_ref, tables_ref, sums_ref, left_ref):
    depth, column, materials = (target_ref[0:1, :], target_ref[1:2, :], target_ref[2:3, :])
    load = lambda c, k: rows_at(fresh_ref, c, k, BLOCK)
    terms = weighted_terms(load, BLOCK // SUB, materials, tables_ref)
    spread_rows(terms, row_masks(depth, 2 * CX), left_ref)
    sums_ref[...] = product(halves(left_ref[...]), jnp.concatenate(column_onehot(column), axis=1), NT)


def near_cross(nodes_ref, chosen_ref, near_ref):
    near_ref[...] = product(halves(nodes_ref[...]), chosen_ref[...].astype(BF16), NT)


def packed_blocks(rows, wide_ref, turned_ref):
    count = rows.shape[0]
    fill = jnp.zeros((LANES - count, rows.shape[1]), F32)
    wide_ref[...] = jnp.concatenate([rows, fill], axis=0).T
    stride = BLOCK * count // LANES
    for c in range(8):
        total = wide_ref[c * BLOCK : c * BLOCK + stride, :]
        for group in range(1, LANES // count):
            start = c * BLOCK + group * stride
            total = total + pltpu.roll(wide_ref[start : start + stride, :], count * group, 1)
        turned_ref[c * stride : (c + 1) * stride, :] = total


def unpacked_blocks(turned_ref, count, wide_ref):
    stride = BLOCK * count // LANES
    for c in range(8):
        value = turned_ref[c * stride : (c + 1) * stride, :]
        for group in range(LANES // count):
            start = c * BLOCK + group * stride
            shift = (LANES - count * group) % LANES
            wide_ref[start : start + stride, :] = pltpu.roll(value, shift, 1) if shift else value
    return wide_ref[...].T[0:count]


def repeated(tile, count):
    while count < LANES:
        tile = tile + pltpu.roll(tile, count, 1)
        count *= 2
    return tile


def arrived_tags(from_inner, from_outer):
    low, high = by_side(from_inner, from_outer, parity("gx"))
    packed = repeated(low + pltpu.roll(high, MCAP, 1), 2 * MCAP)
    return packed.astype(jnp.int32) - (iota((SUB, LANES), 0) == 1).astype(jnp.int32)


def put_packed(ref, sums):
    ref[PACK - SUB : PACK, :] = jnp.zeros((SUB, LANES), F32)
    for x in range(DEPTHS):
        ref[KEPT * x : KEPT * (x + 1), :] = sums[x * SUB : x * SUB + KEPT]


def sums_two(
    kept_sums_ref, from_near_ref, to_far_ref, tables_ref,
    own_ref, message_ref,
    left_ref, wide_ref, turned_ref,
):
    tags = repeated(from_near_ref[MSG - SUB : MSG, :], MCAP).astype(jnp.int32)
    cells, materials = (tags[0:1], tags[1:2] - 1)
    packed_blocks(joined(from_near_ref[0 : MSG - SUB, :]), wide_ref, turned_ref)
    stride = turned_ref.shape[0] // 8
    load = lambda c, k: rows_at(turned_ref, c, k, stride)
    terms = weighted_terms(load, stride // SUB, materials, tables_ref)
    own, _ = own_and_far_depth()
    spread_rows(terms, row_masks((cells >> 5) + own, 2 * CX), left_ref)
    onehots = jnp.concatenate(column_onehot((cells & (CY - 1)) + CY), axis=1)
    sums = product(halves(left_ref[...]), onehots, NT) + kept_sums_ref[...]
    odd = parity("gx")
    first, second = (sums[0:BRICK], sums[CX * SUB : CX * SUB + BRICK])
    put_packed(own_ref, jnp.where(odd, first, second))
    put_packed(message_ref, jnp.where(odd, second, first))
    message_ref[PACK : PACK + MSG, :] = to_far_ref[...]


def arrange_depth(from_near_ref, from_far_ref, turned_ref, new_meta_ref, wide_ref):
    rows, tags = (slice(0, MSG - SUB), slice(MSG - SUB, MSG))
    far = from_far_ref[PACK : PACK + MSG, :]
    new_meta_ref[...] = arrived_tags(from_near_ref[tags, :], far[tags])
    low, high = by_side(from_near_ref[rows, :], far[rows], parity("gx"))
    packed_blocks(jnp.concatenate([joined(low), joined(high)], axis=0), wide_ref, turned_ref)


def arrange_cross(yo_ref, yi_ref, cross_ref, tags_ref, wide_ref):
    low, high = by_side(yi_ref[...], yo_ref[...], parity("gy"))
    tags_ref[...] = low[SUB : 2 * SUB] + pltpu.roll(high[SUB : 2 * SUB], 2 * MCAP, 1)
    rows = jnp.concatenate([joined(low[2 * SUB :]), joined(high[2 * SUB :])], axis=0)
    packed_blocks(rows, wide_ref, cross_ref)


def advance_two(
    kept_ref, meta_ref, slots_ref, tables_ref, chosen_ref, tags_ref,
    fresh_ref, velocity_ref, far_message_ref, near_message_ref,
    packed_ref,
):
    velocity_two(slots_ref, packed_ref, velocity_ref)
    cells, materials = (meta_ref[0:1, :], meta_ref[1:2, :])

    def store(c, k, value):
        fresh_ref[c * BLOCK + k * SUB : c * BLOCK + (k + 1) * SUB, :] = value

    near = gathered(halves(velocity_ref[...]), cells >> 5, (cells & (CY - 1)) + CY)
    load = lambda c, k: rows_at(kept_ref, c, k, BLOCK)
    move_points(load, store, BLOCK // SUB, node_getter(near), materials, tables_ref)
    emit_movers(fresh_ref[...], chosen_ref, tags_ref, far_message_ref, near_message_ref)


def near_movers(slots_ref, index):
    lane = iota((NEAR, LANES), 1)
    rest = slots_ref[index, PACK:SLOT, :]
    parts = []
    for part in range(NEAR // SUB):
        parts.append(pltpu.roll(rest, (2 * SHARE - REST * part) % LANES, 1))
    nodes = jnp.concatenate(parts, axis=0)
    for half in range(2):
        first = SHARE * half
        moved = pltpu.roll(slots_ref[index, half * NEAR : (half + 1) * NEAR, :], LANES - SPAN + first, 1)
        nodes = jnp.where((lane >= first) & (lane < first + SHARE), moved, nodes)
    return nodes


def settle(
    fresh_ref, old_meta_ref, velocity_ref, turned_ref, new_meta_ref, tables_ref, slots_ref, cross_ref, tags_ref,
    rows_ref, tail_ref,
    wide_ref, middle_ref, out_ref, small_ref,
):
    alive = jnp.broadcast_to(old_meta_ref[1:2, :], fresh_ref.shape) >= 0
    rows_ref[0:LANES, :] = jnp.where(alive, fresh_ref[...], 0.0).T
    parts = halves(velocity_ref[...])

    stride = turned_ref.shape[0] // 8
    cells, materials = (new_meta_ref[0:1, :], new_meta_ref[1:2, :])

    def store_small(c, k, value):
        small_ref[c * stride + k * SUB : c * stride + (k + 1) * SUB, :] = value

    load = lambda c, k: rows_at(turned_ref, c, k, stride)
    near = gathered(parts, cells >> 5, (cells & (CY - 1)) + CY)
    move_points(load, store_small, stride // SUB, node_getter(near), materials, tables_ref)
    rows_ref[LANES : LANES + 2 * MCAP, :] = unpacked_blocks(small_ref, 2 * MCAP, wide_ref)

    gy = lax.axis_index("gy")
    odd = parity("gy")
    lane = iota((SUB, LANES), 1)
    tags = tags_ref[...]
    tail = jnp.zeros((SUB, LANES), F32)
    for start, shift in ((32, 32), (48, 16), (96, 80), (112, 64)):
        tail = jnp.where((lane >= start) & (lane < start + MCAP), pltpu.roll(tags, shift, 1), tail)
    materials_row = (iota((SUB, LANES), 0) == 1).astype(jnp.int32)
    tail = tail.astype(jnp.int32) - materials_row
    tail_ref[...] = jnp.where(lane < 2 * MCAP, new_meta_ref[...], tail)
    tags = repeated(tags, 4 * MCAP).astype(jnp.int32) - materials_row

    last = slots_ref.shape[0] - 1
    below = near_movers(slots_ref, jnp.maximum(gy - 1, 0))
    above = near_movers(slots_ref, jnp.minimum(gy + 1, last))
    below = jnp.where(odd, below, pltpu.roll(below, LANES - 2 * MCAP, 1))
    above = jnp.where(odd, above, pltpu.roll(above, 2 * MCAP, 1))
    many = iota((NEAR, LANES), 1)
    nodes = jnp.where(many < 2 * MCAP, below, jnp.where(many < 4 * MCAP, above, 0.0))
    nodes = nodes + pltpu.roll(nodes, 4 * MCAP, 1)

    def node_of(a, b, component):
        row = 2 * (4 * a + b) + component
        return nodes[row : row + 1]

    half = cross_ref.shape[0] // 8
    kinds = tags[1:2]

    def store_middle(c, k, value):
        middle_ref[c * half + k * SUB : c * half + (k + 1) * SUB, :] = value

    move_points(lambda c, k: rows_at(cross_ref, c, k, half), store_middle, half // SUB, node_of, kinds, tables_ref)
    row_lane = lane[0:1]
    second = (row_lane & MCAP) != 0
    cell = jnp.where(second, tags[2:3], tags[0:1])
    side = jnp.where((row_lane & (2 * MCAP)) != 0, 2 * CY, 0)
    near = gathered(parts, cell >> 5, (cell & (CY - 1)) + jnp.where(second, side, CY))

    def store_out(c, k, value):
        out_ref[c * half + k * SUB : c * half + (k + 1) * SUB, :] = value

    move_points(
        lambda c, k: rows_at(middle_ref, c, k, half), store_out, half // SUB, node_getter(near), kinds, tables_ref
    )
    last = unpacked_blocks(out_ref, 4 * MCAP, wide_ref)
    for group, index in enumerate((2, 6, 3, 7)):
        start = LANES + index * MCAP
        rows_ref[start : start + MCAP, :] = last[group * MCAP : (group + 1) * MCAP]


def assemble(
    part_ref, old_meta_ref, tail_ref, xo_ref, xi_ref,
    points_ref, cells_ref, mats_ref,
    tags_ref, rows_ref, sems,
):
    base = points_ref.shape[0] - 4 * MCAP
    odd = lax.axis_index("gx") & 1
    copies = []
    for index, (first, last) in enumerate(((0, base), (base + 2 * MCAP, base + 4 * MCAP))):
        copies.append(pltpu.make_async_copy(part_ref.at[first:last], points_ref.at[first:last], sems.at[index]))
        copies[-1].start()
    for index, (ref, region) in enumerate(((xo_ref, odd), (xi_ref, 1 - odd))):
        start = pl.multiple_of(base + region * MCAP, MCAP)
        rows_ref[index] = joined(ref[0 : MSG - SUB, :])
        copies.append(
            pltpu.make_async_copy(rows_ref.at[index], points_ref.at[pl.ds(start, MCAP), :], sems.at[2 + index])
        )
        copies[-1].start()
    arrived = arrived_tags(xi_ref[MSG - SUB : MSG, :], xo_ref[MSG - SUB : MSG, :])
    lane = iota((1, LANES), 1)
    here = (lane >= 4 * MCAP) & (lane < 6 * MCAP)
    for row, ref in ((0, cells_ref), (1, mats_ref)):
        tags_ref[row, 0:1, :] = old_meta_ref[row : row + 1, :]
        tags_ref[row, 1:2, :] = jnp.where(here, arrived[row : row + 1], tail_ref[row : row + 1, :])
        copies.append(pltpu.make_async_copy(tags_ref.at[row], ref, sems.at[4 + row]))
        copies[-1].start()
    for copy in copies:
        copy.wait()


def shards(
    points,
    block_cell,
    block_mat,
    density,
    shear_modulus,
    lame_modulus,
    mig_slot_a,
    mig_dest_a,
    mig_cell_a,
    mig_slot_b,
    mig_dest_b,
    mig_cell_b,
):
    wide = 8 * BLOCK
    I32 = jnp.int32
    row = lambda value: value.reshape(1, -1)
    cells, mats = (row(block_cell), row(block_mat))
    list_a = (row(mig_slot_a), row(mig_dest_a), row(mig_cell_a))
    list_b = (row(mig_slot_b), row(mig_dest_b), row(mig_cell_b))

    halo = ((HALO, LANES), F32)
    tile = ((SUB, LANES), F32)
    tags = ((SUB, LANES), I32)
    grid = ((ROWS, LANES), F32)
    message = ((MSG, LANES), F32)
    cross_message = ((CROSS_MSG, LANES), F32)
    turned_form = ((wide, LANES), F32)
    half_form = ((wide // 2, LANES), F32)
    quarter_form = ((wide // 4, LANES), F32)
    near_form = ((NEAR, LANES), F32)
    slots_form = ((lax.axis_size("gy"), SLOT, LANES), F32)
    scratch = lambda form: pltpu.VMEM(*form)
    left = pltpu.VMEM((ROWS, 4 * LANES), F32)

    def along_depth(far, near):
        return (swap(far, "gx", 1), swap(near, "gx", 0))

    turned, terms = call(
        terms_one, (turned_form, ((16 * SUB, LANES), F32)), (), (IN_VMEM,), points
    )
    sums, inner, outer, meta, lists, tables = call(
        sums_one,
        (grid, halo, halo, tags, tags, ((3 * NMAT, LANES), F32)),
        (left,),
        (IN_VMEM,) * 12,
        terms, cells, mats, row(density), row(shear_modulus), row(lame_modulus), *list_a, *list_b,
    )
    picked, picked_tags, chosen = call(
        pick_cross,
        (((4 * MCAP, wide), F32), tile, ((LANES, LANES), F32)),
        (),
        (IN_VMEM,) * 3,
        points, meta, lists,
    )
    merged, inner, outer = call(
        merge_one,
        (grid, cross_message, cross_message),
        (),
        (IN_VMEM,) * 5,
        sums, *along_depth(outer, inner), picked, picked_tags,
    )
    cross_far, cross_near = (swap(outer, "gy", 1), swap(inner, "gy", 0))
    chosen_form = ((2 * MCAP, LANES), F32)
    chosen_a, chosen_b, tags_a, tags_b, kept_a, kept_b, target = call(
        plan_depth,
        (chosen_form, chosen_form, tile, tile, tags, tags, tags),
        (),
        (IN_VMEM,) * 2,
        meta, lists,
    )
    fresh, nodes, far, near = call(
        advance_one,
        (turned_form, near_form, message, message),
        (scratch(grid),),
        (IN_VMEM,) * 8,
        turned, meta, merged, cross_far, cross_near, tables, chosen_a, tags_a,
    )
    from_near = swap(near, "gx", 0)
    pair_form = ((PAIR, LANES), F32)
    pair_left = pltpu.VMEM((PAIR, 4 * LANES), F32)
    (kept_sums,) = call(sums_kept, (pair_form,), (pair_left,), (IN_VMEM,) * 3, fresh, target, tables)
    (near_nodes,) = call(near_cross, (near_form,), (), (IN_VMEM,) * 2, nodes, chosen)
    packed_form = ((PACK, LANES), F32)
    own, far_message = call(
        sums_two,
        (packed_form, ((PACK + MSG, LANES), F32)),
        (pair_left, scratch(turned_form), pltpu.VMEM((wide // 8, LANES), F32)),
        (IN_VMEM,) * 4,
        kept_sums, from_near, far, tables,
    )
    from_far = swap(far_message, "gx", 1)
    cross, cross_tags = call(
        arrange_cross, (half_form, tile), (scratch(turned_form),), (IN_VMEM,) * 2, cross_far, cross_near
    )
    merged, halo_message = call(
        merge_far,
        (packed_form, ((2 * SUB, LANES), F32)),
        (),
        (IN_VMEM,) * 4,
        own, from_far, near_nodes, cross_tags,
    )
    turned, new_meta = call(
        arrange_depth, (quarter_form, tags), (scratch(turned_form),), (IN_VMEM,) * 2, from_near, from_far
    )
    (slots,) = call(
        merge_two,
        (slots_form,),
        (pltpu.VMEM((SLOT, LANES), F32),),
        (IN_VMEM,) * 4,
        merged, swap(halo_message, "gx", 0), near_nodes, new_meta,
    )
    slots = lax.all_to_all(slots, "gy", 0, 0)
    fresh, velocity, far, near = call(
        advance_two,
        (turned_form, grid, message, message),
        (scratch(packed_form),),
        (IN_VMEM,) * 6,
        fresh, kept_a, slots, tables, chosen_b, tags_b,
    )
    arrived = along_depth(far, near)
    final_form = ((2 * LANES, wide), F32)
    part, tail = call(
        settle,
        (final_form, tags),
        (
            scratch(turned_form),
            scratch(half_form),
            scratch(half_form),
            scratch(quarter_form),
        ),
        (IN_VMEM,) * 9,
        fresh, kept_b, velocity, turned, new_meta, tables, slots, cross, cross_tags,
    )
    final_points, final_cells, final_mats = call(
        assemble,
        (final_form, ((2, LANES), I32), ((2, LANES), I32)),
        (pltpu.VMEM((2, 2, LANES), I32), pltpu.VMEM((2, MCAP, wide), F32), pltpu.SemaphoreType.DMA((6,))),
        (IN_VMEM,) * 5,
        part, kept_b, tail, *arrived,
        out_specs=(IN_HBM,) * 3,
    )
    return (final_points, final_cells.reshape(-1), final_mats.reshape(-1))


def solution(mesh):
    split = P(("gx", "gy"))
    rows = P(("gx", "gy"), None)
    return jax.shard_map(
        shards,
        mesh=mesh,
        in_specs=(rows, split, split, P(), P(), P()) + (split,) * 6,
        out_specs=(rows, split, split),
        check_vma=False,
    )
```

```python
import jax
import jax.numpy as jnp
from jax import lax
from jax.experimental import pallas as pl
from jax.experimental.pallas import tpu as pltpu
from jax.sharding import PartitionSpec as P

CX = 16
CY = 32
BLOCK = 64
NMAT = 8
MCAP = 16
LANES = 128
SUB = 8
ROWS = 160
HALO = 24
TOP = CX * SUB
PIECES = 8 * BLOCK // LANES
MSG = PIECES * MCAP + SUB
DEPTHS = CX + 3
BRICK = DEPTHS * SUB
PAIR = (2 * CX + 4) * SUB
KEPT = 3
PACK = 64
NEAR = 32
SHARE = 29
REST = 4 * MCAP - 2 * SHARE
SLOT = PACK + SUB
CROSS_MSG = 2 * SUB + PIECES * 2 * MCAP
SPAN = 3 * CY + 3

TIME_STEP = 0.2
MASS_FLOOR = 0.25
VOLUME = 1.0 / BLOCK
VMEM_LIMIT = 12 * 1024 * 1024

IN_VMEM = pl.BlockSpec(memory_space=pltpu.VMEM)
IN_HBM = pl.BlockSpec(memory_space=pltpu.HBM)
F32 = jnp.float32
BF16 = jnp.bfloat16
NN = (((1,), (0,)), ((), ()))
NT = (((1,), (1,)), ((), ()))


def call(kernel, outs, scratch, in_specs, *operands, out_specs=None, flops=1 << 22, bytes_accessed=1 << 19):
    return pl.pallas_call(
        kernel,
        out_shape=tuple(jax.ShapeDtypeStruct(shape, dtype) for shape, dtype in outs),
        in_specs=in_specs,
        out_specs=out_specs or tuple(IN_VMEM for _ in outs),
        scratch_shapes=scratch,
        compiler_params=pltpu.CompilerParams(vmem_limit_bytes=VMEM_LIMIT),
        cost_estimate=pl.CostEstimate(flops=flops, bytes_accessed=bytes_accessed, transcendentals=0),
    )(*operands)


def swap(value, axis, first):
    count = lax.axis_size(axis)
    pairs = []
    for low in range(first, count - 1, 2):
        pairs += [(low, low + 1), (low + 1, low)]
    return lax.ppermute(value, axis, pairs)


def iota(shape, dim):
    return lax.broadcasted_iota(jnp.int32, shape, dim)


def halves(value):
    high = value.astype(BF16)
    return (high, (value - high.astype(F32)).astype(BF16))


def product(parts, onehot, dims):
    rows = parts[0].shape[0]
    stacked = lax.dot_general(jnp.concatenate(parts, axis=0), onehot, dims, preferred_element_type=F32)
    total = stacked[0:rows]
    for index in range(1, len(parts)):
        total = total + stacked[index * rows : (index + 1) * rows]
    return total


def select_rows(onehot, rows):
    high, low = halves(rows)
    twice = jnp.concatenate([onehot, onehot], axis=1)
    return lax.dot_general(twice, jnp.concatenate([high, low], axis=0), NN, preferred_element_type=F32)


def stencil(u):
    p = jnp.maximum(0.25 - u, 0.0)
    q = jnp.maximum(u - 0.75, 0.0)
    p2 = p * p
    q2 = q * q
    weight = (p2, (1.0 - u) - 2.0 * p2 + q2, u + p2 - 2.0 * q2, q2)
    slope = (-2.0 * p, 4.0 * p + 2.0 * q - 1.0, 1.0 - 2.0 * p - 4.0 * q, 2.0 * q)
    return (weight, slope)


def by_material(materials, tables_ref, which):
    value = jnp.zeros(materials.shape, F32)
    for index in range(NMAT):
        row = which * NMAT + index
        value = jnp.where(materials == index, tables_ref[row : row + 1, :], value)
    return value


def column_onehot(column_of):
    first = jnp.broadcast_to(column_of, (LANES, LANES))
    column = iota((LANES, LANES), 0)
    return [(column == first + b).astype(F32).astype(BF16) for b in range(4)]


def row_masks(depth_of, count=CX):
    depth = jnp.broadcast_to(depth_of, (SUB, LANES))
    return [depth == index for index in range(count)]


def scaled(terms, materials, tables_ref):
    sub = iota((SUB, LANES), 0)
    wide = lambda row: jnp.broadcast_to(row, (SUB, LANES))
    mass = jnp.where((sub < KEPT) & (wide(materials) >= 0), wide(by_material(materials, tables_ref, 0) * VOLUME), 0.0)
    push = jnp.where((sub > 0) & (sub < KEPT) & (wide(materials) >= 0), -VOLUME * TIME_STEP, 0.0)
    return [[term * mass + pltpu.roll(term, SUB - 2, 0) * push for term in row] for row in terms]


def weighted_terms(load, chunks, materials, tables_ref):
    sub = iota((SUB, LANES), 0)
    wide = lambda row: jnp.broadcast_to(row, (SUB, LANES))
    rho = wide(by_material(materials, tables_ref, 0))
    scale = jnp.where(sub == 0, rho * VOLUME, VOLUME)
    scale = jnp.where((sub < KEPT) & (wide(materials) >= 0), scale, 0.0)
    stencils = [(stencil(load(0, k)), stencil(load(1, k))) for k in range(chunks)]
    points = [
        (rho * load(2, k), rho * load(3, k)) + tuple(-TIME_STEP * load(c, k) for c in (4, 5, 6))
        for k in range(chunks)
    ]
    terms = [[None] * 4 for _ in range(4)]
    for b in range(4):
        acc = [[None] * KEPT for _ in range(4)]
        for k in range(chunks):
            (weight_x, slope_x), (weight_y, slope_y) = stencils[k]
            wy, dy = weight_y[b], slope_y[b]
            px, py, sxx, syy, sxy = points[k]
            g1, h1 = (wy * px + dy * sxy, wy * sxx)
            g2, h2 = (wy * py + dy * syy, wy * sxy)
            for a in range(4):
                wx, dx = weight_x[a], slope_x[a]
                new = (wx * wy, wx * g1 + dx * h1, wx * g2 + dx * h2)
                acc[a] = [n if o is None else o + n for o, n in zip(acc[a], new)]
        for a in range(4):
            packed = jnp.zeros((SUB, LANES), F32)
            for q in range(KEPT):
                total = jnp.sum(acc[a][q], axis=0, keepdims=True)
                packed = jnp.where(sub == q, jnp.broadcast_to(total, (SUB, LANES)), packed)
            terms[a][b] = packed * scale
    return terms


def node_terms(load, chunks):
    sub = iota((SUB, LANES), 0)
    stencils = [(stencil(load(0, k)), stencil(load(1, k))) for k in range(chunks)]
    terms = [[None] * 4 for _ in range(4)]
    for b in range(4):
        acc = [[None] * 5 for _ in range(4)]
        for k in range(chunks):
            (weight_x, slope_x), (weight_y, slope_y) = stencils[k]
            wy, dy = weight_y[b], slope_y[b]
            sxy = load(6, k)
            y1 = wy * load(2, k)
            y2 = wy * load(3, k)
            y3 = wy * load(4, k)
            y4 = wy * sxy
            y5 = dy * sxy
            y6 = dy * load(5, k)
            for a in range(4):
                wx, dx = weight_x[a], slope_x[a]
                new = (wx * wy, wx * y1, wx * y2, dx * y3 + wx * y5, dx * y4 + wx * y6)
                acc[a] = [n if o is None else o + n for o, n in zip(acc[a], new)]
        for a in range(4):
            packed = jnp.zeros((SUB, LANES), F32)
            for q in range(5):
                total = jnp.sum(acc[a][q], axis=0, keepdims=True)
                packed = jnp.where(sub == q, jnp.broadcast_to(total, (SUB, LANES)), packed)
            terms[a][b] = packed
    return terms


def spread_rows(terms, masks, left_ref):
    zero = jnp.zeros((SUB, LANES), F32)
    for b in range(4):
        for x in range(left_ref.shape[0] // SUB):
            total = zero
            for a in range(4):
                if 0 <= x - a < len(masks):
                    total = total + jnp.where(masks[x - a], terms[a][b], zero)
            left_ref[x * SUB : (x + 1) * SUB, b * LANES : (b + 1) * LANES] = total


def parity(axis):
    return (lax.axis_index(axis) & 1) == 1


def spread_table(table_ref, rows_ref, first):
    table = table_ref[...]
    for index in range(NMAT):
        row = first + index
        rows_ref[row : row + 1, :] = jnp.broadcast_to(table[:, index : index + 1], (1, LANES))


def terms_one(points_ref, meta_ref, turned_ref, terms_ref):
    del meta_ref
    turned_ref[...] = points_ref[...].T
    load = lambda c, k: rows_at(turned_ref, c, k, BLOCK)
    terms = node_terms(load, BLOCK // SUB)
    for a in range(4):
        for b in range(4):
            row = (4 * a + b) * SUB
            terms_ref[row : row + SUB, :] = terms[a][b]


def blank(blank_ref):
    blank_ref[...] = jnp.zeros_like(blank_ref)


def prepare(
    blank_ref, cells_ref, mats_ref, density_ref, shear_ref, lame_ref,
    slot_a_ref, dest_a_ref, cell_a_ref, slot_b_ref, dest_b_ref, cell_b_ref,
    meta_ref, lists_ref, tables_ref,
):
    for which, table_ref in enumerate((density_ref, shear_ref, lame_ref)):
        spread_table(table_ref, tables_ref, which * NMAT)
    lists_ref[...] = blank_ref[...]
    for index, ref in enumerate((slot_a_ref, dest_a_ref, cell_a_ref, slot_b_ref, dest_b_ref, cell_b_ref)):
        entries = ref[...]
        rest = jnp.full((1, LANES - entries.shape[1]), -1, jnp.int32)
        lists_ref[index : index + 1, :] = jnp.concatenate([entries, rest], axis=1)
    meta_ref[...] = blank_ref[...]
    meta_ref[0:1, :] = cells_ref[...]
    meta_ref[1:2, :] = mats_ref[...]


def sums_one(terms_ref, meta_ref, tables_ref, sums_ref, inner_ref, outer_ref, left_ref):
    cells, materials = (meta_ref[0:1, :], meta_ref[1:2, :])
    terms = [[terms_ref[(4 * a + b) * SUB : (4 * a + b + 1) * SUB, :] for b in range(4)] for a in range(4)]
    terms = scaled(terms, materials, tables_ref)
    spread_rows(terms, row_masks(cells >> 5), left_ref)
    sums = product(halves(left_ref[...]), jnp.concatenate(column_onehot(cells & (CY - 1)), axis=1), NT)
    sums_ref[...] = sums
    to_inner, to_outer = by_side(sums[0:HALO], sums[TOP : TOP + HALO], parity("gx"))
    inner_ref[...] = to_inner
    outer_ref[...] = to_outer


def by_side(inner, outer, odd):
    return (jnp.where(odd, inner, outer), jnp.where(odd, outer, inner))


def put_pieces(ref, first, rows):
    count = rows.shape[0]
    for piece in range(PIECES):
        start = first + piece * count
        ref[start : start + count, :] = rows[:, piece * LANES : (piece + 1) * LANES]


def joined(pieces):
    count = pieces.shape[0] // PIECES
    return jnp.concatenate([pieces[piece * count : (piece + 1) * count] for piece in range(PIECES)], axis=1)


def matches(dests, targets):
    dest = jnp.broadcast_to(dests, (2 * SUB, LANES))
    sub = iota(dest.shape, 0)
    matched = jnp.zeros(dest.shape, F32)
    for o, target in enumerate(targets):
        matched = jnp.where((sub == o) & (dest == target), 1.0, matched)
    square = (LANES, LANES)
    earlier = (iota(square, 0) < iota(square, 1)).astype(F32).astype(BF16)
    rank = lax.dot_general(matched.astype(BF16), earlier, NN, preferred_element_type=F32)
    return (matched, rank)


def placing_rows(matched, rank, groups):
    blank = jnp.zeros((MCAP, LANES), F32)
    place = iota((MCAP, LANES), 0).astype(F32)
    rows = []
    for o in groups:
        if o is None:
            rows.append(blank)
            continue
        hit = jnp.broadcast_to(rank[o : o + 1], blank.shape) == place
        rows.append(jnp.where(hit, jnp.broadcast_to(matched[o : o + 1], blank.shape), 0.0))
    rows += [blank] * (LANES // MCAP - len(groups))
    return jnp.concatenate(rows, axis=0).astype(BF16)


def holding(slots):
    square = (LANES, LANES)
    return (iota(square, 0) == jnp.broadcast_to(slots, square)).astype(F32).astype(BF16)


def small_rows(*rows):
    sub = iota((2 * SUB, LANES), 0)
    value = jnp.zeros((2 * SUB, LANES), F32)
    for index, row in enumerate(rows):
        value = jnp.where(sub == index, jnp.broadcast_to(row.astype(F32), value.shape), value)
    return value.astype(BF16)


def turned_to(small, onehot):
    return lax.dot_general(small, onehot, NT, preferred_element_type=F32)


def tag_tile(*rows):
    sub = iota((SUB, LANES), 0)
    tile = jnp.zeros((SUB, LANES), F32)
    for index, row in enumerate(rows):
        tile = jnp.where(sub == index, jnp.broadcast_to(row, tile.shape), tile)
    return tile


def home_and_steps():
    across = lax.axis_size("gy")
    gx, gy = (lax.axis_index("gx"), lax.axis_index("gy"))
    return (gx * across + gy, across - 2 * across * (gx & 1), 1 - 2 * (gy & 1))


def pick_cross(points_ref, meta_ref, lists_ref, rows_ref, tags_ref, chosen_ref):
    home, _, step_y = home_and_steps()
    chosen = places = None
    for first, groups in ((0, (0, None, 1, None)), (3, (None, 0, None, 1))):
        matched, rank = matches(lists_ref[first + 1 : first + 2, :], (home + step_y, home - step_y))
        placing = placing_rows(matched, rank, groups)
        part = turned_to(placing, holding(lists_ref[first : first + 1, :]))
        cell = lists_ref[first + 2 : first + 3, :]
        place = turned_to(small_rows(cell >> 5, cell & (CY - 1)), placing)
        chosen = part if chosen is None else chosen + part
        places = place if places is None else places + place
    chosen_ref[...] = chosen
    onehot = chosen.astype(BF16)
    cells, materials = (meta_ref[0:1, :], meta_ref[1:2, :])
    found = turned_to(small_rows(materials + 1, cells >> 5, cells & (CY - 1)), onehot)
    tags_ref[...] = tag_tile(
        places[0:1] * float(CY) + places[1:2], found[0:1], found[1:2] * float(CY) + found[2:3]
    )
    rows_ref[...] = select_rows(onehot[0 : 4 * MCAP], points_ref[...])


def merge_rows(sums_ref, from_outer_ref, from_inner_ref, merged_ref):
    from_low, from_high = by_side(from_inner_ref[...], from_outer_ref[...], parity("gx"))
    merged_ref[...] = sums_ref[...]
    merged_ref[0:HALO] = sums_ref[0:HALO] + from_low
    merged_ref[TOP : TOP + HALO] = sums_ref[TOP : TOP + HALO] + from_high


def merge_one(
    sums_ref, from_outer_ref, from_inner_ref, rows_ref, tags_ref,
    merged_ref, inner_ref, outer_ref,
):
    merge_rows(sums_ref, from_outer_ref, from_inner_ref, merged_ref)
    lane = iota((SUB, LANES), 1)
    low = jnp.zeros((SUB, LANES), F32)
    high = jnp.zeros((SUB, LANES), F32)
    for x in range(DEPTHS):
        row = merged_ref[x * SUB : (x + 1) * SUB, :]
        here = (lane >= 3 * x) & (lane < 3 * x + 3)
        shift = 3 * x
        low = jnp.where(here, pltpu.roll(row, shift, 1) if shift else row, low)
        high = jnp.where(here, pltpu.roll(row, (shift - CY) % LANES, 1), high)
    to_inner, to_outer = by_side(low, high, parity("gy"))
    movers = 2 * MCAP
    tags = tags_ref[...]
    for ref, halo, tag, first in (
        (inner_ref, to_inner, tags, 0),
        (outer_ref, to_outer, pltpu.roll(tags, LANES - movers, 1), movers),
    ):
        ref[0:SUB, :] = halo
        ref[SUB : 2 * SUB, :] = jnp.where(lane < movers, tag, 0.0)
        put_pieces(ref, 2 * SUB, rows_ref[first : first + movers, :])


def merge_far(own_ref, from_far_ref, near_nodes_ref, cross_tags_ref, merged_ref, halo_ref):
    del near_nodes_ref, cross_tags_ref
    merged = own_ref[...] + from_far_ref[0:PACK, :]
    merged_ref[...] = merged
    low = jnp.where(iota((2 * SUB, LANES), 0) < 3 * KEPT, merged[0 : 2 * SUB], 0.0)
    halo_ref[...] = jnp.where(parity("gx"), low, merged[PACK - 2 * SUB : PACK])


def merge_two(sums_ref, from_near_ref, near_ref, new_meta_ref, slots_ref, slot_ref):
    del new_meta_ref
    odd = parity("gx")
    from_near = from_near_ref[...]
    slot_ref[0:PACK, :] = sums_ref[...]
    last = PACK - 2 * SUB
    slot_ref[0 : 2 * SUB] = sums_ref[0 : 2 * SUB] + jnp.where(odd, from_near, 0.0)
    slot_ref[last:PACK] = sums_ref[last:PACK] + jnp.where(odd, 0.0, from_near)
    lane = iota((NEAR, LANES), 1)
    near = near_ref[...]
    for half in range(2):
        start = half * NEAR
        moved = pltpu.roll(near, SPAN - SHARE * half, 1)
        slot_ref[start : start + NEAR, :] = jnp.where(lane >= SPAN, moved, slot_ref[start : start + NEAR, :])
    lane = iota((SUB, LANES), 1)
    rest = jnp.zeros((SUB, LANES), F32)
    for part in range(NEAR // SUB):
        moved = pltpu.roll(near[part * SUB : (part + 1) * SUB], LANES - 2 * SHARE + REST * part, 1)
        rest = jnp.where((lane >= REST * part) & (lane < REST * (part + 1)), moved, rest)
    slot_ref[PACK:SLOT, :] = rest
    value = slot_ref[...]
    for index in range(slots_ref.shape[0]):
        slots_ref[index] = value


def put_velocity(row, x, node_y, velocity_ref):
    node_x = lax.axis_index("gx") * CX - 1 + x
    inside_x = (node_x > 0) & (node_x < CX * lax.axis_size("gx") - 1)
    inside_y = (node_y > 0) & (node_y < CY * lax.axis_size("gy") - 1)
    mass = jnp.maximum(jnp.broadcast_to(row[0:1], (SUB, LANES)), MASS_FLOOR)
    value = row / mass
    velocity_ref[x * SUB : (x + 1) * SUB, :] = jnp.where(inside_y & inside_x, value, 0.0)


def velocity_one(merged_ref, from_inner, from_outer, velocity_ref):
    low, high = by_side(from_inner, from_outer, parity("gy"))
    lane = iota((SUB, LANES), 1)
    node_y = lax.axis_index("gy") * CY - 1 + lane
    for x in range(DEPTHS):
        row = merged_ref[x * SUB : (x + 1) * SUB, :]
        shift = 3 * x
        row = row + jnp.where(lane < 3, pltpu.roll(low, LANES - shift, 1) if shift else low, 0.0)
        row = row + jnp.where(
            (lane >= CY) & (lane < CY + 3), pltpu.roll(high, (CY - shift) % LANES, 1), 0.0
        )
        put_velocity(row, x, node_y, velocity_ref)
    velocity_ref[DEPTHS * SUB :, :] = jnp.zeros((ROWS - DEPTHS * SUB, LANES), F32)


def velocity_two(slots_ref, packed_ref, velocity_ref):
    gy = lax.axis_index("gy")
    lane = iota((PACK, LANES), 1)
    total = jnp.zeros((PACK, LANES), F32)
    for index in range(slots_ref.shape[0]):
        shift = CY * (index - gy)
        moved = pltpu.roll(slots_ref[index, 0:PACK, :], shift & (LANES - 1), 1)
        valid = (lane >= shift) & (lane < SPAN + shift) & (lane < SPAN)
        total = total + jnp.where(valid, moved, 0.0)
    packed_ref[...] = total
    node_y = (gy - 1) * CY - 1 + iota((SUB, LANES), 1)
    for x in range(DEPTHS):
        put_velocity(packed_ref[KEPT * x : KEPT * x + SUB, :], x, node_y, velocity_ref)
    velocity_ref[DEPTHS * SUB :, :] = jnp.zeros((ROWS - DEPTHS * SUB, LANES), F32)


def gathered(velocity_parts, depth_of, column_of):
    masks = row_masks(depth_of)
    near = [[None] * 4 for _ in range(4)]
    columns = product(velocity_parts, jnp.concatenate(column_onehot(column_of), axis=1), NN)
    for b in range(4):
        column = columns[:, b * LANES : (b + 1) * LANES]
        for a in range(4):
            total = jnp.zeros((SUB, LANES), F32)
            for x in range(CX):
                total = jnp.where(masks[x], column[(x + a) * SUB : (x + a + 1) * SUB], total)
            near[a][b] = total
    return near


def move_points(load, store, chunks, node_of, materials, tables_ref):
    wide = lambda row: jnp.broadcast_to(row, (SUB, LANES))
    twice_shear = wide(2.0 * by_material(materials, tables_ref, 1))
    lame = wide(by_material(materials, tables_ref, 2))
    alive = wide(materials) >= 0
    for k in range(chunks):
        u, v = (load(0, k), load(1, k))
        weight_x, slope_x = stencil(u)
        weight_y, slope_y = stencil(v)
        speed, along, across = ([], [], [])
        for component in range(2):
            value = rate_x = rate_y = None
            for a in range(4):
                inner = slant = None
                for b in range(4):
                    node = wide(node_of(a, b, component))
                    term, tilt = (weight_y[b] * node, slope_y[b] * node)
                    inner = term if b == 0 else inner + term
                    slant = tilt if b == 0 else slant + tilt
                add = (weight_x[a] * inner, slope_x[a] * inner, weight_x[a] * slant)
                if a == 0:
                    value, rate_x, rate_y = add
                else:
                    value, rate_x, rate_y = (value + add[0], rate_x + add[1], rate_y + add[2])
            speed.append(value)
            along.append(rate_x)
            across.append(rate_y)
        rate_xx, rate_yy = (along[0], across[1])
        rate_xy = 0.5 * (across[0] + along[1])
        spherical = lame * (rate_xx + rate_yy)
        stress_xx = load(4, k) + TIME_STEP * (twice_shear * rate_xx + spherical)
        stress_yy = load(5, k) + TIME_STEP * (twice_shear * rate_yy + spherical)
        stress_xy = load(6, k) + TIME_STEP * twice_shear * rate_xy
        fresh = (
            jnp.clip(u + TIME_STEP * speed[0], 0.0, 1.0),
            jnp.clip(v + TIME_STEP * speed[1], 0.0, 1.0),
            speed[0],
            speed[1],
            stress_xx,
            stress_yy,
            stress_xy,
            jnp.maximum(load(7, k), -0.5 * (stress_xx + stress_yy)),
        )
        for c in range(8):
            store(c, k, jnp.where(alive, fresh[c], 0.0))


def node_getter(near):
    return lambda a, b, component: near[a][b][component + 1 : component + 2]


def emit_movers(advanced, chosen_ref, tags_ref, far_ref, near_ref):
    rows = select_rows(chosen_ref[...].astype(BF16), advanced)
    tags = tags_ref[...]
    lane = iota((SUB, LANES), 1)
    for o, ref in enumerate((far_ref, near_ref)):
        put_pieces(ref, 0, rows[o * MCAP : (o + 1) * MCAP])
        tag = pltpu.roll(tags, LANES - o * MCAP, 1) if o else tags
        ref[MSG - SUB : MSG, :] = jnp.where(lane < MCAP, tag, 0.0)


def own_and_far_depth():
    odd = lax.axis_index("gx") & 1
    return (CX - CX * odd, CX * odd)


def departures(cells, materials, lists):
    home, step_x, _ = home_and_steps()
    slots, dests, cell = (lists[0:1], lists[1:2], lists[2:3])
    moving = (dests >= 0) & (dests != home)
    low, high, far = (dests == home - 1, dests == home + 1, dests == home - step_x)
    carried = jnp.where(low | high | far, 1, 0)
    own, other = own_and_far_depth()
    depth = (cell >> 5) + jnp.where(far, other, own)
    column = (cell & (CY - 1)) + jnp.where(high, 2 * CY, jnp.where(far, CY, 0))
    entries = small_rows(jnp.where(moving, 1, 0), carried, carried * depth, carried * column)
    found = turned_to(entries, holding(slots)).astype(jnp.int32)
    gone, across = (found[0:1] > 0, found[1:2] > 0)
    sub = iota((SUB, LANES), 0)
    wide = lambda value: jnp.broadcast_to(value, (SUB, LANES))
    kept = jnp.where(
        sub == 0,
        wide(jnp.where(gone, 0, cells)),
        wide(jnp.where(gone, -1, materials)),
    )
    target = jnp.where(
        sub == 0,
        wide(jnp.where(across, found[2:3], (cells >> 5) + own)),
        jnp.where(
            sub == 1,
            wide(jnp.where(across, found[3:4], (cells & (CY - 1)) + CY)),
            wide(jnp.where(gone & ~across, -1, materials)),
        ),
    )
    return (kept, target)


def plan_depth(
    meta_ref, lists_ref,
    chosen_a_ref, chosen_b_ref, tags_a_ref, tags_b_ref, kept_a_ref, kept_b_ref, target_ref, stays_ref,
):
    home, step_x, _ = home_and_steps()
    cells, materials = (meta_ref[0:1, :], meta_ref[1:2, :])
    for first, chosen_ref, tags_ref in ((0, chosen_a_ref, tags_a_ref), (3, chosen_b_ref, tags_b_ref)):
        matched, rank = matches(lists_ref[first + 1 : first + 2, :], (home - step_x, home + step_x))
        placing = placing_rows(matched, rank, (0, 1))
        chosen = turned_to(placing, holding(lists_ref[first : first + 1, :]))
        chosen_ref[...] = chosen[0 : 2 * MCAP]
        cell = lists_ref[first + 2 : first + 3, :]
        places = turned_to(small_rows(cell >> 5, cell & (CY - 1)), placing)
        kinds = turned_to(small_rows(materials + 1), chosen.astype(BF16))
        tags_ref[...] = tag_tile(places[0:1] * float(CY) + places[1:2], kinds[0:1])
    kept, target = departures(cells, materials, lists_ref[0:3, :])
    kept_a_ref[...] = kept
    target_ref[...] = target
    kept, _ = departures(kept[0:1], kept[1:2], lists_ref[3:6, :])
    kept_b_ref[...] = kept
    stays_ref[...] = jnp.broadcast_to((kept[1:2] >= 0).astype(F32), stays_ref.shape).T


def rows_at(ref, c, k, stride):
    return ref[c * stride + k * SUB : c * stride + (k + 1) * SUB, :]


def advance_one(
    turned_ref, meta_ref, merged_ref, yo_ref, yi_ref, tables_ref, chosen_ref, tags_ref,
    fresh_ref, nodes_ref, far_message_ref, near_message_ref,
    velocity_ref,
):
    velocity_one(merged_ref, yi_ref[0:SUB, :], yo_ref[0:SUB, :], velocity_ref)
    cells, materials = (meta_ref[0:1, :], meta_ref[1:2, :])

    def store(c, k, value):
        fresh_ref[c * BLOCK + k * SUB : c * BLOCK + (k + 1) * SUB, :] = value

    near = gathered(halves(velocity_ref[...]), cells >> 5, cells & (CY - 1))
    load = lambda c, k: rows_at(turned_ref, c, k, BLOCK)
    move_points(load, store, BLOCK // SUB, node_getter(near), materials, tables_ref)
    emit_movers(fresh_ref[...].T, chosen_ref, tags_ref, far_message_ref, near_message_ref)
    for a in range(4):
        for b in range(4):
            row = 2 * (4 * a + b)
            nodes_ref[row : row + 2, :] = near[a][b][1:3]


def sums_kept(fresh_ref, target_ref, tables_ref, sums_ref, left_ref):
    depth, column, materials = (target_ref[0:1, :], target_ref[1:2, :], target_ref[2:3, :])
    load = lambda c, k: rows_at(fresh_ref, c, k, BLOCK)
    terms = weighted_terms(load, BLOCK // SUB, materials, tables_ref)
    spread_rows(terms, row_masks(depth, 2 * CX), left_ref)
    sums_ref[...] = product(halves(left_ref[...]), jnp.concatenate(column_onehot(column), axis=1), NT)


def near_cross(nodes_ref, chosen_ref, near_ref):
    near_ref[...] = product(halves(nodes_ref[...]), chosen_ref[...].astype(BF16), NT)


def packed_blocks(rows, wide_ref, turned_ref):
    count = rows.shape[0]
    fill = jnp.zeros((LANES - count, rows.shape[1]), F32)
    wide_ref[...] = jnp.concatenate([rows, fill], axis=0).T
    stride = BLOCK * count // LANES
    for c in range(8):
        total = wide_ref[c * BLOCK : c * BLOCK + stride, :]
        for group in range(1, LANES // count):
            start = c * BLOCK + group * stride
            total = total + pltpu.roll(wide_ref[start : start + stride, :], count * group, 1)
        turned_ref[c * stride : (c + 1) * stride, :] = total


def repeated(tile, count):
    while count < LANES:
        tile = tile + pltpu.roll(tile, count, 1)
        count *= 2
    return tile


def arrived_tags(from_inner, from_outer):
    low, high = by_side(from_inner, from_outer, parity("gx"))
    packed = repeated(low + pltpu.roll(high, MCAP, 1), 2 * MCAP)
    return packed.astype(jnp.int32) - (iota((SUB, LANES), 0) == 1).astype(jnp.int32)


def put_packed(ref, sums):
    ref[PACK - SUB : PACK, :] = jnp.zeros((SUB, LANES), F32)
    for x in range(DEPTHS):
        ref[KEPT * x : KEPT * (x + 1), :] = sums[x * SUB : x * SUB + KEPT]


def sums_two(
    kept_sums_ref, from_near_ref, to_far_ref, tables_ref,
    own_ref, message_ref,
    left_ref, wide_ref, turned_ref,
):
    tags = repeated(from_near_ref[MSG - SUB : MSG, :], MCAP).astype(jnp.int32)
    cells, materials = (tags[0:1], tags[1:2] - 1)
    packed_blocks(joined(from_near_ref[0 : MSG - SUB, :]), wide_ref, turned_ref)
    stride = turned_ref.shape[0] // 8
    load = lambda c, k: rows_at(turned_ref, c, k, stride)
    terms = weighted_terms(load, stride // SUB, materials, tables_ref)
    spread_rows(terms, row_masks(cells >> 5), left_ref)
    onehots = jnp.concatenate(column_onehot((cells & (CY - 1)) + CY), axis=1)
    part = product(halves(left_ref[...]), onehots, NT)
    odd = parity("gx")
    first, second = (kept_sums_ref[0:BRICK, :], kept_sums_ref[CX * SUB : CX * SUB + BRICK, :])
    put_packed(own_ref, jnp.where(odd, first, second) + part[0:BRICK])
    far = jnp.where(odd, second, first)
    low = far[0:HALO] + jnp.where(odd, part[TOP : TOP + HALO], 0.0)
    high = far[TOP : TOP + HALO] + jnp.where(odd, 0.0, part[0:HALO])
    put_packed(message_ref, jnp.concatenate([low, far[HALO:TOP], high], axis=0))
    message_ref[PACK : PACK + MSG, :] = to_far_ref[...]


def arrange_depth(from_near_ref, from_far_ref, turned_ref, new_meta_ref, wide_ref):
    rows, tags = (slice(0, MSG - SUB), slice(MSG - SUB, MSG))
    far = from_far_ref[PACK : PACK + MSG, :]
    new_meta_ref[...] = arrived_tags(from_near_ref[tags, :], far[tags])
    low, high = by_side(from_near_ref[rows, :], far[rows], parity("gx"))
    packed_blocks(jnp.concatenate([joined(low), joined(high)], axis=0), wide_ref, turned_ref)


def arrange_cross(yo_ref, yi_ref, cross_ref, tags_ref, wide_ref):
    low, high = by_side(yi_ref[...], yo_ref[...], parity("gy"))
    tags_ref[...] = low[SUB : 2 * SUB] + pltpu.roll(high[SUB : 2 * SUB], 2 * MCAP, 1)
    rows = jnp.concatenate([joined(low[2 * SUB :]), joined(high[2 * SUB :])], axis=0)
    packed_blocks(rows, wide_ref, cross_ref)


def advance_two(
    kept_ref, meta_ref, slots_ref, tables_ref, chosen_ref, tags_ref,
    rows_ref, velocity_ref, far_message_ref, near_message_ref,
    packed_ref, fresh_ref,
):
    velocity_two(slots_ref, packed_ref, velocity_ref)
    cells, materials = (meta_ref[0:1, :], meta_ref[1:2, :])

    def store(c, k, value):
        fresh_ref[c * BLOCK + k * SUB : c * BLOCK + (k + 1) * SUB, :] = value

    near = gathered(halves(velocity_ref[...]), cells >> 5, (cells & (CY - 1)) + CY)
    load = lambda c, k: rows_at(kept_ref, c, k, BLOCK)
    move_points(load, store, BLOCK // SUB, node_getter(near), materials, tables_ref)
    advanced = fresh_ref[...].T
    rows_ref[...] = advanced
    emit_movers(advanced, chosen_ref, tags_ref, far_message_ref, near_message_ref)


def near_movers(slots_ref, index):
    lane = iota((NEAR, LANES), 1)
    rest = slots_ref[index, PACK:SLOT, :]
    parts = []
    for part in range(NEAR // SUB):
        parts.append(pltpu.roll(rest, (2 * SHARE - REST * part) % LANES, 1))
    nodes = jnp.concatenate(parts, axis=0)
    for half in range(2):
        first = SHARE * half
        moved = pltpu.roll(slots_ref[index, half * NEAR : (half + 1) * NEAR, :], LANES - SPAN + first, 1)
        nodes = jnp.where((lane >= first) & (lane < first + SHARE), moved, nodes)
    return nodes


def settle(
    advanced_ref, stays_ref, velocity_ref, turned_ref, new_meta_ref, tables_ref, slots_ref, cross_ref, tags_ref,
    rows_ref, tail_ref,
    wide_ref, middle_ref, out_ref, small_ref,
):
    stays = stays_ref[...] > 0.5
    for piece in range(PIECES):
        columns = slice(piece * LANES, (piece + 1) * LANES)
        rows_ref[0:LANES, columns] = jnp.where(stays, advanced_ref[:, columns], 0.0)
    parts = halves(velocity_ref[...])

    stride = turned_ref.shape[0] // 8
    cells, materials = (new_meta_ref[0:1, :], new_meta_ref[1:2, :])

    def store_small(c, k, value):
        small_ref[c * stride + k * SUB : c * stride + (k + 1) * SUB, :] = value

    load = lambda c, k: rows_at(turned_ref, c, k, stride)
    near = gathered(parts, cells >> 5, (cells & (CY - 1)) + CY)
    move_points(load, store_small, stride // SUB, node_getter(near), materials, tables_ref)

    gy = lax.axis_index("gy")
    odd = parity("gy")
    lane = iota((SUB, LANES), 1)
    tags = tags_ref[...]
    tail = jnp.zeros((SUB, LANES), F32)
    for start, shift in ((32, 32), (48, 16), (96, 80), (112, 64)):
        tail = jnp.where((lane >= start) & (lane < start + MCAP), pltpu.roll(tags, shift, 1), tail)
    materials_row = (iota((SUB, LANES), 0) == 1).astype(jnp.int32)
    tail = tail.astype(jnp.int32) - materials_row
    tail_ref[...] = jnp.where(lane < 2 * MCAP, new_meta_ref[...], tail)
    tags = repeated(tags, 4 * MCAP).astype(jnp.int32) - materials_row

    last = slots_ref.shape[0] - 1
    below = near_movers(slots_ref, jnp.maximum(gy - 1, 0))
    above = near_movers(slots_ref, jnp.minimum(gy + 1, last))
    below = jnp.where(odd, below, pltpu.roll(below, LANES - 2 * MCAP, 1))
    above = jnp.where(odd, above, pltpu.roll(above, 2 * MCAP, 1))
    many = iota((NEAR, LANES), 1)
    nodes = jnp.where(many < 2 * MCAP, below, jnp.where(many < 4 * MCAP, above, 0.0))
    nodes = nodes + pltpu.roll(nodes, 4 * MCAP, 1)

    def node_of(a, b, component):
        row = 2 * (4 * a + b) + component
        return nodes[row : row + 1]

    half = cross_ref.shape[0] // 8
    kinds = tags[1:2]

    def store_middle(c, k, value):
        middle_ref[c * half + k * SUB : c * half + (k + 1) * SUB, :] = value

    move_points(lambda c, k: rows_at(cross_ref, c, k, half), store_middle, half // SUB, node_of, kinds, tables_ref)
    row_lane = lane[0:1]
    second = (row_lane & MCAP) != 0
    cell = jnp.where(second, tags[2:3], tags[0:1])
    side = jnp.where((row_lane & (2 * MCAP)) != 0, 2 * CY, 0)
    near = gathered(parts, cell >> 5, (cell & (CY - 1)) + jnp.where(second, side, CY))

    def store_out(c, k, value):
        out_ref[c * half + k * SUB : c * half + (k + 1) * SUB, :] = value

    move_points(
        lambda c, k: rows_at(middle_ref, c, k, half), store_out, half // SUB, node_getter(near), kinds, tables_ref
    )
    crossed = lane < 4 * MCAP
    for c in range(8):
        for k in range(BLOCK // SUB):
            group, rest = divmod(k * SUB, half)
            first = out_ref[c * half + rest : c * half + rest + SUB, :]
            first = pltpu.roll(first, LANES - 4 * MCAP * group, 1) if group else first
            group, rest = divmod(k * SUB, stride)
            second = small_ref[c * stride + rest : c * stride + rest + SUB, :]
            second = pltpu.roll(second, (4 * MCAP - 2 * MCAP * group) % LANES, 1)
            wide_ref[c * BLOCK + k * SUB : c * BLOCK + (k + 1) * SUB, :] = jnp.where(crossed, first, second)
    last = wide_ref[...].T
    rows_ref[LANES : LANES + 2 * MCAP, :] = last[4 * MCAP : 6 * MCAP]
    for group, index in enumerate((2, 6, 3, 7)):
        start = LANES + index * MCAP
        rows_ref[start : start + MCAP, :] = last[group * MCAP : (group + 1) * MCAP]


def assemble(
    part_ref, old_meta_ref, tail_ref, xo_ref, xi_ref,
    points_ref, cells_ref, mats_ref,
    tags_ref, rows_ref, sems,
):
    base = points_ref.shape[0] - 4 * MCAP
    odd = lax.axis_index("gx") & 1
    copies = []
    for index, (first, last) in enumerate(((0, base), (base + 2 * MCAP, base + 4 * MCAP))):
        copies.append(pltpu.make_async_copy(part_ref.at[first:last], points_ref.at[first:last], sems.at[index]))
        copies[-1].start()
    for index, (ref, region) in enumerate(((xo_ref, odd), (xi_ref, 1 - odd))):
        start = pl.multiple_of(base + region * MCAP, MCAP)
        rows_ref[index] = joined(ref[0 : MSG - SUB, :])
        copies.append(
            pltpu.make_async_copy(rows_ref.at[index], points_ref.at[pl.ds(start, MCAP), :], sems.at[2 + index])
        )
        copies[-1].start()
    arrived = arrived_tags(xi_ref[MSG - SUB : MSG, :], xo_ref[MSG - SUB : MSG, :])
    lane = iota((1, LANES), 1)
    here = (lane >= 4 * MCAP) & (lane < 6 * MCAP)
    for row, ref in ((0, cells_ref), (1, mats_ref)):
        tags_ref[row, 0:1, :] = old_meta_ref[row : row + 1, :]
        tags_ref[row, 1:2, :] = jnp.where(here, arrived[row : row + 1], tail_ref[row : row + 1, :])
        copies.append(pltpu.make_async_copy(tags_ref.at[row], ref, sems.at[4 + row]))
        copies[-1].start()
    for copy in copies:
        copy.wait()


def shards(
    points,
    block_cell,
    block_mat,
    density,
    shear_modulus,
    lame_modulus,
    mig_slot_a,
    mig_dest_a,
    mig_cell_a,
    mig_slot_b,
    mig_dest_b,
    mig_cell_b,
):
    wide = 8 * BLOCK
    I32 = jnp.int32
    row = lambda value: value.reshape(1, -1)
    cells, mats = (row(block_cell), row(block_mat))
    list_a = (row(mig_slot_a), row(mig_dest_a), row(mig_cell_a))
    list_b = (row(mig_slot_b), row(mig_dest_b), row(mig_cell_b))

    halo = ((HALO, LANES), F32)
    tile = ((SUB, LANES), F32)
    tags = ((SUB, LANES), I32)
    grid = ((ROWS, LANES), F32)
    message = ((MSG, LANES), F32)
    cross_message = ((CROSS_MSG, LANES), F32)
    turned_form = ((wide, LANES), F32)
    half_form = ((wide // 2, LANES), F32)
    quarter_form = ((wide // 4, LANES), F32)
    near_form = ((NEAR, LANES), F32)
    slots_form = ((lax.axis_size("gy"), SLOT, LANES), F32)
    scratch = lambda form: pltpu.VMEM(*form)
    left = pltpu.VMEM((ROWS, 4 * LANES), F32)

    def along_depth(far, near):
        return (swap(far, "gx", 1), swap(near, "gx", 0))

    (nothing,) = call(blank, (tags,), (), (), flops=1 << 28, bytes_accessed=1 << 10)
    meta, lists, tables = call(
        prepare,
        (tags, tags, ((3 * NMAT, LANES), F32)),
        (),
        (IN_VMEM,) * 12,
        nothing, cells, mats, row(density), row(shear_modulus), row(lame_modulus), *list_a, *list_b,
    )
    turned, terms = call(
        terms_one, (turned_form, ((16 * SUB, LANES), F32)), (), (IN_VMEM,) * 2, points, meta
    )
    sums, inner, outer = call(sums_one, (grid, halo, halo), (left,), (IN_VMEM,) * 3, terms, meta, tables)
    picked, picked_tags, chosen = call(
        pick_cross,
        (((4 * MCAP, wide), F32), tile, ((LANES, LANES), F32)),
        (),
        (IN_VMEM,) * 3,
        points, meta, lists,
    )
    merged, inner, outer = call(
        merge_one,
        (grid, cross_message, cross_message),
        (),
        (IN_VMEM,) * 5,
        sums, *along_depth(outer, inner), picked, picked_tags,
    )
    cross_far, cross_near = (swap(outer, "gy", 1), swap(inner, "gy", 0))
    chosen_form = ((2 * MCAP, LANES), F32)
    chosen_a, chosen_b, tags_a, tags_b, kept_a, kept_b, target, stays = call(
        plan_depth,
        (chosen_form, chosen_form, tile, tile, tags, tags, tags, ((LANES, LANES), F32)),
        (),
        (IN_VMEM,) * 2,
        meta, lists,
    )
    fresh, nodes, far, near = call(
        advance_one,
        (turned_form, near_form, message, message),
        (scratch(grid),),
        (IN_VMEM,) * 8,
        turned, meta, merged, cross_far, cross_near, tables, chosen_a, tags_a,
    )
    from_near = swap(near, "gx", 0)
    pair_form = ((PAIR, LANES), F32)
    pair_left = pltpu.VMEM((PAIR, 4 * LANES), F32)
    (kept_sums,) = call(sums_kept, (pair_form,), (pair_left,), (IN_VMEM,) * 3, fresh, target, tables)
    (near_nodes,) = call(near_cross, (near_form,), (), (IN_VMEM,) * 2, nodes, chosen)
    packed_form = ((PACK, LANES), F32)
    own, far_message = call(
        sums_two,
        (packed_form, ((PACK + MSG, LANES), F32)),
        (left, scratch(turned_form), pltpu.VMEM((wide // 8, LANES), F32)),
        (IN_VMEM,) * 4,
        kept_sums, from_near, far, tables,
    )
    from_far = swap(far_message, "gx", 1)
    cross, cross_tags = call(
        arrange_cross, (half_form, tile), (scratch(turned_form),), (IN_VMEM,) * 2, cross_far, cross_near
    )
    merged, halo_message = call(
        merge_far,
        (packed_form, ((2 * SUB, LANES), F32)),
        (),
        (IN_VMEM,) * 4,
        own, from_far, near_nodes, cross_tags,
    )
    turned, new_meta = call(
        arrange_depth, (quarter_form, tags), (scratch(turned_form),), (IN_VMEM,) * 2, from_near, from_far
    )
    (slots,) = call(
        merge_two,
        (slots_form,),
        (pltpu.VMEM((SLOT, LANES), F32),),
        (IN_VMEM,) * 4,
        merged, swap(halo_message, "gx", 0), near_nodes, new_meta,
    )
    slots = lax.all_to_all(slots, "gy", 0, 0)
    advanced, velocity, far, near = call(
        advance_two,
        (((LANES, wide), F32), grid, message, message),
        (scratch(packed_form), scratch(turned_form)),
        (IN_VMEM,) * 6,
        fresh, kept_a, slots, tables, chosen_b, tags_b,
    )
    arrived = along_depth(far, near)
    final_form = ((2 * LANES, wide), F32)
    part, tail = call(
        settle,
        (final_form, tags),
        (
            scratch(turned_form),
            scratch(half_form),
            scratch(half_form),
            scratch(quarter_form),
        ),
        (IN_VMEM,) * 9,
        advanced, stays, velocity, turned, new_meta, tables, slots, cross, cross_tags,
    )
    final_points, final_cells, final_mats = call(
        assemble,
        (final_form, ((2, LANES), I32), ((2, LANES), I32)),
        (pltpu.VMEM((2, 2, LANES), I32), pltpu.VMEM((2, MCAP, wide), F32), pltpu.SemaphoreType.DMA((6,))),
        (IN_VMEM,) * 5,
        part, kept_b, tail, *arrived,
        out_specs=(IN_HBM,) * 3,
    )
    return (final_points, final_cells.reshape(-1), final_mats.reshape(-1))


def solution(mesh):
    split = P(("gx", "gy"))
    rows = P(("gx", "gy"), None)
    return jax.shard_map(
        shards,
        mesh=mesh,
        in_specs=(rows, split, split, P(), P(), P()) + (split,) * 6,
        out_specs=(rows, split, split),
        check_vma=False,
    )
```

```python
import jax
import jax.numpy as jnp
from jax import lax
from jax.experimental import pallas as pl
from jax.experimental.pallas import tpu as pltpu
from jax.sharding import PartitionSpec as P

CX = 16
CY = 32
BLOCK = 64
NMAT = 8
MCAP = 16
LANES = 128
SUB = 8
ROWS = 160
HALO = 24
TOP = CX * SUB
PIECES = 8 * BLOCK // LANES
MSG = PIECES * MCAP + SUB
DEPTHS = CX + 3
BRICK = DEPTHS * SUB
PAIR = (2 * CX + 4) * SUB
KEPT = 3
PACK = 64
NEAR = 32
HALF = LANES // 2
SLOT = PACK // 2 + 2 * SUB
CROSS_MSG = 2 * SUB + PIECES * 2 * MCAP
SPAN = 3 * CY + 3

TIME_STEP = 0.2
MASS_FLOOR = 0.25
VOLUME = 1.0 / BLOCK
VMEM_LIMIT = 12 * 1024 * 1024

IN_VMEM = pl.BlockSpec(memory_space=pltpu.VMEM)
IN_HBM = pl.BlockSpec(memory_space=pltpu.HBM)
F32 = jnp.float32
BF16 = jnp.bfloat16
NN = (((1,), (0,)), ((), ()))
NT = (((1,), (1,)), ((), ()))


def call(kernel, outs, scratch, in_specs, *operands, out_specs=None, flops=1 << 22, bytes_accessed=1 << 19):
    return pl.pallas_call(
        kernel,
        out_shape=tuple(jax.ShapeDtypeStruct(shape, dtype) for shape, dtype in outs),
        in_specs=in_specs,
        out_specs=out_specs or tuple(IN_VMEM for _ in outs),
        scratch_shapes=scratch,
        compiler_params=pltpu.CompilerParams(vmem_limit_bytes=VMEM_LIMIT),
        cost_estimate=pl.CostEstimate(flops=flops, bytes_accessed=bytes_accessed, transcendentals=0),
    )(*operands)


def swap(value, axis, first):
    count = lax.axis_size(axis)
    pairs = []
    for low in range(first, count - 1, 2):
        pairs += [(low, low + 1), (low + 1, low)]
    return lax.ppermute(value, axis, pairs)


def chip_columns():
    down, across = (lax.axis_size("gx"), lax.axis_size("gy"))
    return [list(range(first * across, (first + 2) * across)) for first in range(0, down, 2)]


def iota(shape, dim):
    return lax.broadcasted_iota(jnp.int32, shape, dim)


def halves(value):
    high = value.astype(BF16)
    return (high, (value - high.astype(F32)).astype(BF16))


def product(parts, onehot, dims):
    rows = parts[0].shape[0]
    stacked = lax.dot_general(jnp.concatenate(parts, axis=0), onehot, dims, preferred_element_type=F32)
    total = stacked[0:rows]
    for index in range(1, len(parts)):
        total = total + stacked[index * rows : (index + 1) * rows]
    return total


def select_rows(onehot, rows):
    high, low = halves(rows)
    twice = jnp.concatenate([onehot, onehot], axis=1)
    return lax.dot_general(twice, jnp.concatenate([high, low], axis=0), NN, preferred_element_type=F32)


def stencil(u):
    p = jnp.maximum(0.25 - u, 0.0)
    q = jnp.maximum(u - 0.75, 0.0)
    p2 = p * p
    q2 = q * q
    weight = (p2, (1.0 - u) - 2.0 * p2 + q2, u + p2 - 2.0 * q2, q2)
    slope = (-2.0 * p, 4.0 * p + 2.0 * q - 1.0, 1.0 - 2.0 * p - 4.0 * q, 2.0 * q)
    return (weight, slope)


def by_material(materials, tables_ref, which):
    value = jnp.zeros(materials.shape, F32)
    for index in range(NMAT):
        row = which * NMAT + index
        value = jnp.where(materials == index, tables_ref[row : row + 1, :], value)
    return value


def column_onehot(column_of):
    first = jnp.broadcast_to(column_of, (LANES, LANES))
    column = iota((LANES, LANES), 0)
    return [(column == first + b).astype(F32).astype(BF16) for b in range(4)]


def row_masks(depth_of, count=CX):
    depth = jnp.broadcast_to(depth_of, (SUB, LANES))
    return [depth == index for index in range(count)]


def scaled(terms, materials, tables_ref):
    sub = iota((SUB, LANES), 0)
    wide = lambda row: jnp.broadcast_to(row, (SUB, LANES))
    mass = jnp.where((sub < KEPT) & (wide(materials) >= 0), wide(by_material(materials, tables_ref, 0) * VOLUME), 0.0)
    push = jnp.where((sub > 0) & (sub < KEPT) & (wide(materials) >= 0), -VOLUME * TIME_STEP, 0.0)
    return [[term * mass + pltpu.roll(term, SUB - 2, 0) * push for term in row] for row in terms]


def weighted_terms(load, chunks, materials, tables_ref):
    sub = iota((SUB, LANES), 0)
    wide = lambda row: jnp.broadcast_to(row, (SUB, LANES))
    rho = wide(by_material(materials, tables_ref, 0))
    scale = jnp.where(sub == 0, rho * VOLUME, VOLUME)
    scale = jnp.where((sub < KEPT) & (wide(materials) >= 0), scale, 0.0)
    stencils = [(stencil(load(0, k)), stencil(load(1, k))) for k in range(chunks)]
    points = [
        (rho * load(2, k), rho * load(3, k)) + tuple(-TIME_STEP * load(c, k) for c in (4, 5, 6))
        for k in range(chunks)
    ]
    terms = [[None] * 4 for _ in range(4)]
    for b in range(4):
        acc = [[None] * KEPT for _ in range(4)]
        for k in range(chunks):
            (weight_x, slope_x), (weight_y, slope_y) = stencils[k]
            wy, dy = weight_y[b], slope_y[b]
            px, py, sxx, syy, sxy = points[k]
            g1, h1 = (wy * px + dy * sxy, wy * sxx)
            g2, h2 = (wy * py + dy * syy, wy * sxy)
            for a in range(4):
                wx, dx = weight_x[a], slope_x[a]
                new = (wx * wy, wx * g1 + dx * h1, wx * g2 + dx * h2)
                acc[a] = [n if o is None else o + n for o, n in zip(acc[a], new)]
        for a in range(4):
            packed = jnp.zeros((SUB, LANES), F32)
            for q in range(KEPT):
                total = jnp.sum(acc[a][q], axis=0, keepdims=True)
                packed = jnp.where(sub == q, jnp.broadcast_to(total, (SUB, LANES)), packed)
            terms[a][b] = packed * scale
    return terms


def node_terms(load, chunks):
    sub = iota((SUB, LANES), 0)
    stencils = [(stencil(load(0, k)), stencil(load(1, k))) for k in range(chunks)]
    terms = [[None] * 4 for _ in range(4)]
    for b in range(4):
        acc = [[None] * 5 for _ in range(4)]
        for k in range(chunks):
            (weight_x, slope_x), (weight_y, slope_y) = stencils[k]
            wy, dy = weight_y[b], slope_y[b]
            sxy = load(6, k)
            y1 = wy * load(2, k)
            y2 = wy * load(3, k)
            y3 = wy * load(4, k)
            y4 = wy * sxy
            y5 = dy * sxy
            y6 = dy * load(5, k)
            for a in range(4):
                wx, dx = weight_x[a], slope_x[a]
                new = (wx * wy, wx * y1, wx * y2, dx * y3 + wx * y5, dx * y4 + wx * y6)
                acc[a] = [n if o is None else o + n for o, n in zip(acc[a], new)]
        for a in range(4):
            packed = jnp.zeros((SUB, LANES), F32)
            for q in range(5):
                total = jnp.sum(acc[a][q], axis=0, keepdims=True)
                packed = jnp.where(sub == q, jnp.broadcast_to(total, (SUB, LANES)), packed)
            terms[a][b] = packed
    return terms


def spread_rows(terms, masks, left_ref):
    zero = jnp.zeros((SUB, LANES), F32)
    for b in range(4):
        for x in range(left_ref.shape[0] // SUB):
            total = zero
            for a in range(4):
                if 0 <= x - a < len(masks):
                    total = total + jnp.where(masks[x - a], terms[a][b], zero)
            left_ref[x * SUB : (x + 1) * SUB, b * LANES : (b + 1) * LANES] = total


def parity(axis):
    return (lax.axis_index(axis) & 1) == 1


def spread_table(table_ref, rows_ref, first):
    table = table_ref[...]
    for index in range(NMAT):
        row = first + index
        rows_ref[row : row + 1, :] = jnp.broadcast_to(table[:, index : index + 1], (1, LANES))


def terms_one(points_ref, meta_ref, turned_ref, terms_ref):
    del meta_ref
    turned_ref[...] = points_ref[...].T
    load = lambda c, k: rows_at(turned_ref, c, k, BLOCK)
    terms = node_terms(load, BLOCK // SUB)
    for a in range(4):
        for b in range(4):
            row = (4 * a + b) * SUB
            terms_ref[row : row + SUB, :] = terms[a][b]


def blank(blank_ref):
    blank_ref[...] = jnp.zeros_like(blank_ref)


def prepare(
    blank_ref, cells_ref, mats_ref, density_ref, shear_ref, lame_ref,
    slot_a_ref, dest_a_ref, cell_a_ref, slot_b_ref, dest_b_ref, cell_b_ref,
    meta_ref, lists_ref, tables_ref,
):
    for which, table_ref in enumerate((density_ref, shear_ref, lame_ref)):
        spread_table(table_ref, tables_ref, which * NMAT)
    lists_ref[...] = blank_ref[...]
    for index, ref in enumerate((slot_a_ref, dest_a_ref, cell_a_ref, slot_b_ref, dest_b_ref, cell_b_ref)):
        entries = ref[...]
        rest = jnp.full((1, LANES - entries.shape[1]), -1, jnp.int32)
        lists_ref[index : index + 1, :] = jnp.concatenate([entries, rest], axis=1)
    meta_ref[...] = blank_ref[...]
    meta_ref[0:1, :] = cells_ref[...]
    meta_ref[1:2, :] = mats_ref[...]


def sums_one(terms_ref, meta_ref, tables_ref, sums_ref, inner_ref, outer_ref, left_ref):
    cells, materials = (meta_ref[0:1, :], meta_ref[1:2, :])
    terms = [[terms_ref[(4 * a + b) * SUB : (4 * a + b + 1) * SUB, :] for b in range(4)] for a in range(4)]
    terms = scaled(terms, materials, tables_ref)
    spread_rows(terms, row_masks(cells >> 5), left_ref)
    sums = product(halves(left_ref[...]), jnp.concatenate(column_onehot(cells & (CY - 1)), axis=1), NT)
    sums_ref[...] = sums
    to_inner, to_outer = by_side(sums[0:HALO], sums[TOP : TOP + HALO], parity("gx"))
    inner_ref[...] = to_inner
    outer_ref[...] = to_outer


def by_side(inner, outer, odd):
    return (jnp.where(odd, inner, outer), jnp.where(odd, outer, inner))


def put_pieces(ref, first, rows):
    count = rows.shape[0]
    for piece in range(PIECES):
        start = first + piece * count
        ref[start : start + count, :] = rows[:, piece * LANES : (piece + 1) * LANES]


def joined(pieces):
    count = pieces.shape[0] // PIECES
    return jnp.concatenate([pieces[piece * count : (piece + 1) * count] for piece in range(PIECES)], axis=1)


def matches(dests, targets):
    dest = jnp.broadcast_to(dests, (2 * SUB, LANES))
    sub = iota(dest.shape, 0)
    matched = jnp.zeros(dest.shape, F32)
    for o, target in enumerate(targets):
        matched = jnp.where((sub == o) & (dest == target), 1.0, matched)
    square = (LANES, LANES)
    earlier = (iota(square, 0) < iota(square, 1)).astype(F32).astype(BF16)
    rank = lax.dot_general(matched.astype(BF16), earlier, NN, preferred_element_type=F32)
    return (matched, rank)


def placing_rows(matched, rank, groups):
    blank = jnp.zeros((MCAP, LANES), F32)
    place = iota((MCAP, LANES), 0).astype(F32)
    rows = []
    for o in groups:
        if o is None:
            rows.append(blank)
            continue
        hit = jnp.broadcast_to(rank[o : o + 1], blank.shape) == place
        rows.append(jnp.where(hit, jnp.broadcast_to(matched[o : o + 1], blank.shape), 0.0))
    rows += [blank] * (LANES // MCAP - len(groups))
    return jnp.concatenate(rows, axis=0).astype(BF16)


def holding(slots):
    square = (LANES, LANES)
    return (iota(square, 0) == jnp.broadcast_to(slots, square)).astype(F32).astype(BF16)


def small_rows(*rows):
    sub = iota((2 * SUB, LANES), 0)
    value = jnp.zeros((2 * SUB, LANES), F32)
    for index, row in enumerate(rows):
        value = jnp.where(sub == index, jnp.broadcast_to(row.astype(F32), value.shape), value)
    return value.astype(BF16)


def turned_to(small, onehot):
    return lax.dot_general(small, onehot, NT, preferred_element_type=F32)


def tag_tile(*rows):
    sub = iota((SUB, LANES), 0)
    tile = jnp.zeros((SUB, LANES), F32)
    for index, row in enumerate(rows):
        tile = jnp.where(sub == index, jnp.broadcast_to(row, tile.shape), tile)
    return tile


def home_and_steps():
    across = lax.axis_size("gy")
    gx, gy = (lax.axis_index("gx"), lax.axis_index("gy"))
    return (gx * across + gy, across - 2 * across * (gx & 1), 1 - 2 * (gy & 1))


def pick_cross(points_ref, meta_ref, lists_ref, rows_ref, tags_ref, chosen_ref):
    home, _, step_y = home_and_steps()
    chosen = places = None
    for first, groups in ((0, (0, None, 1, None)), (3, (None, 0, None, 1))):
        matched, rank = matches(lists_ref[first + 1 : first + 2, :], (home + step_y, home - step_y))
        placing = placing_rows(matched, rank, groups)
        part = turned_to(placing, holding(lists_ref[first : first + 1, :]))
        cell = lists_ref[first + 2 : first + 3, :]
        place = turned_to(small_rows(cell >> 5, cell & (CY - 1)), placing)
        chosen = part if chosen is None else chosen + part
        places = place if places is None else places + place
    chosen_ref[...] = chosen
    onehot = chosen.astype(BF16)
    cells, materials = (meta_ref[0:1, :], meta_ref[1:2, :])
    found = turned_to(small_rows(materials + 1, cells >> 5, cells & (CY - 1)), onehot)
    tags_ref[...] = tag_tile(
        places[0:1] * float(CY) + places[1:2], found[0:1], found[1:2] * float(CY) + found[2:3]
    )
    rows_ref[...] = select_rows(onehot[0 : 4 * MCAP], points_ref[...])


def merge_rows(sums_ref, from_outer_ref, from_inner_ref, merged_ref):
    from_low, from_high = by_side(from_inner_ref[...], from_outer_ref[...], parity("gx"))
    merged_ref[...] = sums_ref[...]
    merged_ref[0:HALO] = sums_ref[0:HALO] + from_low
    merged_ref[TOP : TOP + HALO] = sums_ref[TOP : TOP + HALO] + from_high


def merge_one(
    sums_ref, from_outer_ref, from_inner_ref, rows_ref, tags_ref,
    merged_ref, inner_ref, outer_ref,
):
    merge_rows(sums_ref, from_outer_ref, from_inner_ref, merged_ref)
    lane = iota((SUB, LANES), 1)
    low = jnp.zeros((SUB, LANES), F32)
    high = jnp.zeros((SUB, LANES), F32)
    for x in range(DEPTHS):
        row = merged_ref[x * SUB : (x + 1) * SUB, :]
        here = (lane >= 3 * x) & (lane < 3 * x + 3)
        shift = 3 * x
        low = jnp.where(here, pltpu.roll(row, shift, 1) if shift else row, low)
        high = jnp.where(here, pltpu.roll(row, (shift - CY) % LANES, 1), high)
    to_inner, to_outer = by_side(low, high, parity("gy"))
    movers = 2 * MCAP
    tags = tags_ref[...]
    for ref, halo, tag, first in (
        (inner_ref, to_inner, tags, 0),
        (outer_ref, to_outer, pltpu.roll(tags, LANES - movers, 1), movers),
    ):
        ref[0:SUB, :] = halo
        ref[SUB : 2 * SUB, :] = jnp.where(lane < movers, tag, 0.0)
        put_pieces(ref, 2 * SUB, rows_ref[first : first + movers, :])


def merge_far(own_ref, from_far_ref, near_ref, cross_tags_ref, merged_ref, slots_ref):
    del cross_tags_ref
    merged = own_ref[...] + from_far_ref[0:PACK, :]
    merged_ref[...] = merged
    gy = lax.axis_index("gy")
    mine = lax.axis_index("gx") & 1
    low = jnp.where(iota((2 * SUB, LANES), 0) < 3 * KEPT, merged[0 : 2 * SUB], 0.0)
    halo = jnp.where(parity("gx"), low, merged[PACK - 2 * SUB : PACK])
    near = near_ref[...]
    tile_lane = iota((SUB, LANES), 1)
    velocities = []
    for start in (0, HALF // 2):
        tile = jnp.zeros((SUB, LANES), F32)
        for part in range(NEAR // SUB):
            shift = (part * NEAR - start) % LANES
            rows = near[part * SUB : (part + 1) * SUB]
            moved = pltpu.roll(rows, shift, 1) if shift else rows
            tile = jnp.where((tile_lane >= part * NEAR) & (tile_lane < (part + 1) * NEAR), moved, tile)
        velocities.append(tile)
    down, up = by_side(velocities[0], velocities[1], parity("gy"))
    lane = iota((PACK, LANES), 1)
    half_lane = iota((PACK // 2, LANES), 1)
    halo_lane = iota((2 * SUB, LANES), 1)
    across = slots_ref.shape[0] // 2
    for index in range(across):
        away = index - gy
        first = jnp.where(away > 0, 0, CY)
        shift = CY * away + first
        source = lane + shift
        valid = (source >= 0) & (source < SPAN) & (lane + first < SPAN)
        window = jnp.where(valid, pltpu.roll(merged, (-shift) & (LANES - 1), 1), 0.0)
        slot = mine * across + index
        right = pltpu.roll(window[PACK // 2 :], HALF, 1)
        slots_ref[slot, 0 : PACK // 2, :] = jnp.where(half_lane < HALF, window[0 : PACK // 2], right)
        rest = jnp.zeros((SUB, LANES), F32)
        for group in range(PACK // SUB):
            moved = pltpu.roll(window[group * SUB : (group + 1) * SUB], HALF + 3 * group, 1)
            rest = jnp.where((tile_lane >= 3 * group) & (tile_lane < 3 * group + 3), moved, rest)
        slots_ref[slot, PACK // 2 : PACK // 2 + SUB, :] = rest
        slots_ref[slot, PACK // 2 + SUB : SLOT, :] = jnp.where(away > 0, up, down)
        shift = CY * away
        source = halo_lane + shift
        valid = (source >= 0) & (source < SPAN) & (halo_lane < SPAN)
        slot = (1 - mine) * across + index
        slots_ref[slot, 0 : 2 * SUB, :] = jnp.where(valid, pltpu.roll(halo, (-shift) & (LANES - 1), 1), 0.0)
        slots_ref[slot, 2 * SUB : SLOT, :] = jnp.zeros((SLOT - 2 * SUB, LANES), F32)


def put_velocity(row, x, node_y, velocity_ref):
    node_x = lax.axis_index("gx") * CX - 1 + x
    inside_x = (node_x > 0) & (node_x < CX * lax.axis_size("gx") - 1)
    inside_y = (node_y > 0) & (node_y < CY * lax.axis_size("gy") - 1)
    mass = jnp.maximum(jnp.broadcast_to(row[0:1], (SUB, LANES)), MASS_FLOOR)
    value = row / mass
    velocity_ref[x * SUB : (x + 1) * SUB, :] = jnp.where(inside_y & inside_x, value, 0.0)


def velocity_one(merged_ref, from_inner, from_outer, velocity_ref):
    low, high = by_side(from_inner, from_outer, parity("gy"))
    lane = iota((SUB, LANES), 1)
    node_y = lax.axis_index("gy") * CY - 1 + lane
    for x in range(DEPTHS):
        row = merged_ref[x * SUB : (x + 1) * SUB, :]
        shift = 3 * x
        row = row + jnp.where(lane < 3, pltpu.roll(low, LANES - shift, 1) if shift else low, 0.0)
        row = row + jnp.where(
            (lane >= CY) & (lane < CY + 3), pltpu.roll(high, (CY - shift) % LANES, 1), 0.0
        )
        put_velocity(row, x, node_y, velocity_ref)
    velocity_ref[DEPTHS * SUB :, :] = jnp.zeros((ROWS - DEPTHS * SUB, LANES), F32)


def velocity_two(slots_ref, merged_ref, packed_ref, velocity_ref):
    gy = lax.axis_index("gy")
    mine = lax.axis_index("gx") & 1
    odd = parity("gx")
    across = slots_ref.shape[0] // 2
    part = PACK // 2 + SUB
    from_low = jnp.zeros((part, LANES), F32)
    from_high = jnp.zeros((part, LANES), F32)
    halo = jnp.zeros((2 * SUB, LANES), F32)
    for index in range(across):
        value = slots_ref[mine * across + index, 0:part, :]
        from_low = from_low + jnp.where(index < gy, value, 0.0)
        from_high = from_high + jnp.where(index > gy, value, 0.0)
        halo = halo + slots_ref[(1 - mine) * across + index, 0 : 2 * SUB, :]
    half_lane = iota((PACK // 2, LANES), 1)
    tile_lane = iota((SUB, LANES), 1)
    total = merged_ref[...]
    for value, first in ((from_low, 0), (from_high, CY)):
        body = value[0 : PACK // 2]
        upper = jnp.where(half_lane < HALF, body, 0.0)
        lower = jnp.where(half_lane < HALF, pltpu.roll(body, HALF, 1), 0.0)
        rest = []
        for group in range(PACK // SUB):
            moved = pltpu.roll(value[PACK // 2 :], HALF - 3 * group, 1)
            rest.append(jnp.where((tile_lane >= HALF) & (tile_lane < HALF + 3), moved, 0.0))
        window = jnp.concatenate([upper, lower], axis=0) + jnp.concatenate(rest, axis=0)
        total = total + (pltpu.roll(window, first, 1) if first else window)
    packed_ref[...] = total
    last = PACK - 2 * SUB
    packed_ref[0 : 2 * SUB, :] = total[0 : 2 * SUB] + jnp.where(odd, halo, 0.0)
    packed_ref[last:PACK, :] = total[last:PACK] + jnp.where(odd, 0.0, halo)
    node_y = (gy - 1) * CY - 1 + iota((SUB, LANES), 1)
    for x in range(DEPTHS):
        put_velocity(packed_ref[KEPT * x : KEPT * x + SUB, :], x, node_y, velocity_ref)
    velocity_ref[DEPTHS * SUB :, :] = jnp.zeros((ROWS - DEPTHS * SUB, LANES), F32)


def gathered(velocity_parts, depth_of, column_of):
    masks = row_masks(depth_of)
    near = [[None] * 4 for _ in range(4)]
    columns = product(velocity_parts, jnp.concatenate(column_onehot(column_of), axis=1), NN)
    for b in range(4):
        column = columns[:, b * LANES : (b + 1) * LANES]
        for a in range(4):
            total = jnp.zeros((SUB, LANES), F32)
            for x in range(CX):
                total = jnp.where(masks[x], column[(x + a) * SUB : (x + a + 1) * SUB], total)
            near[a][b] = total
    return near


def move_points(load, store, chunks, node_of, materials, tables_ref):
    wide = lambda row: jnp.broadcast_to(row, (SUB, LANES))
    twice_shear = wide(2.0 * by_material(materials, tables_ref, 1))
    lame = wide(by_material(materials, tables_ref, 2))
    alive = wide(materials) >= 0
    for k in range(chunks):
        u, v = (load(0, k), load(1, k))
        weight_x, slope_x = stencil(u)
        weight_y, slope_y = stencil(v)
        speed, along, across = ([], [], [])
        for component in range(2):
            value = rate_x = rate_y = None
            for a in range(4):
                inner = slant = None
                for b in range(4):
                    node = wide(node_of(a, b, component))
                    term, tilt = (weight_y[b] * node, slope_y[b] * node)
                    inner = term if b == 0 else inner + term
                    slant = tilt if b == 0 else slant + tilt
                add = (weight_x[a] * inner, slope_x[a] * inner, weight_x[a] * slant)
                if a == 0:
                    value, rate_x, rate_y = add
                else:
                    value, rate_x, rate_y = (value + add[0], rate_x + add[1], rate_y + add[2])
            speed.append(value)
            along.append(rate_x)
            across.append(rate_y)
        rate_xx, rate_yy = (along[0], across[1])
        rate_xy = 0.5 * (across[0] + along[1])
        spherical = lame * (rate_xx + rate_yy)
        stress_xx = load(4, k) + TIME_STEP * (twice_shear * rate_xx + spherical)
        stress_yy = load(5, k) + TIME_STEP * (twice_shear * rate_yy + spherical)
        stress_xy = load(6, k) + TIME_STEP * twice_shear * rate_xy
        fresh = (
            jnp.clip(u + TIME_STEP * speed[0], 0.0, 1.0),
            jnp.clip(v + TIME_STEP * speed[1], 0.0, 1.0),
            speed[0],
            speed[1],
            stress_xx,
            stress_yy,
            stress_xy,
            jnp.maximum(load(7, k), -0.5 * (stress_xx + stress_yy)),
        )
        for c in range(8):
            store(c, k, jnp.where(alive, fresh[c], 0.0))


def node_getter(near):
    return lambda a, b, component: near[a][b][component + 1 : component + 2]


def emit_movers(advanced, chosen_ref, tags_ref, far_ref, near_ref):
    rows = select_rows(chosen_ref[...].astype(BF16), advanced)
    tags = tags_ref[...]
    lane = iota((SUB, LANES), 1)
    for o, ref in enumerate((far_ref, near_ref)):
        put_pieces(ref, 0, rows[o * MCAP : (o + 1) * MCAP])
        tag = pltpu.roll(tags, LANES - o * MCAP, 1) if o else tags
        ref[MSG - SUB : MSG, :] = jnp.where(lane < MCAP, tag, 0.0)


def own_and_far_depth():
    odd = lax.axis_index("gx") & 1
    return (CX - CX * odd, CX * odd)


def departures(cells, materials, lists):
    home, step_x, _ = home_and_steps()
    slots, dests, cell = (lists[0:1], lists[1:2], lists[2:3])
    moving = (dests >= 0) & (dests != home)
    low, high, far = (dests == home - 1, dests == home + 1, dests == home - step_x)
    carried = jnp.where(low | high | far, 1, 0)
    own, other = own_and_far_depth()
    depth = (cell >> 5) + jnp.where(far, other, own)
    column = (cell & (CY - 1)) + jnp.where(high, 2 * CY, jnp.where(far, CY, 0))
    entries = small_rows(jnp.where(moving, 1, 0), carried, carried * depth, carried * column)
    found = turned_to(entries, holding(slots)).astype(jnp.int32)
    gone, across = (found[0:1] > 0, found[1:2] > 0)
    sub = iota((SUB, LANES), 0)
    wide = lambda value: jnp.broadcast_to(value, (SUB, LANES))
    kept = jnp.where(
        sub == 0,
        wide(jnp.where(gone, 0, cells)),
        wide(jnp.where(gone, -1, materials)),
    )
    target = jnp.where(
        sub == 0,
        wide(jnp.where(across, found[2:3], (cells >> 5) + own)),
        jnp.where(
            sub == 1,
            wide(jnp.where(across, found[3:4], (cells & (CY - 1)) + CY)),
            wide(jnp.where(gone & ~across, -1, materials)),
        ),
    )
    return (kept, target)


def plan_depth(
    meta_ref, lists_ref,
    chosen_a_ref, chosen_b_ref, tags_a_ref, tags_b_ref, kept_a_ref, kept_b_ref, target_ref, stays_ref,
):
    home, step_x, _ = home_and_steps()
    cells, materials = (meta_ref[0:1, :], meta_ref[1:2, :])
    for first, chosen_ref, tags_ref in ((0, chosen_a_ref, tags_a_ref), (3, chosen_b_ref, tags_b_ref)):
        matched, rank = matches(lists_ref[first + 1 : first + 2, :], (home - step_x, home + step_x))
        placing = placing_rows(matched, rank, (0, 1))
        chosen = turned_to(placing, holding(lists_ref[first : first + 1, :]))
        chosen_ref[...] = chosen[0 : 2 * MCAP]
        cell = lists_ref[first + 2 : first + 3, :]
        places = turned_to(small_rows(cell >> 5, cell & (CY - 1)), placing)
        kinds = turned_to(small_rows(materials + 1), chosen.astype(BF16))
        tags_ref[...] = tag_tile(places[0:1] * float(CY) + places[1:2], kinds[0:1])
    kept, target = departures(cells, materials, lists_ref[0:3, :])
    kept_a_ref[...] = kept
    target_ref[...] = target
    kept, _ = departures(kept[0:1], kept[1:2], lists_ref[3:6, :])
    kept_b_ref[...] = kept
    stays_ref[...] = jnp.broadcast_to((kept[1:2] >= 0).astype(F32), stays_ref.shape).T


def rows_at(ref, c, k, stride):
    return ref[c * stride + k * SUB : c * stride + (k + 1) * SUB, :]


def advance_one(
    turned_ref, meta_ref, merged_ref, yo_ref, yi_ref, tables_ref, chosen_ref, tags_ref,
    fresh_ref, nodes_ref, far_message_ref, near_message_ref,
    velocity_ref,
):
    velocity_one(merged_ref, yi_ref[0:SUB, :], yo_ref[0:SUB, :], velocity_ref)
    cells, materials = (meta_ref[0:1, :], meta_ref[1:2, :])

    def store(c, k, value):
        fresh_ref[c * BLOCK + k * SUB : c * BLOCK + (k + 1) * SUB, :] = value

    near = gathered(halves(velocity_ref[...]), cells >> 5, cells & (CY - 1))
    load = lambda c, k: rows_at(turned_ref, c, k, BLOCK)
    move_points(load, store, BLOCK // SUB, node_getter(near), materials, tables_ref)
    emit_movers(fresh_ref[...].T, chosen_ref, tags_ref, far_message_ref, near_message_ref)
    for a in range(4):
        for b in range(4):
            row = 2 * (4 * a + b)
            nodes_ref[row : row + 2, :] = near[a][b][1:3]


def sums_kept(fresh_ref, target_ref, tables_ref, sums_ref, left_ref):
    depth, column, materials = (target_ref[0:1, :], target_ref[1:2, :], target_ref[2:3, :])
    load = lambda c, k: rows_at(fresh_ref, c, k, BLOCK)
    terms = weighted_terms(load, BLOCK // SUB, materials, tables_ref)
    spread_rows(terms, row_masks(depth, 2 * CX), left_ref)
    sums_ref[...] = product(halves(left_ref[...]), jnp.concatenate(column_onehot(column), axis=1), NT)


def near_cross(nodes_ref, chosen_ref, near_ref):
    near_ref[...] = product(halves(nodes_ref[...]), chosen_ref[...].astype(BF16), NT)


def packed_blocks(rows, wide_ref, turned_ref):
    count = rows.shape[0]
    fill = jnp.zeros((LANES - count, rows.shape[1]), F32)
    wide_ref[...] = jnp.concatenate([rows, fill], axis=0).T
    stride = BLOCK * count // LANES
    for c in range(8):
        total = wide_ref[c * BLOCK : c * BLOCK + stride, :]
        for group in range(1, LANES // count):
            start = c * BLOCK + group * stride
            total = total + pltpu.roll(wide_ref[start : start + stride, :], count * group, 1)
        turned_ref[c * stride : (c + 1) * stride, :] = total


def repeated(tile, count):
    while count < LANES:
        tile = tile + pltpu.roll(tile, count, 1)
        count *= 2
    return tile


def arrived_tags(from_inner, from_outer):
    low, high = by_side(from_inner, from_outer, parity("gx"))
    packed = repeated(low + pltpu.roll(high, MCAP, 1), 2 * MCAP)
    return packed.astype(jnp.int32) - (iota((SUB, LANES), 0) == 1).astype(jnp.int32)


def put_packed(ref, sums):
    ref[PACK - SUB : PACK, :] = jnp.zeros((SUB, LANES), F32)
    for x in range(DEPTHS):
        ref[KEPT * x : KEPT * (x + 1), :] = sums[x * SUB : x * SUB + KEPT]


def sums_two(
    kept_sums_ref, from_near_ref, to_far_ref, tables_ref,
    own_ref, message_ref,
    left_ref, wide_ref, turned_ref,
):
    tags = repeated(from_near_ref[MSG - SUB : MSG, :], MCAP).astype(jnp.int32)
    cells, materials = (tags[0:1], tags[1:2] - 1)
    packed_blocks(joined(from_near_ref[0 : MSG - SUB, :]), wide_ref, turned_ref)
    stride = turned_ref.shape[0] // 8
    load = lambda c, k: rows_at(turned_ref, c, k, stride)
    terms = weighted_terms(load, stride // SUB, materials, tables_ref)
    spread_rows(terms, row_masks(cells >> 5), left_ref)
    onehots = jnp.concatenate(column_onehot((cells & (CY - 1)) + CY), axis=1)
    part = product(halves(left_ref[...]), onehots, NT)
    odd = parity("gx")
    first, second = (kept_sums_ref[0:BRICK, :], kept_sums_ref[CX * SUB : CX * SUB + BRICK, :])
    put_packed(own_ref, jnp.where(odd, first, second) + part[0:BRICK])
    far = jnp.where(odd, second, first)
    low = far[0:HALO] + jnp.where(odd, part[TOP : TOP + HALO], 0.0)
    high = far[TOP : TOP + HALO] + jnp.where(odd, 0.0, part[0:HALO])
    put_packed(message_ref, jnp.concatenate([low, far[HALO:TOP], high], axis=0))
    message_ref[PACK : PACK + MSG, :] = to_far_ref[...]


def arrange_depth(from_near_ref, from_far_ref, turned_ref, new_meta_ref, wide_ref):
    rows, tags = (slice(0, MSG - SUB), slice(MSG - SUB, MSG))
    far = from_far_ref[PACK : PACK + MSG, :]
    new_meta_ref[...] = arrived_tags(from_near_ref[tags, :], far[tags])
    low, high = by_side(from_near_ref[rows, :], far[rows], parity("gx"))
    packed_blocks(jnp.concatenate([joined(low), joined(high)], axis=0), wide_ref, turned_ref)


def arrange_cross(yo_ref, yi_ref, cross_ref, tags_ref, wide_ref):
    low, high = by_side(yi_ref[...], yo_ref[...], parity("gy"))
    tags_ref[...] = low[SUB : 2 * SUB] + pltpu.roll(high[SUB : 2 * SUB], 2 * MCAP, 1)
    rows = jnp.concatenate([joined(low[2 * SUB :]), joined(high[2 * SUB :])], axis=0)
    packed_blocks(rows, wide_ref, cross_ref)


def advance_two(
    kept_ref, meta_ref, slots_ref, merged_ref, tables_ref, chosen_ref, tags_ref,
    rows_ref, velocity_ref, far_message_ref, near_message_ref,
    packed_ref, fresh_ref,
):
    velocity_two(slots_ref, merged_ref, packed_ref, velocity_ref)
    cells, materials = (meta_ref[0:1, :], meta_ref[1:2, :])

    def store(c, k, value):
        fresh_ref[c * BLOCK + k * SUB : c * BLOCK + (k + 1) * SUB, :] = value

    near = gathered(halves(velocity_ref[...]), cells >> 5, (cells & (CY - 1)) + CY)
    load = lambda c, k: rows_at(kept_ref, c, k, BLOCK)
    move_points(load, store, BLOCK // SUB, node_getter(near), materials, tables_ref)
    advanced = fresh_ref[...].T
    rows_ref[...] = advanced
    emit_movers(advanced, chosen_ref, tags_ref, far_message_ref, near_message_ref)


def near_movers(slots_ref, index):
    lane = iota((SUB, LANES), 1)
    tile = slots_ref[index, PACK // 2 + SUB : SLOT, :]
    parts = []
    for part in range(NEAR // SUB):
        moved = pltpu.roll(tile, LANES - part * NEAR, 1) if part else tile
        parts.append(jnp.where(lane < 2 * MCAP, moved, 0.0))
    return jnp.concatenate(parts, axis=0)


def settle(
    advanced_ref, stays_ref, velocity_ref, turned_ref, new_meta_ref, tables_ref, slots_ref, cross_ref, tags_ref,
    rows_ref, tail_ref,
    wide_ref, middle_ref, out_ref, small_ref,
):
    stays = stays_ref[...] > 0.5
    for piece in range(PIECES):
        columns = slice(piece * LANES, (piece + 1) * LANES)
        rows_ref[0:LANES, columns] = jnp.where(stays, advanced_ref[:, columns], 0.0)
    parts = halves(velocity_ref[...])

    stride = turned_ref.shape[0] // 8
    cells, materials = (new_meta_ref[0:1, :], new_meta_ref[1:2, :])

    def store_small(c, k, value):
        small_ref[c * stride + k * SUB : c * stride + (k + 1) * SUB, :] = value

    load = lambda c, k: rows_at(turned_ref, c, k, stride)
    near = gathered(parts, cells >> 5, (cells & (CY - 1)) + CY)
    move_points(load, store_small, stride // SUB, node_getter(near), materials, tables_ref)

    gy = lax.axis_index("gy")
    lane = iota((SUB, LANES), 1)
    tags = tags_ref[...]
    tail = jnp.zeros((SUB, LANES), F32)
    for start, shift in ((32, 32), (48, 16), (96, 80), (112, 64)):
        tail = jnp.where((lane >= start) & (lane < start + MCAP), pltpu.roll(tags, shift, 1), tail)
    materials_row = (iota((SUB, LANES), 0) == 1).astype(jnp.int32)
    tail = tail.astype(jnp.int32) - materials_row
    tail_ref[...] = jnp.where(lane < 2 * MCAP, new_meta_ref[...], tail)
    tags = repeated(tags, 4 * MCAP).astype(jnp.int32) - materials_row

    across = slots_ref.shape[0] // 2
    column = (lax.axis_index("gx") & 1) * across
    below = near_movers(slots_ref, column + jnp.maximum(gy - 1, 0))
    above = near_movers(slots_ref, column + jnp.minimum(gy + 1, across - 1))
    nodes = below + pltpu.roll(above, 2 * MCAP, 1)
    nodes = nodes + pltpu.roll(nodes, 4 * MCAP, 1)

    def node_of(a, b, component):
        row = 2 * (4 * a + b) + component
        return nodes[row : row + 1]

    half = cross_ref.shape[0] // 8
    kinds = tags[1:2]

    def store_middle(c, k, value):
        middle_ref[c * half + k * SUB : c * half + (k + 1) * SUB, :] = value

    move_points(lambda c, k: rows_at(cross_ref, c, k, half), store_middle, half // SUB, node_of, kinds, tables_ref)
    row_lane = lane[0:1]
    second = (row_lane & MCAP) != 0
    cell = jnp.where(second, tags[2:3], tags[0:1])
    side = jnp.where((row_lane & (2 * MCAP)) != 0, 2 * CY, 0)
    near = gathered(parts, cell >> 5, (cell & (CY - 1)) + jnp.where(second, side, CY))

    def store_out(c, k, value):
        out_ref[c * half + k * SUB : c * half + (k + 1) * SUB, :] = value

    move_points(
        lambda c, k: rows_at(middle_ref, c, k, half), store_out, half // SUB, node_getter(near), kinds, tables_ref
    )
    crossed = lane < 4 * MCAP
    for c in range(8):
        for k in range(BLOCK // SUB):
            group, rest = divmod(k * SUB, half)
            first = out_ref[c * half + rest : c * half + rest + SUB, :]
            first = pltpu.roll(first, LANES - 4 * MCAP * group, 1) if group else first
            group, rest = divmod(k * SUB, stride)
            second = small_ref[c * stride + rest : c * stride + rest + SUB, :]
            second = pltpu.roll(second, (4 * MCAP - 2 * MCAP * group) % LANES, 1)
            wide_ref[c * BLOCK + k * SUB : c * BLOCK + (k + 1) * SUB, :] = jnp.where(crossed, first, second)
    last = wide_ref[...].T
    rows_ref[LANES : LANES + 2 * MCAP, :] = last[4 * MCAP : 6 * MCAP]
    for group, index in enumerate((2, 6, 3, 7)):
        start = LANES + index * MCAP
        rows_ref[start : start + MCAP, :] = last[group * MCAP : (group + 1) * MCAP]


def assemble(
    part_ref, old_meta_ref, tail_ref, xo_ref, xi_ref,
    points_ref, cells_ref, mats_ref,
    tags_ref, rows_ref, sems,
):
    base = points_ref.shape[0] - 4 * MCAP
    odd = lax.axis_index("gx") & 1
    copies = []
    for index, (first, last) in enumerate(((0, base), (base + 2 * MCAP, base + 4 * MCAP))):
        copies.append(pltpu.make_async_copy(part_ref.at[first:last], points_ref.at[first:last], sems.at[index]))
        copies[-1].start()
    for index, (ref, region) in enumerate(((xo_ref, odd), (xi_ref, 1 - odd))):
        start = pl.multiple_of(base + region * MCAP, MCAP)
        rows_ref[index] = joined(ref[0 : MSG - SUB, :])
        copies.append(
            pltpu.make_async_copy(rows_ref.at[index], points_ref.at[pl.ds(start, MCAP), :], sems.at[2 + index])
        )
        copies[-1].start()
    arrived = arrived_tags(xi_ref[MSG - SUB : MSG, :], xo_ref[MSG - SUB : MSG, :])
    lane = iota((1, LANES), 1)
    here = (lane >= 4 * MCAP) & (lane < 6 * MCAP)
    for row, ref in ((0, cells_ref), (1, mats_ref)):
        tags_ref[row, 0:1, :] = old_meta_ref[row : row + 1, :]
        tags_ref[row, 1:2, :] = jnp.where(here, arrived[row : row + 1], tail_ref[row : row + 1, :])
        copies.append(pltpu.make_async_copy(tags_ref.at[row], ref, sems.at[4 + row]))
        copies[-1].start()
    for copy in copies:
        copy.wait()


def shards(
    points,
    block_cell,
    block_mat,
    density,
    shear_modulus,
    lame_modulus,
    mig_slot_a,
    mig_dest_a,
    mig_cell_a,
    mig_slot_b,
    mig_dest_b,
    mig_cell_b,
):
    wide = 8 * BLOCK
    I32 = jnp.int32
    row = lambda value: value.reshape(1, -1)
    cells, mats = (row(block_cell), row(block_mat))
    list_a = (row(mig_slot_a), row(mig_dest_a), row(mig_cell_a))
    list_b = (row(mig_slot_b), row(mig_dest_b), row(mig_cell_b))

    halo = ((HALO, LANES), F32)
    tile = ((SUB, LANES), F32)
    tags = ((SUB, LANES), I32)
    grid = ((ROWS, LANES), F32)
    message = ((MSG, LANES), F32)
    cross_message = ((CROSS_MSG, LANES), F32)
    turned_form = ((wide, LANES), F32)
    half_form = ((wide // 2, LANES), F32)
    quarter_form = ((wide // 4, LANES), F32)
    near_form = ((NEAR, LANES), F32)
    slots_form = ((2 * lax.axis_size("gy"), SLOT, LANES), F32)
    scratch = lambda form: pltpu.VMEM(*form)
    left = pltpu.VMEM((ROWS, 4 * LANES), F32)

    def along_depth(far, near):
        return (swap(far, "gx", 1), swap(near, "gx", 0))

    (nothing,) = call(blank, (tags,), (), (), flops=1 << 28, bytes_accessed=1 << 10)
    meta, lists, tables = call(
        prepare,
        (tags, tags, ((3 * NMAT, LANES), F32)),
        (),
        (IN_VMEM,) * 12,
        nothing, cells, mats, row(density), row(shear_modulus), row(lame_modulus), *list_a, *list_b,
    )
    turned, terms = call(
        terms_one, (turned_form, ((16 * SUB, LANES), F32)), (), (IN_VMEM,) * 2, points, meta
    )
    sums, inner, outer = call(sums_one, (grid, halo, halo), (left,), (IN_VMEM,) * 3, terms, meta, tables)
    picked, picked_tags, chosen = call(
        pick_cross,
        (((4 * MCAP, wide), F32), tile, ((LANES, LANES), F32)),
        (),
        (IN_VMEM,) * 3,
        points, meta, lists,
    )
    merged, inner, outer = call(
        merge_one,
        (grid, cross_message, cross_message),
        (),
        (IN_VMEM,) * 5,
        sums, *along_depth(outer, inner), picked, picked_tags,
    )
    cross_far, cross_near = (swap(outer, "gy", 1), swap(inner, "gy", 0))
    chosen_form = ((2 * MCAP, LANES), F32)
    chosen_a, chosen_b, tags_a, tags_b, kept_a, kept_b, target, stays = call(
        plan_depth,
        (chosen_form, chosen_form, tile, tile, tags, tags, tags, ((LANES, LANES), F32)),
        (),
        (IN_VMEM,) * 2,
        meta, lists,
    )
    fresh, nodes, far, near = call(
        advance_one,
        (turned_form, near_form, message, message),
        (scratch(grid),),
        (IN_VMEM,) * 8,
        turned, meta, merged, cross_far, cross_near, tables, chosen_a, tags_a,
    )
    from_near = swap(near, "gx", 0)
    pair_form = ((PAIR, LANES), F32)
    pair_left = pltpu.VMEM((PAIR, 4 * LANES), F32)
    (kept_sums,) = call(sums_kept, (pair_form,), (pair_left,), (IN_VMEM,) * 3, fresh, target, tables)
    (near_nodes,) = call(near_cross, (near_form,), (), (IN_VMEM,) * 2, nodes, chosen)
    packed_form = ((PACK, LANES), F32)
    own, far_message = call(
        sums_two,
        (packed_form, ((PACK + MSG, LANES), F32)),
        (left, scratch(turned_form), pltpu.VMEM((wide // 8, LANES), F32)),
        (IN_VMEM,) * 4,
        kept_sums, from_near, far, tables,
    )
    from_far = swap(far_message, "gx", 1)
    cross, cross_tags = call(
        arrange_cross, (half_form, tile), (scratch(turned_form),), (IN_VMEM,) * 2, cross_far, cross_near
    )
    merged, slots = call(
        merge_far, (packed_form, slots_form), (), (IN_VMEM,) * 4, own, from_far, near_nodes, cross_tags
    )
    turned, new_meta = call(
        arrange_depth, (quarter_form, tags), (scratch(turned_form),), (IN_VMEM,) * 2, from_near, from_far
    )
    slots = lax.all_to_all(slots, ("gx", "gy"), 0, 0, axis_index_groups=chip_columns())
    advanced, velocity, far, near = call(
        advance_two,
        (((LANES, wide), F32), grid, message, message),
        (scratch(packed_form), scratch(turned_form)),
        (IN_VMEM,) * 7,
        fresh, kept_a, slots, merged, tables, chosen_b, tags_b,
    )
    arrived = along_depth(far, near)
    final_form = ((2 * LANES, wide), F32)
    part, tail = call(
        settle,
        (final_form, tags),
        (
            scratch(turned_form),
            scratch(half_form),
            scratch(half_form),
            scratch(quarter_form),
        ),
        (IN_VMEM,) * 9,
        advanced, stays, velocity, turned, new_meta, tables, slots, cross, cross_tags,
    )
    final_points, final_cells, final_mats = call(
        assemble,
        (final_form, ((2, LANES), I32), ((2, LANES), I32)),
        (pltpu.VMEM((2, 2, LANES), I32), pltpu.VMEM((2, MCAP, wide), F32), pltpu.SemaphoreType.DMA((6,))),
        (IN_VMEM,) * 5,
        part, kept_b, tail, *arrived,
        out_specs=(IN_HBM,) * 3,
    )
    return (final_points, final_cells.reshape(-1), final_mats.reshape(-1))


def solution(mesh):
    split = P(("gx", "gy"))
    rows = P(("gx", "gy"), None)
    return jax.shard_map(
        shards,
        mesh=mesh,
        in_specs=(rows, split, split, P(), P(), P()) + (split,) * 6,
        out_specs=(rows, split, split),
        check_vma=False,
    )
```

```python
import jax
import jax.numpy as jnp
from jax import lax
from jax.experimental import pallas as pl
from jax.experimental.pallas import tpu as pltpu
from jax.sharding import PartitionSpec as P

CX = 16
CY = 32
BLOCK = 64
NMAT = 8
MCAP = 16
LANES = 128
SUB = 8
ROWS = 160
HALO = 24
TOP = CX * SUB
PIECES = 8 * BLOCK // LANES
MSG = PIECES * MCAP + SUB
DEPTHS = CX + 3
BRICK = DEPTHS * SUB
PAIR = (2 * CX + 4) * SUB
KEPT = 3
PACK = 64
NEAR = 32
HALF = LANES // 2
REACH = range(-3, 4)
SLOT = PACK // 2 + 2 * SUB
CROSS_MSG = 2 * SUB + PIECES * 2 * MCAP
SPAN = 3 * CY + 3

TIME_STEP = 0.2
MASS_FLOOR = 0.25
VOLUME = 1.0 / BLOCK
VMEM_LIMIT = 12 * 1024 * 1024

IN_VMEM = pl.BlockSpec(memory_space=pltpu.VMEM)
IN_HBM = pl.BlockSpec(memory_space=pltpu.HBM)
F32 = jnp.float32
BF16 = jnp.bfloat16
NN = (((1,), (0,)), ((), ()))
NT = (((1,), (1,)), ((), ()))


def call(kernel, outs, scratch, in_specs, *operands, out_specs=None, flops=1 << 22, bytes_accessed=1 << 19):
    return pl.pallas_call(
        kernel,
        out_shape=tuple(jax.ShapeDtypeStruct(shape, dtype) for shape, dtype in outs),
        in_specs=in_specs,
        out_specs=out_specs or tuple(IN_VMEM for _ in outs),
        scratch_shapes=scratch,
        compiler_params=pltpu.CompilerParams(vmem_limit_bytes=VMEM_LIMIT),
        cost_estimate=pl.CostEstimate(flops=flops, bytes_accessed=bytes_accessed, transcendentals=0),
    )(*operands)


def swap(value, axis, first):
    count = lax.axis_size(axis)
    pairs = []
    for low in range(first, count - 1, 2):
        pairs += [(low, low + 1), (low + 1, low)]
    return lax.ppermute(value, axis, pairs)


def chip_columns():
    down, across = (lax.axis_size("gx"), lax.axis_size("gy"))
    return [list(range(first * across, (first + 2) * across)) for first in range(0, down, 2)]


def iota(shape, dim):
    return lax.broadcasted_iota(jnp.int32, shape, dim)


def halves(value):
    high = value.astype(BF16)
    return (high, (value - high.astype(F32)).astype(BF16))


def product(parts, onehot, dims):
    rows = parts[0].shape[0]
    stacked = lax.dot_general(jnp.concatenate(parts, axis=0), onehot, dims, preferred_element_type=F32)
    total = stacked[0:rows]
    for index in range(1, len(parts)):
        total = total + stacked[index * rows : (index + 1) * rows]
    return total


def select_rows(onehot, rows):
    high, low = halves(rows)
    twice = jnp.concatenate([onehot, onehot], axis=1)
    return lax.dot_general(twice, jnp.concatenate([high, low], axis=0), NN, preferred_element_type=F32)


def stencil(u):
    p = jnp.maximum(0.25 - u, 0.0)
    q = jnp.maximum(u - 0.75, 0.0)
    p2 = p * p
    q2 = q * q
    weight = (p2, (1.0 - u) - 2.0 * p2 + q2, u + p2 - 2.0 * q2, q2)
    slope = (-2.0 * p, 4.0 * p + 2.0 * q - 1.0, 1.0 - 2.0 * p - 4.0 * q, 2.0 * q)
    return (weight, slope)


def by_material(materials, tables_ref, which):
    value = jnp.zeros(materials.shape, F32)
    for index in range(NMAT):
        row = which * NMAT + index
        value = jnp.where(materials == index, tables_ref[row : row + 1, :], value)
    return value


def column_onehot(column_of):
    first = jnp.broadcast_to(column_of, (LANES, LANES))
    column = iota((LANES, LANES), 0)
    return [(column == first + b).astype(F32).astype(BF16) for b in range(4)]


def row_masks(depth_of, count=CX):
    depth = jnp.broadcast_to(depth_of, (SUB, LANES))
    return [depth == index for index in range(count)]


def scaled(terms, materials, tables_ref):
    sub = iota((SUB, LANES), 0)
    wide = lambda row: jnp.broadcast_to(row, (SUB, LANES))
    mass = jnp.where((sub < KEPT) & (wide(materials) >= 0), wide(by_material(materials, tables_ref, 0) * VOLUME), 0.0)
    push = jnp.where((sub > 0) & (sub < KEPT) & (wide(materials) >= 0), -VOLUME * TIME_STEP, 0.0)
    return [[term * mass + pltpu.roll(term, SUB - 2, 0) * push for term in row] for row in terms]


def weighted_terms(load, chunks, materials, tables_ref):
    sub = iota((SUB, LANES), 0)
    wide = lambda row: jnp.broadcast_to(row, (SUB, LANES))
    rho = wide(by_material(materials, tables_ref, 0))
    scale = jnp.where(sub == 0, rho * VOLUME, VOLUME)
    scale = jnp.where((sub < KEPT) & (wide(materials) >= 0), scale, 0.0)
    stencils = [(stencil(load(0, k)), stencil(load(1, k))) for k in range(chunks)]
    points = [
        (rho * load(2, k), rho * load(3, k)) + tuple(-TIME_STEP * load(c, k) for c in (4, 5, 6))
        for k in range(chunks)
    ]
    terms = [[None] * 4 for _ in range(4)]
    for b in range(4):
        acc = [[None] * KEPT for _ in range(4)]
        for k in range(chunks):
            (weight_x, slope_x), (weight_y, slope_y) = stencils[k]
            wy, dy = weight_y[b], slope_y[b]
            px, py, sxx, syy, sxy = points[k]
            g1, h1 = (wy * px + dy * sxy, wy * sxx)
            g2, h2 = (wy * py + dy * syy, wy * sxy)
            for a in range(4):
                wx, dx = weight_x[a], slope_x[a]
                new = (wx * wy, wx * g1 + dx * h1, wx * g2 + dx * h2)
                acc[a] = [n if o is None else o + n for o, n in zip(acc[a], new)]
        for a in range(4):
            packed = jnp.zeros((SUB, LANES), F32)
            for q in range(KEPT):
                total = jnp.sum(acc[a][q], axis=0, keepdims=True)
                packed = jnp.where(sub == q, jnp.broadcast_to(total, (SUB, LANES)), packed)
            terms[a][b] = packed * scale
    return terms


def node_terms(load, chunks):
    sub = iota((SUB, LANES), 0)
    stencils = [(stencil(load(0, k)), stencil(load(1, k))) for k in range(chunks)]
    terms = [[None] * 4 for _ in range(4)]
    for b in range(4):
        acc = [[None] * 5 for _ in range(4)]
        for k in range(chunks):
            (weight_x, slope_x), (weight_y, slope_y) = stencils[k]
            wy, dy = weight_y[b], slope_y[b]
            sxy = load(6, k)
            y1 = wy * load(2, k)
            y2 = wy * load(3, k)
            y3 = wy * load(4, k)
            y4 = wy * sxy
            y5 = dy * sxy
            y6 = dy * load(5, k)
            for a in range(4):
                wx, dx = weight_x[a], slope_x[a]
                new = (wx * wy, wx * y1, wx * y2, dx * y3 + wx * y5, dx * y4 + wx * y6)
                acc[a] = [n if o is None else o + n for o, n in zip(acc[a], new)]
        for a in range(4):
            packed = jnp.zeros((SUB, LANES), F32)
            for q in range(5):
                total = jnp.sum(acc[a][q], axis=0, keepdims=True)
                packed = jnp.where(sub == q, jnp.broadcast_to(total, (SUB, LANES)), packed)
            terms[a][b] = packed
    return terms


def spread_rows(terms, masks, left_ref):
    zero = jnp.zeros((SUB, LANES), F32)
    for b in range(4):
        for x in range(left_ref.shape[0] // SUB):
            total = zero
            for a in range(4):
                if 0 <= x - a < len(masks):
                    total = total + jnp.where(masks[x - a], terms[a][b], zero)
            left_ref[x * SUB : (x + 1) * SUB, b * LANES : (b + 1) * LANES] = total


def parity(axis):
    return (lax.axis_index(axis) & 1) == 1


def spread_table(table_ref, rows_ref, first):
    table = table_ref[...]
    for index in range(NMAT):
        row = first + index
        rows_ref[row : row + 1, :] = jnp.broadcast_to(table[:, index : index + 1], (1, LANES))


def terms_one(points_ref, meta_ref, turned_ref, terms_ref):
    del meta_ref
    turned_ref[...] = points_ref[...].T
    load = lambda c, k: rows_at(turned_ref, c, k, BLOCK)
    terms = node_terms(load, BLOCK // SUB)
    for a in range(4):
        for b in range(4):
            row = (4 * a + b) * SUB
            terms_ref[row : row + SUB, :] = terms[a][b]


def blank(blank_ref):
    blank_ref[...] = jnp.zeros_like(blank_ref)


def prepare(
    blank_ref, cells_ref, mats_ref, density_ref, shear_ref, lame_ref,
    slot_a_ref, dest_a_ref, cell_a_ref, slot_b_ref, dest_b_ref, cell_b_ref,
    meta_ref, lists_ref, tables_ref,
):
    for which, table_ref in enumerate((density_ref, shear_ref, lame_ref)):
        spread_table(table_ref, tables_ref, which * NMAT)
    lists_ref[...] = blank_ref[...]
    for index, ref in enumerate((slot_a_ref, dest_a_ref, cell_a_ref, slot_b_ref, dest_b_ref, cell_b_ref)):
        entries = ref[...]
        rest = jnp.full((1, LANES - entries.shape[1]), -1, jnp.int32)
        lists_ref[index : index + 1, :] = jnp.concatenate([entries, rest], axis=1)
    meta_ref[...] = blank_ref[...]
    meta_ref[0:1, :] = cells_ref[...]
    meta_ref[1:2, :] = mats_ref[...]


def sums_one(terms_ref, meta_ref, tables_ref, sums_ref, inner_ref, outer_ref, left_ref):
    cells, materials = (meta_ref[0:1, :], meta_ref[1:2, :])
    terms = [[terms_ref[(4 * a + b) * SUB : (4 * a + b + 1) * SUB, :] for b in range(4)] for a in range(4)]
    terms = scaled(terms, materials, tables_ref)
    spread_rows(terms, row_masks(cells >> 5), left_ref)
    sums = product(halves(left_ref[...]), jnp.concatenate(column_onehot(cells & (CY - 1)), axis=1), NT)
    sums_ref[...] = sums
    to_inner, to_outer = by_side(sums[0:HALO], sums[TOP : TOP + HALO], parity("gx"))
    inner_ref[...] = to_inner
    outer_ref[...] = to_outer


def by_side(inner, outer, odd):
    return (jnp.where(odd, inner, outer), jnp.where(odd, outer, inner))


def put_pieces(ref, first, rows):
    count = rows.shape[0]
    for piece in range(PIECES):
        start = first + piece * count
        ref[start : start + count, :] = rows[:, piece * LANES : (piece + 1) * LANES]


def joined(pieces):
    count = pieces.shape[0] // PIECES
    return jnp.concatenate([pieces[piece * count : (piece + 1) * count] for piece in range(PIECES)], axis=1)


def matches(dests, targets):
    dest = jnp.broadcast_to(dests, (2 * SUB, LANES))
    sub = iota(dest.shape, 0)
    matched = jnp.zeros(dest.shape, F32)
    for o, target in enumerate(targets):
        matched = jnp.where((sub == o) & (dest == target), 1.0, matched)
    square = (LANES, LANES)
    earlier = (iota(square, 0) < iota(square, 1)).astype(F32).astype(BF16)
    rank = lax.dot_general(matched.astype(BF16), earlier, NN, preferred_element_type=F32)
    return (matched, rank)


def placing_rows(matched, rank, groups):
    blank = jnp.zeros((MCAP, LANES), F32)
    place = iota((MCAP, LANES), 0).astype(F32)
    rows = []
    for o in groups:
        if o is None:
            rows.append(blank)
            continue
        hit = jnp.broadcast_to(rank[o : o + 1], blank.shape) == place
        rows.append(jnp.where(hit, jnp.broadcast_to(matched[o : o + 1], blank.shape), 0.0))
    rows += [blank] * (LANES // MCAP - len(groups))
    return jnp.concatenate(rows, axis=0).astype(BF16)


def holding(slots):
    square = (LANES, LANES)
    return (iota(square, 0) == jnp.broadcast_to(slots, square)).astype(F32).astype(BF16)


def small_rows(*rows):
    sub = iota((2 * SUB, LANES), 0)
    value = jnp.zeros((2 * SUB, LANES), F32)
    for index, row in enumerate(rows):
        value = jnp.where(sub == index, jnp.broadcast_to(row.astype(F32), value.shape), value)
    return value.astype(BF16)


def turned_to(small, onehot):
    return lax.dot_general(small, onehot, NT, preferred_element_type=F32)


def tag_tile(*rows):
    sub = iota((SUB, LANES), 0)
    tile = jnp.zeros((SUB, LANES), F32)
    for index, row in enumerate(rows):
        tile = jnp.where(sub == index, jnp.broadcast_to(row, tile.shape), tile)
    return tile


def home_and_steps():
    across = lax.axis_size("gy")
    gx, gy = (lax.axis_index("gx"), lax.axis_index("gy"))
    return (gx * across + gy, across - 2 * across * (gx & 1), 1 - 2 * (gy & 1))


def pick_cross(points_ref, meta_ref, lists_ref, rows_ref, tags_ref, chosen_ref):
    home, _, step_y = home_and_steps()
    chosen = places = None
    for first, groups in ((0, (0, None, 1, None)), (3, (None, 0, None, 1))):
        matched, rank = matches(lists_ref[first + 1 : first + 2, :], (home + step_y, home - step_y))
        placing = placing_rows(matched, rank, groups)
        part = turned_to(placing, holding(lists_ref[first : first + 1, :]))
        cell = lists_ref[first + 2 : first + 3, :]
        place = turned_to(small_rows(cell >> 5, cell & (CY - 1)), placing)
        chosen = part if chosen is None else chosen + part
        places = place if places is None else places + place
    chosen_ref[...] = chosen
    onehot = chosen.astype(BF16)
    cells, materials = (meta_ref[0:1, :], meta_ref[1:2, :])
    found = turned_to(small_rows(materials + 1, cells >> 5, cells & (CY - 1)), onehot)
    tags_ref[...] = tag_tile(
        places[0:1] * float(CY) + places[1:2], found[0:1], found[1:2] * float(CY) + found[2:3]
    )
    rows_ref[...] = select_rows(onehot[0 : 4 * MCAP], points_ref[...])


def merge_rows(sums_ref, from_outer_ref, from_inner_ref, merged_ref):
    from_low, from_high = by_side(from_inner_ref[...], from_outer_ref[...], parity("gx"))
    merged_ref[...] = sums_ref[...]
    merged_ref[0:HALO] = sums_ref[0:HALO] + from_low
    merged_ref[TOP : TOP + HALO] = sums_ref[TOP : TOP + HALO] + from_high


def merge_one(
    sums_ref, from_outer_ref, from_inner_ref, rows_ref, tags_ref,
    merged_ref, inner_ref, outer_ref,
):
    merge_rows(sums_ref, from_outer_ref, from_inner_ref, merged_ref)
    lane = iota((SUB, LANES), 1)
    low = jnp.zeros((SUB, LANES), F32)
    high = jnp.zeros((SUB, LANES), F32)
    for x in range(DEPTHS):
        row = merged_ref[x * SUB : (x + 1) * SUB, :]
        here = (lane >= 3 * x) & (lane < 3 * x + 3)
        shift = 3 * x
        low = jnp.where(here, pltpu.roll(row, shift, 1) if shift else row, low)
        high = jnp.where(here, pltpu.roll(row, (shift - CY) % LANES, 1), high)
    to_inner, to_outer = by_side(low, high, parity("gy"))
    movers = 2 * MCAP
    tags = tags_ref[...]
    for ref, halo, tag, first in (
        (inner_ref, to_inner, tags, 0),
        (outer_ref, to_outer, pltpu.roll(tags, LANES - movers, 1), movers),
    ):
        ref[0:SUB, :] = halo
        ref[SUB : 2 * SUB, :] = jnp.where(lane < movers, tag, 0.0)
        put_pieces(ref, 2 * SUB, rows_ref[first : first + movers, :])


def merge_far(own_ref, from_far_ref, near_ref, cross_tags_ref, merged_ref, slots_ref):
    del cross_tags_ref
    merged = own_ref[...] + from_far_ref[0:PACK, :]
    merged_ref[...] = merged
    gy = lax.axis_index("gy")
    mine = lax.axis_index("gx") & 1
    low = jnp.where(iota((2 * SUB, LANES), 0) < 3 * KEPT, merged[0 : 2 * SUB], 0.0)
    halo = jnp.where(parity("gx"), low, merged[PACK - 2 * SUB : PACK])
    near = near_ref[...]
    tile_lane = iota((SUB, LANES), 1)
    velocities = []
    for start in (0, HALF // 2):
        tile = jnp.zeros((SUB, LANES), F32)
        for part in range(NEAR // SUB):
            shift = (part * NEAR - start) % LANES
            rows = near[part * SUB : (part + 1) * SUB]
            moved = pltpu.roll(rows, shift, 1) if shift else rows
            tile = jnp.where((tile_lane >= part * NEAR) & (tile_lane < (part + 1) * NEAR), moved, tile)
        velocities.append(tile)
    down, up = by_side(velocities[0], velocities[1], parity("gy"))
    lane = iota((PACK, LANES), 1)
    half_lane = iota((PACK // 2, LANES), 1)
    halo_lane = iota((2 * SUB, LANES), 1)
    across = slots_ref.shape[0] // 2
    unread = mine * across + gy
    for away in REACH:
        index = gy + away
        there = (index >= 0) & (index < across)
        shift = CY * away
        source = halo_lane + shift
        valid = (source >= 0) & (source < SPAN) & (halo_lane < SPAN)
        moved = pltpu.roll(halo, (-shift) % LANES, 1) if away else halo
        slot = jnp.where(there, (1 - mine) * across + index, unread)
        slots_ref[slot, 0 : 2 * SUB, :] = jnp.where(valid, moved, 0.0)
        if away == 0:
            continue
        slot = jnp.where(there, mine * across + index, unread)
        first = 0 if away > 0 else CY
        shift += first
        source = lane + shift
        valid = (source >= 0) & (source < SPAN) & (lane + first < SPAN)
        moved = pltpu.roll(merged, (-shift) % LANES, 1) if shift else merged
        window = jnp.where(valid, moved, 0.0)
        right = pltpu.roll(window[PACK // 2 :], HALF, 1)
        slots_ref[slot, 0 : PACK // 2, :] = jnp.where(half_lane < HALF, window[0 : PACK // 2], right)
        rest = jnp.zeros((SUB, LANES), F32)
        if away not in (2, 3):
            for group in range(PACK // SUB):
                moved = pltpu.roll(window[group * SUB : (group + 1) * SUB], HALF + 3 * group, 1)
                rest = jnp.where((tile_lane >= 3 * group) & (tile_lane < 3 * group + 3), moved, rest)
        slots_ref[slot, PACK // 2 : PACK // 2 + SUB, :] = rest
        slots_ref[slot, PACK // 2 + SUB : SLOT, :] = up if away > 0 else down


def put_velocity(row, x, node_y, velocity_ref):
    node_x = lax.axis_index("gx") * CX - 1 + x
    inside_x = (node_x > 0) & (node_x < CX * lax.axis_size("gx") - 1)
    inside_y = (node_y > 0) & (node_y < CY * lax.axis_size("gy") - 1)
    mass = jnp.maximum(jnp.broadcast_to(row[0:1], (SUB, LANES)), MASS_FLOOR)
    value = row / mass
    velocity_ref[x * SUB : (x + 1) * SUB, :] = jnp.where(inside_y & inside_x, value, 0.0)


def velocity_one(merged_ref, from_inner, from_outer, velocity_ref):
    low, high = by_side(from_inner, from_outer, parity("gy"))
    lane = iota((SUB, LANES), 1)
    node_y = lax.axis_index("gy") * CY - 1 + lane
    for x in range(DEPTHS):
        row = merged_ref[x * SUB : (x + 1) * SUB, :]
        shift = 3 * x
        row = row + jnp.where(lane < 3, pltpu.roll(low, LANES - shift, 1) if shift else low, 0.0)
        row = row + jnp.where(
            (lane >= CY) & (lane < CY + 3), pltpu.roll(high, (CY - shift) % LANES, 1), 0.0
        )
        put_velocity(row, x, node_y, velocity_ref)
    velocity_ref[DEPTHS * SUB :, :] = jnp.zeros((ROWS - DEPTHS * SUB, LANES), F32)


def velocity_two(slots_ref, merged_ref, packed_ref, velocity_ref):
    gy = lax.axis_index("gy")
    mine = lax.axis_index("gx") & 1
    odd = parity("gx")
    across = slots_ref.shape[0] // 2
    part = PACK // 2 + SUB
    from_low = jnp.zeros((part, LANES), F32)
    from_high = jnp.zeros((part, LANES), F32)
    halo = jnp.zeros((2 * SUB, LANES), F32)
    for away in REACH:
        index = gy + away
        there = (index >= 0) & (index < across)
        index = jnp.clip(index, 0, across - 1)
        halo = halo + jnp.where(there, slots_ref[(1 - mine) * across + index, 0 : 2 * SUB, :], 0.0)
        if away == 0:
            continue
        value = jnp.where(there, slots_ref[mine * across + index, 0:part, :], 0.0)
        if away < 0:
            from_low = from_low + value
        else:
            from_high = from_high + value
    half_lane = iota((PACK // 2, LANES), 1)
    tile_lane = iota((SUB, LANES), 1)
    total = merged_ref[...]
    for value, first in ((from_low, 0), (from_high, CY)):
        body = value[0 : PACK // 2]
        upper = jnp.where(half_lane < HALF, body, 0.0)
        lower = jnp.where(half_lane < HALF, pltpu.roll(body, HALF, 1), 0.0)
        rest = []
        for group in range(PACK // SUB):
            moved = pltpu.roll(value[PACK // 2 :], HALF - 3 * group, 1)
            rest.append(jnp.where((tile_lane >= HALF) & (tile_lane < HALF + 3), moved, 0.0))
        window = jnp.concatenate([upper, lower], axis=0) + jnp.concatenate(rest, axis=0)
        total = total + (pltpu.roll(window, first, 1) if first else window)
    packed_ref[...] = total
    last = PACK - 2 * SUB
    packed_ref[0 : 2 * SUB, :] = total[0 : 2 * SUB] + jnp.where(odd, halo, 0.0)
    packed_ref[last:PACK, :] = total[last:PACK] + jnp.where(odd, 0.0, halo)
    node_y = (gy - 1) * CY - 1 + iota((SUB, LANES), 1)
    for x in range(DEPTHS):
        put_velocity(packed_ref[KEPT * x : KEPT * x + SUB, :], x, node_y, velocity_ref)
    velocity_ref[DEPTHS * SUB :, :] = jnp.zeros((ROWS - DEPTHS * SUB, LANES), F32)


def gathered(velocity_parts, depth_of, column_of):
    masks = row_masks(depth_of)
    near = [[None] * 4 for _ in range(4)]
    columns = product(velocity_parts, jnp.concatenate(column_onehot(column_of), axis=1), NN)
    for b in range(4):
        column = columns[:, b * LANES : (b + 1) * LANES]
        for a in range(4):
            total = jnp.zeros((SUB, LANES), F32)
            for x in range(CX):
                total = jnp.where(masks[x], column[(x + a) * SUB : (x + a + 1) * SUB], total)
            near[a][b] = total
    return near


def move_points(load, store, chunks, node_of, materials, tables_ref):
    wide = lambda row: jnp.broadcast_to(row, (SUB, LANES))
    twice_shear = wide(2.0 * by_material(materials, tables_ref, 1))
    lame = wide(by_material(materials, tables_ref, 2))
    alive = wide(materials) >= 0
    for k in range(chunks):
        u, v = (load(0, k), load(1, k))
        weight_x, slope_x = stencil(u)
        weight_y, slope_y = stencil(v)
        speed, along, across = ([], [], [])
        for component in range(2):
            value = rate_x = rate_y = None
            for a in range(4):
                inner = slant = None
                for b in range(4):
                    node = wide(node_of(a, b, component))
                    term, tilt = (weight_y[b] * node, slope_y[b] * node)
                    inner = term if b == 0 else inner + term
                    slant = tilt if b == 0 else slant + tilt
                add = (weight_x[a] * inner, slope_x[a] * inner, weight_x[a] * slant)
                if a == 0:
                    value, rate_x, rate_y = add
                else:
                    value, rate_x, rate_y = (value + add[0], rate_x + add[1], rate_y + add[2])
            speed.append(value)
            along.append(rate_x)
            across.append(rate_y)
        rate_xx, rate_yy = (along[0], across[1])
        rate_xy = 0.5 * (across[0] + along[1])
        spherical = lame * (rate_xx + rate_yy)
        stress_xx = load(4, k) + TIME_STEP * (twice_shear * rate_xx + spherical)
        stress_yy = load(5, k) + TIME_STEP * (twice_shear * rate_yy + spherical)
        stress_xy = load(6, k) + TIME_STEP * twice_shear * rate_xy
        fresh = (
            jnp.clip(u + TIME_STEP * speed[0], 0.0, 1.0),
            jnp.clip(v + TIME_STEP * speed[1], 0.0, 1.0),
            speed[0],
            speed[1],
            stress_xx,
            stress_yy,
            stress_xy,
            jnp.maximum(load(7, k), -0.5 * (stress_xx + stress_yy)),
        )
        for c in range(8):
            store(c, k, jnp.where(alive, fresh[c], 0.0))


def node_getter(near):
    return lambda a, b, component: near[a][b][component + 1 : component + 2]


def emit_movers(advanced, chosen_ref, tags_ref, far_ref, near_ref):
    rows = select_rows(chosen_ref[...].astype(BF16), advanced)
    tags = tags_ref[...]
    lane = iota((SUB, LANES), 1)
    for o, ref in enumerate((far_ref, near_ref)):
        put_pieces(ref, 0, rows[o * MCAP : (o + 1) * MCAP])
        tag = pltpu.roll(tags, LANES - o * MCAP, 1) if o else tags
        ref[MSG - SUB : MSG, :] = jnp.where(lane < MCAP, tag, 0.0)


def own_and_far_depth():
    odd = lax.axis_index("gx") & 1
    return (CX - CX * odd, CX * odd)


def departures(cells, materials, lists):
    home, step_x, _ = home_and_steps()
    slots, dests, cell = (lists[0:1], lists[1:2], lists[2:3])
    moving = (dests >= 0) & (dests != home)
    low, high, far = (dests == home - 1, dests == home + 1, dests == home - step_x)
    carried = jnp.where(low | high | far, 1, 0)
    own, other = own_and_far_depth()
    depth = (cell >> 5) + jnp.where(far, other, own)
    column = (cell & (CY - 1)) + jnp.where(high, 2 * CY, jnp.where(far, CY, 0))
    entries = small_rows(jnp.where(moving, 1, 0), carried, carried * depth, carried * column)
    found = turned_to(entries, holding(slots)).astype(jnp.int32)
    gone, across = (found[0:1] > 0, found[1:2] > 0)
    sub = iota((SUB, LANES), 0)
    wide = lambda value: jnp.broadcast_to(value, (SUB, LANES))
    kept = jnp.where(
        sub == 0,
        wide(jnp.where(gone, 0, cells)),
        wide(jnp.where(gone, -1, materials)),
    )
    target = jnp.where(
        sub == 0,
        wide(jnp.where(across, found[2:3], (cells >> 5) + own)),
        jnp.where(
            sub == 1,
            wide(jnp.where(across, found[3:4], (cells & (CY - 1)) + CY)),
            wide(jnp.where(gone & ~across, -1, materials)),
        ),
    )
    return (kept, target)


def plan_depth(
    meta_ref, lists_ref,
    chosen_a_ref, chosen_b_ref, tags_a_ref, tags_b_ref, kept_a_ref, kept_b_ref, target_ref, stays_ref,
):
    home, step_x, _ = home_and_steps()
    cells, materials = (meta_ref[0:1, :], meta_ref[1:2, :])
    for first, chosen_ref, tags_ref in ((0, chosen_a_ref, tags_a_ref), (3, chosen_b_ref, tags_b_ref)):
        matched, rank = matches(lists_ref[first + 1 : first + 2, :], (home - step_x, home + step_x))
        placing = placing_rows(matched, rank, (0, 1))
        chosen = turned_to(placing, holding(lists_ref[first : first + 1, :]))
        chosen_ref[...] = chosen[0 : 2 * MCAP]
        cell = lists_ref[first + 2 : first + 3, :]
        places = turned_to(small_rows(cell >> 5, cell & (CY - 1)), placing)
        kinds = turned_to(small_rows(materials + 1), chosen.astype(BF16))
        tags_ref[...] = tag_tile(places[0:1] * float(CY) + places[1:2], kinds[0:1])
    kept, target = departures(cells, materials, lists_ref[0:3, :])
    kept_a_ref[...] = kept
    target_ref[...] = target
    kept, _ = departures(kept[0:1], kept[1:2], lists_ref[3:6, :])
    kept_b_ref[...] = kept
    stays_ref[...] = jnp.broadcast_to((kept[1:2] >= 0).astype(F32), stays_ref.shape).T


def rows_at(ref, c, k, stride):
    return ref[c * stride + k * SUB : c * stride + (k + 1) * SUB, :]


def advance_one(
    turned_ref, meta_ref, merged_ref, yo_ref, yi_ref, tables_ref, chosen_ref, tags_ref,
    fresh_ref, nodes_ref, far_message_ref, near_message_ref,
    velocity_ref,
):
    velocity_one(merged_ref, yi_ref[0:SUB, :], yo_ref[0:SUB, :], velocity_ref)
    cells, materials = (meta_ref[0:1, :], meta_ref[1:2, :])

    def store(c, k, value):
        fresh_ref[c * BLOCK + k * SUB : c * BLOCK + (k + 1) * SUB, :] = value

    near = gathered(halves(velocity_ref[...]), cells >> 5, cells & (CY - 1))
    load = lambda c, k: rows_at(turned_ref, c, k, BLOCK)
    move_points(load, store, BLOCK // SUB, node_getter(near), materials, tables_ref)
    emit_movers(fresh_ref[...].T, chosen_ref, tags_ref, far_message_ref, near_message_ref)
    for a in range(4):
        for b in range(4):
            row = 2 * (4 * a + b)
            nodes_ref[row : row + 2, :] = near[a][b][1:3]


def sums_kept(fresh_ref, target_ref, tables_ref, sums_ref, left_ref):
    depth, column, materials = (target_ref[0:1, :], target_ref[1:2, :], target_ref[2:3, :])
    load = lambda c, k: rows_at(fresh_ref, c, k, BLOCK)
    terms = weighted_terms(load, BLOCK // SUB, materials, tables_ref)
    spread_rows(terms, row_masks(depth, 2 * CX), left_ref)
    sums_ref[...] = product(halves(left_ref[...]), jnp.concatenate(column_onehot(column), axis=1), NT)


def near_cross(nodes_ref, chosen_ref, near_ref):
    near_ref[...] = product(halves(nodes_ref[...]), chosen_ref[...].astype(BF16), NT)


def packed_blocks(rows, wide_ref, turned_ref):
    count = rows.shape[0]
    fill = jnp.zeros((LANES - count, rows.shape[1]), F32)
    wide_ref[...] = jnp.concatenate([rows, fill], axis=0).T
    stride = BLOCK * count // LANES
    for c in range(8):
        total = wide_ref[c * BLOCK : c * BLOCK + stride, :]
        for group in range(1, LANES // count):
            start = c * BLOCK + group * stride
            total = total + pltpu.roll(wide_ref[start : start + stride, :], count * group, 1)
        turned_ref[c * stride : (c + 1) * stride, :] = total


def repeated(tile, count):
    while count < LANES:
        tile = tile + pltpu.roll(tile, count, 1)
        count *= 2
    return tile


def arrived_tags(from_inner, from_outer):
    low, high = by_side(from_inner, from_outer, parity("gx"))
    packed = repeated(low + pltpu.roll(high, MCAP, 1), 2 * MCAP)
    return packed.astype(jnp.int32) - (iota((SUB, LANES), 0) == 1).astype(jnp.int32)


def put_packed(ref, sums):
    ref[PACK - SUB : PACK, :] = jnp.zeros((SUB, LANES), F32)
    for x in range(DEPTHS):
        ref[KEPT * x : KEPT * (x + 1), :] = sums[x * SUB : x * SUB + KEPT]


def sums_two(
    kept_sums_ref, from_near_ref, to_far_ref, tables_ref,
    own_ref, message_ref,
    left_ref, wide_ref, turned_ref,
):
    tags = repeated(from_near_ref[MSG - SUB : MSG, :], MCAP).astype(jnp.int32)
    cells, materials = (tags[0:1], tags[1:2] - 1)
    packed_blocks(joined(from_near_ref[0 : MSG - SUB, :]), wide_ref, turned_ref)
    stride = turned_ref.shape[0] // 8
    load = lambda c, k: rows_at(turned_ref, c, k, stride)
    terms = weighted_terms(load, stride // SUB, materials, tables_ref)
    spread_rows(terms, row_masks(cells >> 5), left_ref)
    onehots = jnp.concatenate(column_onehot((cells & (CY - 1)) + CY), axis=1)
    part = product(halves(left_ref[...]), onehots, NT)
    odd = parity("gx")
    first, second = (kept_sums_ref[0:BRICK, :], kept_sums_ref[CX * SUB : CX * SUB + BRICK, :])
    put_packed(own_ref, jnp.where(odd, first, second) + part[0:BRICK])
    far = jnp.where(odd, second, first)
    low = far[0:HALO] + jnp.where(odd, part[TOP : TOP + HALO], 0.0)
    high = far[TOP : TOP + HALO] + jnp.where(odd, 0.0, part[0:HALO])
    put_packed(message_ref, jnp.concatenate([low, far[HALO:TOP], high], axis=0))
    message_ref[PACK : PACK + MSG, :] = to_far_ref[...]


def arrange_depth(from_near_ref, from_far_ref, turned_ref, new_meta_ref, wide_ref):
    rows, tags = (slice(0, MSG - SUB), slice(MSG - SUB, MSG))
    far = from_far_ref[PACK : PACK + MSG, :]
    new_meta_ref[...] = arrived_tags(from_near_ref[tags, :], far[tags])
    low, high = by_side(from_near_ref[rows, :], far[rows], parity("gx"))
    packed_blocks(jnp.concatenate([joined(low), joined(high)], axis=0), wide_ref, turned_ref)


def arrange_cross(yo_ref, yi_ref, cross_ref, tags_ref, wide_ref):
    low, high = by_side(yi_ref[...], yo_ref[...], parity("gy"))
    tags_ref[...] = low[SUB : 2 * SUB] + pltpu.roll(high[SUB : 2 * SUB], 2 * MCAP, 1)
    rows = jnp.concatenate([joined(low[2 * SUB :]), joined(high[2 * SUB :])], axis=0)
    packed_blocks(rows, wide_ref, cross_ref)


def advance_two(
    kept_ref, meta_ref, slots_ref, merged_ref, tables_ref, chosen_ref, tags_ref,
    rows_ref, velocity_ref, far_message_ref, near_message_ref,
    packed_ref, fresh_ref,
):
    velocity_two(slots_ref, merged_ref, packed_ref, velocity_ref)
    cells, materials = (meta_ref[0:1, :], meta_ref[1:2, :])

    def store(c, k, value):
        fresh_ref[c * BLOCK + k * SUB : c * BLOCK + (k + 1) * SUB, :] = value

    near = gathered(halves(velocity_ref[...]), cells >> 5, (cells & (CY - 1)) + CY)
    load = lambda c, k: rows_at(kept_ref, c, k, BLOCK)
    move_points(load, store, BLOCK // SUB, node_getter(near), materials, tables_ref)
    advanced = fresh_ref[...].T
    rows_ref[...] = advanced
    emit_movers(advanced, chosen_ref, tags_ref, far_message_ref, near_message_ref)


def near_movers(slots_ref, index):
    lane = iota((SUB, LANES), 1)
    tile = slots_ref[index, PACK // 2 + SUB : SLOT, :]
    parts = []
    for part in range(NEAR // SUB):
        moved = pltpu.roll(tile, LANES - part * NEAR, 1) if part else tile
        parts.append(jnp.where(lane < 2 * MCAP, moved, 0.0))
    return jnp.concatenate(parts, axis=0)


def settle(
    advanced_ref, stays_ref, velocity_ref, from_near_ref, from_far_ref, tables_ref, slots_ref, cross_ref, tags_ref,
    rows_ref, tail_ref,
    wide_ref, middle_ref, out_ref, small_ref, turned_ref, new_meta_ref, other_wide_ref,
):
    arrange_depth(from_near_ref, from_far_ref, turned_ref, new_meta_ref, other_wide_ref)
    stays = stays_ref[...] > 0.5
    for piece in range(PIECES):
        columns = slice(piece * LANES, (piece + 1) * LANES)
        rows_ref[0:LANES, columns] = jnp.where(stays, advanced_ref[:, columns], 0.0)
    parts = halves(velocity_ref[...])

    stride = turned_ref.shape[0] // 8
    cells, materials = (new_meta_ref[0:1, :], new_meta_ref[1:2, :])

    def store_small(c, k, value):
        small_ref[c * stride + k * SUB : c * stride + (k + 1) * SUB, :] = value

    load = lambda c, k: rows_at(turned_ref, c, k, stride)
    near = gathered(parts, cells >> 5, (cells & (CY - 1)) + CY)
    move_points(load, store_small, stride // SUB, node_getter(near), materials, tables_ref)

    gy = lax.axis_index("gy")
    lane = iota((SUB, LANES), 1)
    tags = tags_ref[...]
    tail = jnp.zeros((SUB, LANES), F32)
    for start, shift in ((32, 32), (48, 16), (96, 80), (112, 64)):
        tail = jnp.where((lane >= start) & (lane < start + MCAP), pltpu.roll(tags, shift, 1), tail)
    materials_row = (iota((SUB, LANES), 0) == 1).astype(jnp.int32)
    tail = tail.astype(jnp.int32) - materials_row
    tail_ref[...] = jnp.where(lane < 2 * MCAP, new_meta_ref[...], tail)
    tags = repeated(tags, 4 * MCAP).astype(jnp.int32) - materials_row

    across = slots_ref.shape[0] // 2
    column = (lax.axis_index("gx") & 1) * across
    below = near_movers(slots_ref, column + jnp.maximum(gy - 1, 0))
    above = near_movers(slots_ref, column + jnp.minimum(gy + 1, across - 1))
    nodes = below + pltpu.roll(above, 2 * MCAP, 1)
    nodes = nodes + pltpu.roll(nodes, 4 * MCAP, 1)

    def node_of(a, b, component):
        row = 2 * (4 * a + b) + component
        return nodes[row : row + 1]

    half = cross_ref.shape[0] // 8
    kinds = tags[1:2]

    def store_middle(c, k, value):
        middle_ref[c * half + k * SUB : c * half + (k + 1) * SUB, :] = value

    move_points(lambda c, k: rows_at(cross_ref, c, k, half), store_middle, half // SUB, node_of, kinds, tables_ref)
    row_lane = lane[0:1]
    second = (row_lane & MCAP) != 0
    cell = jnp.where(second, tags[2:3], tags[0:1])
    side = jnp.where((row_lane & (2 * MCAP)) != 0, 2 * CY, 0)
    near = gathered(parts, cell >> 5, (cell & (CY - 1)) + jnp.where(second, side, CY))

    def store_out(c, k, value):
        out_ref[c * half + k * SUB : c * half + (k + 1) * SUB, :] = value

    move_points(
        lambda c, k: rows_at(middle_ref, c, k, half), store_out, half // SUB, node_getter(near), kinds, tables_ref
    )
    crossed = lane < 4 * MCAP
    for c in range(8):
        for k in range(BLOCK // SUB):
            group, rest = divmod(k * SUB, half)
            first = out_ref[c * half + rest : c * half + rest + SUB, :]
            first = pltpu.roll(first, LANES - 4 * MCAP * group, 1) if group else first
            group, rest = divmod(k * SUB, stride)
            second = small_ref[c * stride + rest : c * stride + rest + SUB, :]
            second = pltpu.roll(second, (4 * MCAP - 2 * MCAP * group) % LANES, 1)
            wide_ref[c * BLOCK + k * SUB : c * BLOCK + (k + 1) * SUB, :] = jnp.where(crossed, first, second)
    last = wide_ref[...].T
    rows_ref[LANES : LANES + 2 * MCAP, :] = last[4 * MCAP : 6 * MCAP]
    for group, index in enumerate((2, 6, 3, 7)):
        start = LANES + index * MCAP
        rows_ref[start : start + MCAP, :] = last[group * MCAP : (group + 1) * MCAP]


def assemble(
    part_ref, old_meta_ref, tail_ref, xo_ref, xi_ref,
    points_ref, cells_ref, mats_ref,
    tags_ref, rows_ref, sems,
):
    base = points_ref.shape[0] - 4 * MCAP
    odd = lax.axis_index("gx") & 1
    copies = []
    for index, (first, last) in enumerate(((0, base), (base + 2 * MCAP, base + 4 * MCAP))):
        copies.append(pltpu.make_async_copy(part_ref.at[first:last], points_ref.at[first:last], sems.at[index]))
        copies[-1].start()
    for index, (ref, region) in enumerate(((xo_ref, odd), (xi_ref, 1 - odd))):
        start = pl.multiple_of(base + region * MCAP, MCAP)
        rows_ref[index] = joined(ref[0 : MSG - SUB, :])
        copies.append(
            pltpu.make_async_copy(rows_ref.at[index], points_ref.at[pl.ds(start, MCAP), :], sems.at[2 + index])
        )
        copies[-1].start()
    arrived = arrived_tags(xi_ref[MSG - SUB : MSG, :], xo_ref[MSG - SUB : MSG, :])
    lane = iota((1, LANES), 1)
    here = (lane >= 4 * MCAP) & (lane < 6 * MCAP)
    for row, ref in ((0, cells_ref), (1, mats_ref)):
        tags_ref[row, 0:1, :] = old_meta_ref[row : row + 1, :]
        tags_ref[row, 1:2, :] = jnp.where(here, arrived[row : row + 1], tail_ref[row : row + 1, :])
        copies.append(pltpu.make_async_copy(tags_ref.at[row], ref, sems.at[4 + row]))
        copies[-1].start()
    for copy in copies:
        copy.wait()


def shards(
    points,
    block_cell,
    block_mat,
    density,
    shear_modulus,
    lame_modulus,
    mig_slot_a,
    mig_dest_a,
    mig_cell_a,
    mig_slot_b,
    mig_dest_b,
    mig_cell_b,
):
    wide = 8 * BLOCK
    I32 = jnp.int32
    row = lambda value: value.reshape(1, -1)
    cells, mats = (row(block_cell), row(block_mat))
    list_a = (row(mig_slot_a), row(mig_dest_a), row(mig_cell_a))
    list_b = (row(mig_slot_b), row(mig_dest_b), row(mig_cell_b))

    halo = ((HALO, LANES), F32)
    tile = ((SUB, LANES), F32)
    tags = ((SUB, LANES), I32)
    grid = ((ROWS, LANES), F32)
    message = ((MSG, LANES), F32)
    cross_message = ((CROSS_MSG, LANES), F32)
    turned_form = ((wide, LANES), F32)
    half_form = ((wide // 2, LANES), F32)
    quarter_form = ((wide // 4, LANES), F32)
    near_form = ((NEAR, LANES), F32)
    slots_form = ((2 * lax.axis_size("gy"), SLOT, LANES), F32)
    scratch = lambda form: pltpu.VMEM(*form)
    left = pltpu.VMEM((ROWS, 4 * LANES), F32)

    def along_depth(far, near):
        return (swap(far, "gx", 1), swap(near, "gx", 0))

    (nothing,) = call(blank, (tags,), (), (), flops=1 << 28, bytes_accessed=1 << 10)
    meta, lists, tables = call(
        prepare,
        (tags, tags, ((3 * NMAT, LANES), F32)),
        (),
        (IN_VMEM,) * 12,
        nothing, cells, mats, row(density), row(shear_modulus), row(lame_modulus), *list_a, *list_b,
    )
    turned, terms = call(
        terms_one, (turned_form, ((16 * SUB, LANES), F32)), (), (IN_VMEM,) * 2, points, meta
    )
    sums, inner, outer = call(sums_one, (grid, halo, halo), (left,), (IN_VMEM,) * 3, terms, meta, tables)
    picked, picked_tags, chosen = call(
        pick_cross,
        (((4 * MCAP, wide), F32), tile, ((LANES, LANES), F32)),
        (),
        (IN_VMEM,) * 3,
        points, meta, lists,
    )
    merged, inner, outer = call(
        merge_one,
        (grid, cross_message, cross_message),
        (),
        (IN_VMEM,) * 5,
        sums, *along_depth(outer, inner), picked, picked_tags,
    )
    cross_far, cross_near = (swap(outer, "gy", 1), swap(inner, "gy", 0))
    chosen_form = ((2 * MCAP, LANES), F32)
    chosen_a, chosen_b, tags_a, tags_b, kept_a, kept_b, target, stays = call(
        plan_depth,
        (chosen_form, chosen_form, tile, tile, tags, tags, tags, ((LANES, LANES), F32)),
        (),
        (IN_VMEM,) * 2,
        meta, lists,
    )
    fresh, nodes, far, near = call(
        advance_one,
        (turned_form, near_form, message, message),
        (scratch(grid),),
        (IN_VMEM,) * 8,
        turned, meta, merged, cross_far, cross_near, tables, chosen_a, tags_a,
    )
    from_near = swap(near, "gx", 0)
    pair_form = ((PAIR, LANES), F32)
    pair_left = pltpu.VMEM((PAIR, 4 * LANES), F32)
    (kept_sums,) = call(sums_kept, (pair_form,), (pair_left,), (IN_VMEM,) * 3, fresh, target, tables)
    (near_nodes,) = call(near_cross, (near_form,), (), (IN_VMEM,) * 2, nodes, chosen)
    packed_form = ((PACK, LANES), F32)
    own, far_message = call(
        sums_two,
        (packed_form, ((PACK + MSG, LANES), F32)),
        (left, scratch(turned_form), pltpu.VMEM((wide // 8, LANES), F32)),
        (IN_VMEM,) * 4,
        kept_sums, from_near, far, tables,
    )
    from_far = swap(far_message, "gx", 1)
    cross, cross_tags = call(
        arrange_cross, (half_form, tile), (scratch(turned_form),), (IN_VMEM,) * 2, cross_far, cross_near
    )
    merged, slots = call(
        merge_far, (packed_form, slots_form), (), (IN_VMEM,) * 4, own, from_far, near_nodes, cross_tags
    )
    slots = lax.all_to_all(slots, ("gx", "gy"), 0, 0, axis_index_groups=chip_columns())
    advanced, velocity, far, near = call(
        advance_two,
        (((LANES, wide), F32), grid, message, message),
        (scratch(packed_form), scratch(turned_form)),
        (IN_VMEM,) * 7,
        fresh, kept_a, slots, merged, tables, chosen_b, tags_b,
    )
    arrived = along_depth(far, near)
    final_form = ((2 * LANES, wide), F32)
    part, tail = call(
        settle,
        (final_form, tags),
        (
            scratch(turned_form),
            scratch(half_form),
            scratch(half_form),
            scratch(quarter_form),
            scratch(quarter_form),
            scratch(tags),
            scratch(turned_form),
        ),
        (IN_VMEM,) * 9,
        advanced, stays, velocity, from_near, from_far, tables, slots, cross, cross_tags,
    )
    final_points, final_cells, final_mats = call(
        assemble,
        (final_form, ((2, LANES), I32), ((2, LANES), I32)),
        (pltpu.VMEM((2, 2, LANES), I32), pltpu.VMEM((2, MCAP, wide), F32), pltpu.SemaphoreType.DMA((6,))),
        (IN_VMEM,) * 5,
        part, kept_b, tail, *arrived,
        out_specs=(IN_HBM,) * 3,
    )
    return (final_points, final_cells.reshape(-1), final_mats.reshape(-1))


def solution(mesh):
    split = P(("gx", "gy"))
    rows = P(("gx", "gy"), None)
    return jax.shard_map(
        shards,
        mesh=mesh,
        in_specs=(rows, split, split, P(), P(), P()) + (split,) * 6,
        out_specs=(rows, split, split),
        check_vma=False,
    )
```
